32 devices in a mesh: groups: 2 (over y), seq: 4 (over z), mp: 2 (over x), side: 2 (over core).
Axes of the slice: x: 2, y: 2, z: 4, core: 2. Of those that a mesh axis runs over, the one named last changes fastest.
Arguments:
- teacher_queries: bfloat16 [1024, 4096], P(('groups', 'seq'), ('mp', 'side')), parts along dimension 0, may hold values from -5 to 5
- teacher_keys: bfloat16 [1024, 512], P(('groups', 'seq'), 'mp'), parts along dimension 0, may hold values from -5 to 5
- teacher_values: bfloat16 [1024, 512], P(('groups', 'seq'), 'mp'), parts along dimension 0, may hold values from -18 to 18
- doc_ids: int32 [1024], P(('groups', 'seq')), parts along dimension 0, may hold values from 0 to 11, never falling along the last dimension, each value on 1 to 384 neighbouring positions
- owner: int32 [1024, 1], P(('groups', 'seq')), parts along dimension 0, may hold values from 0 to 3; in each aligned block of 128 rows (0 to 127, 128 to 255, ...) at most 48 rows name the same one
- student_hidden: bfloat16 [1536, 3584], P(('groups', 'seq')), parts along dimension 0, may hold values from -400 to 400
- norm_gain: float32 [3584], replicated, may hold values from 0.5 to 1.5
- proj: bfloat16 [3584, 4096], P('seq', ('mp', 'side')), may hold values from -0.09375 to 0.09375
Outputs:
- grad_hidden: bfloat16 [1536, 3584], P(('groups', 'seq')), parts along dimension 0
- grad_proj: float32 [7168, 4096], P(('groups', 'seq'), ('mp', 'side')), parts along dimension 0
The draws below stay inside these ranges and needn't reach their ends.
There are 2 independent parts, one for each index of `groups`. The reference program is written for one: setup_inputs(seed, part) draws one part's arguments, and reference() takes and returns one part's arrays. A program takes and returns all parts, laid end to end along the dimension named above; an argument that names none is the same for every part. Nothing has to cross between parts.
Inputs may be any that keep to these rules, and one draw needn't show every extreme that they name: `doc_ids`: document numbers never fall along the positions; each document has at most 384 positions. `owner`: among the 128 rows of one sequence shard, no student shard is named more than 48 times.
All inputs are finite; a program needn't handle non-finite values.
Results may differ from the reference program's by a relative error of at most 0.013.
Values may be sent and summed in bfloat16 or wider, within the bound.
No kernel may reach another device: no remote copies, remote signals or barrier semaphores. Data moves between devices by JAX's collectives and lax.ppermute only.
A program may use at most 64 MiB of HBM per device.

```python
import math
import jax
import jax.numpy as jnp
import numpy as np
from jax import lax

D_S = 3584
HD = 128
TH = 32
TKV = 4
DOCS = 12
TOK_DEV = 128
SHARDS = 4
FBLOCKS = 4
TOKENS = 512
LENGTH = 512
SLOTS = 48
CAP = 192
F = 4096


def draw_teacher_queries(key, part):
    key = jax.random.fold_in(key, 11)
    base = jax.random.truncated_normal(key, -5.0, 5.0, (TOKENS, TH * HD), jnp.float32)
    return base.astype(jnp.bfloat16)


def draw_teacher_keys(key, part):
    key = jax.random.fold_in(key, 12)
    base = 2.0 * jax.random.truncated_normal(key, -2.5, 2.5, (TOKENS, TKV * HD), jnp.float32)
    return base.astype(jnp.bfloat16)


def draw_student_hidden(key, part):
    key = jax.random.fold_in(key, 21)
    key_base, key_rows, key_cols = jax.random.split(key, 3)
    total_rows = SHARDS * CAP
    row_scale = jnp.exp(jax.random.uniform(key_rows, (total_rows, 1), jnp.float32, 0.0, 2.302585))
    col_scale = jnp.exp(jax.random.uniform(key_cols, (1, D_S), jnp.float32, 0.0, 2.302585))
    base = jax.random.truncated_normal(key_base, -4.0, 4.0, (total_rows, D_S), jnp.float32)
    return (base * row_scale * col_scale).astype(jnp.bfloat16)


def block_scale(stream_key, shape, cuts, least, high):
    def one(axis_at, parts):
        heights = jax.random.uniform(jax.random.fold_in(jax.random.fold_in(stream_key, 6), axis_at), (parts,), jnp.float32, least / len(cuts), high / len(cuts))
        return jnp.repeat(jnp.exp(heights), shape[axis_at] // parts).reshape((-1,) + (1,) * (len(shape) - axis_at - 1))

    level = one(*cuts[0])
    for cut in cuts[1:]:
        level = level * one(*cut)
    return level


def split_up(number_of, total, most, lean):
    portions = [(1 << 20) // math.isqrt(rank ** lean) + 1 for rank in range(2, number_of + 1)]
    rest, given = total - most - (number_of - 1), [1] * (number_of - 1)
    while rest > 0:
        movable = [i for i in range(number_of - 1) if given[i] < most]
        pool, remaining = sum([portions[i] for i in movable]), rest
        for i in movable:
            addition = min(most - given[i], max(1, remaining * portions[i] // pool), rest)
            given[i] = given[i] + addition
            rest = rest - addition
    return np.array([most] + given)


def ragged(own_key, count, total, bound, lean):
    if count == 2:
        one = jax.random.randint(own_key, (), max(1, total - bound), min(bound, total - 1) + 1)
        return jnp.stack([one, total - one])
    tallies = jnp.asarray(split_up(count, total, bound, lean), jnp.int32)
    twos = (count - 1) // 2
    donor, receiver = tallies[1:1 + 2 * twos:2], tallies[2:2 + 2 * twos:2]
    room = jnp.minimum(donor - 1, bound - receiver)
    moved = jax.random.randint(jax.random.fold_in(own_key, 1), (twos,), 0, 1 << 20) % (room + 1)
    tallies = tallies.at[1:1 + 2 * twos:2].set(donor - moved).at[2:2 + 2 * twos:2].set(receiver + moved)
    return tallies[jax.random.permutation(jax.random.fold_in(own_key, 2), count)]


def routed_block(key, own, number, rows, amount, top, reach, slope):
    order = jax.random.permutation(key, amount)
    heavy_load, usual = shares(amount, rows * top, reach, slope, True), shares(amount, rows * top, reach, slope, False)
    places = jnp.arange(amount)

    def named(tallies, rotation):
        used = int((tallies > 0).sum())
        fixed = max(1, used // 4)
        passed = fixed + (places - fixed + rotation * (used - fixed)) % max(1, amount - fixed)
        return jnp.zeros((amount,), jnp.int32).at[order[jnp.where(places < fixed, places, passed)]].set(jnp.asarray(tallies, jnp.int32))

    tallies = jnp.where(number % 4 == 0, named(heavy_load, number // 4), named(usual, number - number // 4 - 1))
    mixed = jax.random.permutation(jax.random.fold_in(own, 3), amount)
    giver, sink = mixed[0:amount // 2 * 2:2], mixed[1:amount // 2 * 2:2]
    room = jnp.minimum(tallies[giver] - 1, reach - tallies[sink]) // 2
    room = jnp.where((giver == order[0]) | (sink == order[0]) | (tallies[sink] == 0), 0, jnp.maximum(room, 0))
    passed = jax.random.randint(jax.random.fold_in(own, 4), (amount // 2,), 0, 1 << 20) % (room + 1)
    tallies = tallies.at[giver].add(-passed).at[sink].add(passed)
    members = jnp.searchsorted(jnp.cumsum(tallies), jnp.arange(rows * top), side="right").astype(jnp.int32)
    listing = members.reshape(top, rows).T
    listing = listing[jax.random.permutation(jax.random.fold_in(own, 1), rows)]
    rotation = jax.random.randint(jax.random.fold_in(own, 2), (rows, 1), 0, top)
    return jnp.take_along_axis(listing, (jnp.arange(top)[None, :] + rotation) % top, axis=1)


def shares(number_of, total, most, lean, full):
    loads = [(1 << 20) // math.isqrt(grade ** lean) + 1 for grade in range(1, number_of + 1)]
    largest = most if full else min(most, max(-(-total // number_of), total * loads[0] // sum(loads)))
    least = 1 if total - largest >= number_of - 1 else 0
    given, surplus = [largest] + [least] * (number_of - 1), total - largest - least * (number_of - 1)
    while surplus > 0:
        movable = [i for i in range(1, number_of) if given[i] < largest] or [i for i in range(1, number_of) if given[i] < most]
        whole, remaining = sum([loads[i] for i in movable]), surplus
        for i in movable:
            addition = min(most - given[i], max(1, remaining * loads[i] // whole), surplus)
            given[i] = given[i] + addition
            surplus = surplus - addition
    return np.array(given)


def noise(rng, dims, scale, reach, shards=(), kind=jnp.bfloat16):
    result = scale * jax.random.normal(rng, dims, jnp.float32)
    if shards:
        result = result * block_scale(rng, dims, shards, -0.22, 0.18)
    return jnp.clip(result, -reach, reach).astype(kind)


def setup_inputs(seed: int = 0, part: int = 0) -> dict:
    key_list = jax.random.split(jax.random.key(seed), 9)
    part_splits = jax.random.split(jax.random.fold_in(key_list[8], part), 9)
    teacher_queries = draw_teacher_queries(jax.random.fold_in(jax.random.fold_in(key_list[8], part), 71), part)
    teacher_keys = draw_teacher_keys(jax.random.fold_in(jax.random.fold_in(key_list[8], part), 71), part)
    teacher_values = noise(part_splits[2], (TOKENS, TKV * HD), 3.0, 18.0, ((0, 4), (1, 2)))
    doc_ids = jnp.searchsorted(jnp.cumsum(ragged(part_splits[3], DOCS, TOKENS, 3 * LENGTH // 4, 2)), jnp.arange(TOKENS), side="right").astype(jnp.int32)
    owner_keys = jax.random.split(jax.random.fold_in(part_splits[4], 1), TOKENS // TOK_DEV)
    owner_turns = jax.random.permutation(jax.random.fold_in(part_splits[4], 3), TOKENS // TOK_DEV)
    owner = jax.vmap(lambda own, number: routed_block(jax.random.fold_in(part_splits[4], 2), own, number, TOK_DEV, SHARDS, 1, SLOTS, 2))(owner_keys, owner_turns).reshape((TOKENS, 1))
    student_hidden = draw_student_hidden(jax.random.fold_in(jax.random.fold_in(key_list[8], part), 71), part)
    norm_gain = jnp.clip(1.0 + 0.1 * jax.random.normal(key_list[6], (D_S,), jnp.float32), 0.5, 1.5)
    proj = noise(key_list[7], (D_S, F), D_S ** -0.5, 0.09375, ((0, 4), (1, 4)))
    return dict(teacher_queries=teacher_queries, teacher_keys=teacher_keys, teacher_values=teacher_values, doc_ids=doc_ids, owner=owner, student_hidden=student_hidden, norm_gain=norm_gain, proj=proj)


def head_attention(operands):
    query_head, key_head, value_head, doc_row = operands
    scale_factor = 1.0 / math.sqrt(HD)
    scores = jnp.dot(query_head, key_head.T, preferred_element_type=jnp.float32) * scale_factor
    positions = jnp.arange(LENGTH, dtype=jnp.int32)
    allowed = (doc_row[:, None] == doc_row[None, :]) & (positions[None, :] <= positions[:, None])
    masked = jnp.where(allowed, scores, -jnp.inf)
    row_max = lax.optimization_barrier(jnp.max(masked, axis=1, keepdims=True))
    probs = jnp.where(allowed, jnp.exp(scores - row_max), 0.0)
    totals = lax.optimization_barrier(jnp.sum(probs, axis=1, keepdims=True))
    weighted = jnp.dot(probs.astype(jnp.bfloat16), value_head, preferred_element_type=jnp.float32)
    return weighted / totals

def reference(teacher_queries, teacher_keys, teacher_values, doc_ids, owner, student_hidden, norm_gain, proj):
    seq_count = TOKENS // LENGTH
    group_size = TH // TKV
    query_all = teacher_queries.reshape(seq_count, LENGTH, TH, HD).transpose(0, 2, 1, 3).reshape(seq_count * TH, LENGTH, HD)
    key_all = jnp.repeat(teacher_keys.reshape(seq_count, LENGTH, TKV, HD), group_size, axis=2)
    key_all = key_all.transpose(0, 2, 1, 3).reshape(seq_count * TH, LENGTH, HD)
    value_all = jnp.repeat(teacher_values.reshape(seq_count, LENGTH, TKV, HD), group_size, axis=2)
    value_all = value_all.transpose(0, 2, 1, 3).reshape(seq_count * TH, LENGTH, HD)
    doc_all = jnp.repeat(doc_ids.reshape(seq_count, LENGTH), TH, axis=0)
    attended = lax.map(head_attention, (query_all, key_all, value_all, doc_all))
    teacher_rows = attended.reshape(seq_count, TH, LENGTH, HD).transpose(0, 2, 1, 3).reshape(TOKENS, F).astype(jnp.bfloat16)
    positions = jnp.arange(TOKENS, dtype=jnp.int32)
    shard_of = positions // TOK_DEV
    dest = owner[:, 0].astype(jnp.int32)
    onehot = (dest[:, None] == jnp.arange(SHARDS, dtype=jnp.int32)[None, :]).astype(jnp.int32)
    onehot = onehot.reshape(SHARDS, TOK_DEV, SHARDS)
    earlier = (jnp.cumsum(onehot, axis=1) - onehot) * onehot
    rank = lax.optimization_barrier(jnp.sum(earlier, axis=2)).reshape(TOKENS).astype(jnp.int32)
    slot = (dest * CAP + shard_of * SLOTS + rank).astype(jnp.int32)
    targets = jnp.zeros((SHARDS * CAP, F), jnp.bfloat16).at[slot].set(teacher_rows)
    filled = jnp.zeros((SHARDS * CAP,), jnp.float32).at[slot].set(1.0)
    hidden_float = student_hidden.astype(jnp.float32)
    inverse_rms = lax.rsqrt(lax.optimization_barrier(jnp.mean(hidden_float * hidden_float, axis=1, keepdims=True)) + 1e-06)
    normed = (hidden_float * inverse_rms * norm_gain).astype(jnp.bfloat16)
    predicted = jnp.dot(normed, proj, preferred_element_type=jnp.float32)
    delta = ((predicted - targets.astype(jnp.float32)) * filled[:, None]).astype(jnp.bfloat16)
    block_width = F // FBLOCKS
    feature_grad = jnp.zeros((SHARDS * CAP, D_S), jnp.float32)
    for block in range(FBLOCKS):
        delta_block = delta[:, block * block_width:(block + 1) * block_width]
        proj_block = proj[:, block * block_width:(block + 1) * block_width]
        product = jnp.dot(delta_block, proj_block.T, preferred_element_type=jnp.float32).astype(jnp.bfloat16)
        product = lax.optimization_barrier(product)
        feature_grad = feature_grad + product.astype(jnp.float32)
    gain_grad = feature_grad * norm_gain
    mean_term = lax.optimization_barrier(jnp.mean(gain_grad * hidden_float, axis=1, keepdims=True))
    grad_hidden = (inverse_rms * gain_grad - inverse_rms ** 3 * hidden_float * mean_term).astype(jnp.bfloat16)
    factor = 1.0 / math.sqrt(TOKENS)

    def add_block(running, operands):
        normed_block, delta_block = operands
        product = (jnp.dot(normed_block.T, delta_block, preferred_element_type=jnp.float32) * factor).astype(jnp.bfloat16)
        product = lax.optimization_barrier(product)
        return (running + product.astype(jnp.float32), None)
    grad_proj, unused = lax.scan(add_block, jnp.zeros((D_S, F), jnp.float32), (normed.reshape(SHARDS, CAP, D_S), delta.reshape(SHARDS, CAP, F)))
    return (grad_hidden, grad_proj)
```

```python
import math

import jax
import jax.numpy as jnp
from jax import lax
from jax.sharding import PartitionSpec as P

HD = 128
DIRECT = 4
BF = jnp.bfloat16
F32 = jnp.float32


def seq_size():
    return lax.axis_size("seq")


def plane_size():
    return lax.axis_size("mp") * lax.axis_size("side")


def seq_direct():
    return seq_size() <= DIRECT


def plane_direct():
    return lax.axis_size("mp") == 2 and lax.axis_size("side") == 2 and seq_size() == 4


def place(peer):
    if seq_direct():
        return (lax.axis_index("seq") - peer) % seq_size()
    return peer


def shift(x, step):
    n = seq_size()
    return lax.ppermute(x, "seq", [(i, (i + step) % n) for i in range(n)])


def gather_seq(x):
    if not seq_direct():
        return lax.all_gather(x, "seq", axis=0, tiled=False)
    n = seq_size()
    return jnp.stack([x] + [shift(x, step) for step in range(1, n)])


def exchange_seq(piece_for):
    n = seq_size()
    if not seq_direct():
        pieces = jnp.stack([piece_for(z) for z in range(n)])
        return lax.all_to_all(pieces, "seq", split_axis=0, concat_axis=0, tiled=True)
    me = lax.axis_index("seq")
    sent = [shift(piece_for((me + step) % n), step) for step in range(1, n)]
    return jnp.stack([piece_for(me)] + sent)


def swap(x, axis):
    return lax.ppermute(x, axis, [(0, 1), (1, 0)])


def gather_plane(x):
    if not plane_direct():
        return lax.all_gather(x, ("mp", "side"), axis=0, tiled=False)
    side = lax.axis_index("side")
    mp = lax.axis_index("mp")
    mate = swap(x, "side")
    far = swap(x, "mp")
    far_mate = swap(far, "side")
    own = jnp.where(side == 0, jnp.stack([x, mate]), jnp.stack([mate, x]))
    other = jnp.where(side == 0, jnp.stack([far, far_mate]), jnp.stack([far_mate, far]))
    return jnp.where(mp == 0, jnp.concatenate([own, other]), jnp.concatenate([other, own]))


def scatter_plane(piece_for, width):
    if not plane_direct():
        pieces = jnp.concatenate([piece_for(j) for j in range(plane_size())])
        return lax.psum_scatter(
            pieces.astype(BF), ("mp", "side"), scatter_dimension=0, tiled=True
        ).astype(F32)
    side = lax.axis_index("side")
    mp = lax.axis_index("mp")
    away_far = piece_for((1 - mp) * 2 + (1 - side)).astype(BF)
    away_near = piece_for(mp * 2 + (1 - side)).astype(BF)
    got_far = swap(away_far, "side")
    got_near = swap(away_near, "side")
    far = piece_for((1 - mp) * 2 + side) + got_far.astype(F32)
    crossed = swap(far.astype(BF), "mp")
    near = piece_for(mp * 2 + side) + got_near.astype(F32)
    return near + crossed.astype(F32)


def attention(queries, keys, values, key_docs, doc_ids):
    n = seq_size()
    me = lax.axis_index("seq")
    rows = queries.shape[0]
    heads = queries.shape[1] // HD
    peers = jnp.arange(n, dtype=jnp.int32)
    blocks = (me - peers) % n if seq_direct() else peers
    key_pos = (blocks[:, None] * rows + jnp.arange(rows, dtype=jnp.int32)[None, :]).reshape(-1)
    query_pos = me * rows + jnp.arange(rows, dtype=jnp.int32)
    allowed = (key_docs.reshape(-1)[None, :] == doc_ids[:, None]) & (
        key_pos[None, :] <= query_pos[:, None]
    )
    stacked = queries.reshape(rows, heads, HD).transpose(1, 0, 2)
    scale_factor = 1.0 / math.sqrt(HD)
    scores = (
        jnp.einsum("hqd,kd->hqk", stacked, keys.reshape(-1, HD), preferred_element_type=F32)
        * scale_factor
    )
    scores = jnp.where(allowed[None], scores, -1e30)
    top = jnp.max(scores, axis=2, keepdims=True)
    probs = jnp.where(allowed[None], jnp.exp(scores - top), 0.0)
    totals = jnp.sum(probs, axis=2, keepdims=True)
    weighted = jnp.einsum(
        "hqk,kd->hqd", probs.astype(BF), values.reshape(-1, HD), preferred_element_type=F32
    )
    return (weighted / totals).astype(BF).transpose(1, 0, 2).reshape(rows, heads * HD)


def on_device(
    teacher_queries, teacher_keys, teacher_values, doc_ids, owner, student_hidden, norm_gain, proj
):
    n = seq_size()
    me = lax.axis_index("seq")
    side = lax.axis_index("side")
    plane = plane_size()
    mine = lax.axis_index("mp") * lax.axis_size("side") + side
    rows = teacher_queries.shape[0]
    heads = teacher_queries.shape[1] // HD
    kv_local = teacher_keys.shape[1] // HD
    group = heads * lax.axis_size("side") // kv_local
    width = student_hidden.shape[1]
    depth = proj.shape[0]
    capacity = student_hidden.shape[0]
    slots = capacity // n
    shared = n // plane
    held = shared * slots

    hidden = lax.dynamic_slice_in_dim(student_hidden, mine * held, held, 0).astype(F32)
    inverse_rms = lax.rsqrt(jnp.mean(hidden * hidden, axis=1, keepdims=True) + 1e-06)
    normed = (hidden * inverse_rms * norm_gain).astype(BF)
    normed_slots = exchange_seq(
        lambda z: lax.dynamic_slice_in_dim(normed, z * depth, depth, 1)
    )

    head = side * heads // group
    key_head = lax.dynamic_slice_in_dim(teacher_keys, head * HD, HD, 1)
    value_head = lax.dynamic_slice_in_dim(teacher_values, head * HD, HD, 1)
    small = jnp.stack([doc_ids, owner[:, 0]]).astype(BF)
    parcel = gather_seq(jnp.concatenate([key_head, value_head, jnp.pad(small, ((0, 14), (0, 0)))]))
    keys, values = parcel[:, :rows], parcel[:, rows : 2 * rows]
    docs = parcel[:, 2 * rows].astype(jnp.int32)
    owners = parcel[:, 2 * rows + 1].astype(jnp.int32)

    teacher_rows = attention(teacher_queries, keys, values, docs, doc_ids)

    own_blocks = jnp.stack(
        [
            lax.dynamic_index_in_dim(owners, place(mine * shared + b), 0, keepdims=False)
            for b in range(shared)
        ]
    )
    order = jnp.arange(rows, dtype=jnp.int32)
    same = (own_blocks[:, :, None] == own_blocks[:, None, :]) & (order[:, None] > order[None, :])
    rank = jnp.sum(same.astype(jnp.int32), axis=2)
    local = jnp.arange(shared, dtype=jnp.int32)[:, None] * slots + rank
    spots = jnp.arange(n * held, dtype=jnp.int32)
    arrived = place(own_blocks) * held + local
    pick = (arrived.reshape(-1)[:, None] == spots[None, :]).astype(BF)
    leaving = ((own_blocks - me) % n if seq_direct() else own_blocks) * held + local
    drop = (leaving.reshape(-1)[:, None] == spots[None, :]).astype(BF)

    normed_own = jnp.dot(
        pick, normed_slots.reshape(n * held, depth), preferred_element_type=F32
    ).astype(BF)
    normed_rows = gather_plane(normed_own).reshape(n, rows, depth)

    def partial(z):
        block = lax.dynamic_index_in_dim(normed_rows, z, 0, keepdims=False)
        return jnp.dot(block, proj, preferred_element_type=F32)

    if seq_direct():
        sent = [shift(partial((me + step) % n).astype(BF), step) for step in range(1, n)]
        predicted = partial(me)
        for piece in sent:
            predicted = predicted + piece.astype(F32)
    else:
        whole = jnp.dot(
            normed_rows.reshape(n * rows, depth), proj, preferred_element_type=F32
        ).astype(BF)
        predicted = lax.psum_scatter(whole, "seq", scatter_dimension=0, tiled=True).astype(F32)
    delta = (predicted - teacher_rows.astype(F32)).astype(BF)
    deltas = gather_seq(delta)

    def feature_piece(j):
        blocks = [
            lax.dynamic_index_in_dim(deltas, place(j * shared + b), 0, keepdims=False)
            for b in range(shared)
        ]
        return lax.dot_general(
            jnp.concatenate(blocks), proj, (((1,), (1,)), ((), ())), preferred_element_type=F32
        )

    feature_rows = scatter_plane(feature_piece, depth).astype(BF)
    feature_slots = (
        lax.dot_general(drop, feature_rows, (((0,), (0,)), ((), ())), preferred_element_type=F32)
        .astype(BF)
        .reshape(n, held, depth)
    )
    if seq_direct():
        received = [feature_slots[0]] + [shift(feature_slots[k], k) for k in range(1, n)]
        feature_grad = jnp.zeros((held, width), BF)
        for k in range(n):
            feature_grad = lax.dynamic_update_slice_in_dim(
                feature_grad, received[k], ((me - k) % n) * depth, 1
            )
    else:
        received = lax.all_to_all(feature_slots, "seq", split_axis=0, concat_axis=0, tiled=True)
        feature_grad = received.transpose(1, 0, 2).reshape(held, width)

    gain_grad = feature_grad.astype(F32) * norm_gain
    mean_term = jnp.mean(gain_grad * hidden, axis=1, keepdims=True)
    grad_rows = (inverse_rms * gain_grad - inverse_rms**3 * hidden * mean_term).astype(BF)
    grad_hidden = gather_plane(grad_rows).reshape(capacity, width)

    if seq_direct():
        ordered = jnp.stack(
            [
                lax.dynamic_index_in_dim(normed_rows, (me - k) % n, 0, keepdims=False)
                for k in range(n)
            ]
        )
    else:
        ordered = normed_rows
    factor = 1.0 / math.sqrt(rows * n)
    grad_proj = (
        lax.dot_general(
            ordered.reshape(n * rows, depth),
            deltas.reshape(n * rows, -1),
            (((0,), (0,)), ((), ())),
            preferred_element_type=F32,
        )
        * factor
    )
    return (grad_hidden, grad_proj)


def solution(mesh):
    return jax.shard_map(
        on_device,
        mesh=mesh,
        in_specs=(
            P(("groups", "seq"), ("mp", "side")),
            P(("groups", "seq"), "mp"),
            P(("groups", "seq"), "mp"),
            P(("groups", "seq")),
            P(("groups", "seq"), None),
            P(("groups", "seq"), None),
            P(),
            P("seq", ("mp", "side")),
        ),
        out_specs=(P(("groups", "seq"), None), P(("groups", "seq"), ("mp", "side"))),
        check_vma=False,
    )
```

```python
import math

import jax
import jax.numpy as jnp
from jax import lax
from jax.experimental import pallas as pl
from jax.experimental.pallas import tpu as pltpu
from jax.sharding import PartitionSpec as P

HD = 128
LANES = 128
BF = jnp.bfloat16
F32 = jnp.float32
I32 = jnp.int32
PARAMS = pltpu.CompilerParams(vmem_limit_bytes=32 * 1024 * 1024)
PAIRWISE = True


def dot(a, b, dims=((1,), (0,))):
    return lax.dot_general(a, b, (dims, ((), ())), preferred_element_type=F32)


def eye(size):
    return lax.broadcasted_iota(I32, (size, size), 0) == lax.broadcasted_iota(I32, (size, size), 1)


def to_row(column):
    return jnp.sum(jnp.where(eye(column.shape[0]), column, 0.0), axis=0, keepdims=True)


def to_column(row):
    return jnp.sum(jnp.where(eye(row.shape[1]), row, 0.0), axis=1, keepdims=True)


def norm_kernel(at, hidden_ref, gain_ref, owner_ref, docs_ref, *outs):
    pieces, inverse_ref = outs[:-1], outs[-1]
    rows, width = hidden_ref.shape
    depth = width // len(pieces)
    hidden = hidden_ref[...].astype(F32)
    inverse = lax.rsqrt(jnp.sum(hidden * hidden, axis=1, keepdims=True) / width + 1e-06)
    inverse_ref[...] = inverse
    line = lax.broadcasted_iota(I32, (rows, LANES), 0)
    owner_row = to_row(owner_ref[...].astype(F32))
    docs_row = docs_ref[...].astype(F32)
    extra = jnp.where(line == 0, owner_row, jnp.where(line == 1, docs_row, 0.0)).astype(BF)
    for k, piece in enumerate(pieces):
        columns = pl.ds(pl.multiple_of((at[1] ^ k) * depth, LANES), depth)
        block = hidden_ref[:, columns].astype(F32)
        piece[:, :depth] = (block * inverse * gain_ref[:, columns]).astype(BF)
        piece[:, depth:] = extra


def norm_pieces(at, student_hidden, norm_gain, owner, doc_ids, n):
    capacity, width = student_hidden.shape
    rows, depth = capacity // n, width // n
    tokens = owner.shape[0]
    piece = jax.ShapeDtypeStruct((rows, depth + LANES), BF)
    whole = lambda i, s: (0, 0)
    return pl.pallas_call(
        norm_kernel,
        grid_spec=pltpu.PrefetchScalarGridSpec(
            num_scalar_prefetch=1,
            grid=(1,),
            in_specs=[
                pl.BlockSpec((rows, width), lambda i, s: (s[0], 0)),
                pl.BlockSpec((1, width), whole),
                pl.BlockSpec((tokens, 1), whole),
                pl.BlockSpec((1, tokens), whole),
            ],
            out_specs=[pl.BlockSpec((rows, depth + LANES), whole)] * n
            + [pl.BlockSpec((rows, 1), whole)],
        ),
        out_shape=[piece] * n + [jax.ShapeDtypeStruct((rows, 1), F32)],
        compiler_params=PARAMS,
        cost_estimate=pl.CostEstimate(
            flops=6 * rows * width, bytes_accessed=6 * rows * width, transcendentals=rows
        ),
    )(at, student_hidden, norm_gain[None, :], owner, doc_ids[None, :])


def pick_kernel(at, *refs):
    pieces, out_ref, drop_ref = refs[:-2], refs[-2], refs[-1]
    tokens, depth = out_ref.shape
    slots = pieces[0].shape[0]
    spots = slots * len(pieces)
    owner_row = jnp.zeros((1, tokens), F32)
    for k, piece in enumerate(pieces):
        tile = piece[0:16, depth:].astype(F32)[0:1]
        owner_row = owner_row + jnp.where(at[2] == k, tile, 0.0)
    owner = to_column(owner_row)
    earlier = lax.broadcasted_iota(I32, (tokens, tokens), 1) < lax.broadcasted_iota(
        I32, (tokens, tokens), 0
    )
    same = jnp.where(earlier & (owner == owner_row), 1.0, 0.0)
    rank = jnp.sum(same, axis=1, keepdims=True)
    peer = owner.astype(I32) ^ at[1]
    spot = (peer * slots).astype(F32) + rank
    take = (lax.broadcasted_iota(I32, (tokens, spots), 1) == spot.astype(I32)).astype(F32)
    stacked = jnp.concatenate([piece[:, :depth] for piece in pieces], axis=0)
    out_ref[...] = dot(take.astype(BF), stacked).astype(BF)
    spot_row = to_row(spot).astype(I32)
    drop = (lax.broadcasted_iota(I32, (spots, tokens), 0) == spot_row).astype(F32)
    drop_ref[...] = drop.astype(BF)


def pick_rows(at, pieces, tokens):
    slots, wide = pieces[0].shape
    depth = wide - LANES
    spots = slots * len(pieces)
    whole = lambda i, s: (0, 0)
    return pl.pallas_call(
        pick_kernel,
        grid_spec=pltpu.PrefetchScalarGridSpec(
            num_scalar_prefetch=1,
            grid=(1,),
            in_specs=[pl.BlockSpec((slots, wide), whole)] * len(pieces),
            out_specs=[
                pl.BlockSpec((tokens, depth), whole),
                pl.BlockSpec((spots, tokens), whole),
            ],
        ),
        out_shape=[
            jax.ShapeDtypeStruct((tokens, depth), BF),
            jax.ShapeDtypeStruct((spots, tokens), BF),
        ],
        compiler_params=PARAMS,
        cost_estimate=pl.CostEstimate(
            flops=2 * tokens * spots * depth, bytes_accessed=4 * spots * depth, transcendentals=0
        ),
    )(at, *pieces)


def attention_kernel(at, queries_ref, *refs):
    out_ref = refs[-1]
    n = (len(refs) - 1) // 2
    parcels, tiles = refs[:n], refs[n : 2 * n]
    tokens = queries_ref.shape[0]
    me = at[1]
    keys = jnp.concatenate([parcel[:tokens, :] for parcel in parcels], axis=0)
    values = jnp.concatenate([parcel[tokens:, :] for parcel in parcels], axis=0)
    docs = [tile[...].astype(F32)[1:2] for tile in tiles]
    doc_column = to_column(docs[0])
    query_pos = me * tokens + lax.broadcasted_iota(I32, (tokens, tokens), 0)
    within = lax.broadcasted_iota(I32, (tokens, tokens), 1)
    masks = []
    for k in range(n):
        near = (me ^ k) * tokens + within <= query_pos
        masks.append(jnp.where(near & (docs[k] == doc_column), 1.0, 0.0))
    allowed = jnp.concatenate(masks, axis=1) > 0.5
    scale_factor = 1.0 / math.sqrt(HD)
    for h in range(queries_ref.shape[1] // HD):
        columns = slice(h * HD, (h + 1) * HD)
        scores = dot(queries_ref[:, columns], keys, ((1,), (1,))) * scale_factor
        scores = jnp.where(allowed, scores, -1e30)
        top = jnp.max(scores, axis=1, keepdims=True)
        probs = jnp.where(allowed, jnp.exp(scores - top), 0.0)
        total = jnp.sum(probs, axis=1, keepdims=True)
        out_ref[:, columns] = (dot(probs.astype(BF), values) / total).astype(BF)


def attention_rows(at, queries, parcels, pieces):
    tokens, width = queries.shape
    n = len(parcels)
    wide = pieces[0].shape[1]
    whole = lambda i, s: (0, 0)
    return pl.pallas_call(
        attention_kernel,
        grid_spec=pltpu.PrefetchScalarGridSpec(
            num_scalar_prefetch=1,
            grid=(1,),
            in_specs=[pl.BlockSpec((tokens, width), whole)]
            + [pl.BlockSpec((2 * tokens, HD), whole)] * n
            + [pl.BlockSpec((16, LANES), lambda i, s: (0, wide // LANES - 1))] * n,
            out_specs=pl.BlockSpec((tokens, width), whole),
        ),
        out_shape=jax.ShapeDtypeStruct((tokens, width), BF),
        compiler_params=PARAMS,
        cost_estimate=pl.CostEstimate(
            flops=8 * n * tokens * tokens * width,
            bytes_accessed=4 * tokens * width,
            transcendentals=n * tokens * tokens * (width // HD),
        ),
    )(at, queries, *parcels, *pieces)


def rows_kernel(at, hidden_ref, gain_ref, inverse_ref, *refs):
    pieces, out_ref = refs[:-1], refs[-1]
    width = hidden_ref.shape[1]
    depth = width // len(pieces)
    inverse = inverse_ref[...]
    total = jnp.zeros_like(inverse)
    for k, piece in enumerate(pieces):
        columns = pl.ds(pl.multiple_of((at[1] ^ k) * depth, LANES), depth)
        gain_grad = piece[...].astype(F32) * gain_ref[:, columns]
        block = hidden_ref[:, columns].astype(F32)
        total = total + jnp.sum(gain_grad * block, axis=1, keepdims=True)
    lean = inverse * inverse * inverse * (total / width)
    for k, piece in enumerate(pieces):
        columns = pl.ds(pl.multiple_of((at[1] ^ k) * depth, LANES), depth)
        gain_grad = piece[...].astype(F32) * gain_ref[:, columns]
        block = hidden_ref[:, columns].astype(F32)
        out_ref[:, columns] = (inverse * gain_grad - lean * block).astype(BF)


def grad_rows(at, student_hidden, norm_gain, inverse, pieces):
    rows, depth = pieces[0].shape
    width = student_hidden.shape[1]
    whole = lambda i, s: (0, 0)
    return pl.pallas_call(
        rows_kernel,
        grid_spec=pltpu.PrefetchScalarGridSpec(
            num_scalar_prefetch=1,
            grid=(1,),
            in_specs=[
                pl.BlockSpec((rows, width), lambda i, s: (s[0], 0)),
                pl.BlockSpec((1, width), whole),
                pl.BlockSpec((rows, 1), whole),
            ]
            + [pl.BlockSpec((rows, depth), whole)] * len(pieces),
            out_specs=pl.BlockSpec((rows, width), whole),
        ),
        out_shape=jax.ShapeDtypeStruct((rows, width), BF),
        compiler_params=PARAMS,
        cost_estimate=pl.CostEstimate(
            flops=12 * rows * width, bytes_accessed=6 * rows * width, transcendentals=0
        ),
    )(at, student_hidden, norm_gain[None, :], inverse, *pieces)


def swap(x, axis, k=1):
    return lax.ppermute(x, axis, [(i, i ^ k) for i in range(lax.axis_size(axis))])


def turn(entries, by):
    odd, high = by % 2 == 1, by >= 2
    a, b, c, d = entries
    a, b = jnp.where(odd, b, a), jnp.where(odd, a, b)
    c, d = jnp.where(odd, d, c), jnp.where(odd, c, d)
    return [
        jnp.where(high, c, a),
        jnp.where(high, d, b),
        jnp.where(high, a, c),
        jnp.where(high, b, d),
    ]


def pairwise(
    teacher_queries, teacher_keys, teacher_values, doc_ids, owner, student_hidden, norm_gain, proj
):
    n = 4
    me = lax.axis_index("seq")
    side = lax.axis_index("side")
    mine = lax.axis_index("mp") * 2 + side
    rows = teacher_queries.shape[0]
    heads = teacher_queries.shape[1] // HD
    kv_local = teacher_keys.shape[1] // HD
    group = heads * 2 // kv_local
    capacity, width = student_hidden.shape
    slots = capacity // n
    depth = proj.shape[0]
    off = mine ^ me
    at = jnp.stack([mine, me, off]).astype(I32)

    made = norm_pieces(at, student_hidden, norm_gain, owner, doc_ids, n)
    inverse = made[n]
    pieces = [made[0]] + [swap(made[k], "seq", k) for k in range(1, n)]
    normed_own, drop = pick_rows(at, pieces, rows)

    mate = swap(normed_own, "side")
    far = swap(normed_own, "mp")
    far_mate = swap(far, "side")
    normed = turn([normed_own, mate, far, far_mate], off)

    head = side * heads // group
    parcel = jnp.concatenate(
        [
            lax.dynamic_slice_in_dim(teacher_keys, head * HD, HD, 1),
            lax.dynamic_slice_in_dim(teacher_values, head * HD, HD, 1),
        ]
    )
    parcel, mate = lax.optimization_barrier((parcel, mate))
    parcels = [parcel] + [swap(parcel, "seq", k) for k in range(1, n)]
    teacher_rows = attention_rows(at, teacher_queries, parcels, pieces)

    away = dot(normed[3], proj).astype(BF)
    got_over = swap(away, "seq", 1)
    over_own = dot(normed[2], proj)
    over = (over_own + got_over.astype(F32)).astype(BF)
    beside = dot(normed[1], proj).astype(BF)
    beside, over = lax.optimization_barrier((beside, over))
    got_far = swap(over, "seq", 2)
    got_beside = swap(beside, "seq", 1)
    own = lax.optimization_barrier(dot(normed[0], proj))
    predicted = own + got_beside.astype(F32) + got_far.astype(F32)
    delta = (predicted - teacher_rows.astype(F32)).astype(BF)

    delta_far = swap(delta, "seq", 2)
    delta_beside = swap(delta, "seq", 1)
    delta_last = swap(delta_far, "seq", 1)
    deltas = [delta, delta_beside, delta_far, delta_last]

    products = [dot(block, proj, ((1,), (1,))).astype(BF) for block in deltas]
    near, away_near, cross, away_cross = turn(products, off)
    got = swap(jnp.stack([away_near, away_cross]), "side")
    cross = (cross.astype(F32) + got[1].astype(F32)).astype(BF)
    crossed = swap(cross, "mp")
    near = lax.optimization_barrier(near.astype(F32) + got[0].astype(F32))
    feature_rows = (near + crossed.astype(F32)).astype(BF)
    leaving = [dot(drop[k * slots : (k + 1) * slots], feature_rows).astype(BF) for k in range(n)]
    arrived = [leaving[0]] + [swap(leaving[k], "seq", k) for k in range(1, n)]
    grad_own = grad_rows(at, student_hidden, norm_gain, inverse, arrived)

    grad_mate = swap(grad_own, "side")
    grad_far = swap(grad_own, "mp")
    grad_last = swap(grad_far, "side")
    grad_hidden = jnp.zeros((capacity, width), BF)
    for q, block in enumerate([grad_own, grad_mate, grad_far, grad_last]):
        grad_hidden = lax.dynamic_update_slice_in_dim(grad_hidden, block, (mine ^ q) * slots, 0)

    factor = 1.0 / math.sqrt(rows * n)
    grad_proj = dot(jnp.concatenate(normed), jnp.concatenate(deltas), ((0,), (0,))) * factor
    return (grad_hidden, grad_proj)


def general(
    teacher_queries, teacher_keys, teacher_values, doc_ids, owner, student_hidden, norm_gain, proj
):
    n = lax.axis_size("seq")
    me = lax.axis_index("seq")
    side = lax.axis_index("side")
    plane = lax.axis_size("mp") * lax.axis_size("side")
    mine = lax.axis_index("mp") * lax.axis_size("side") + side
    rows = teacher_queries.shape[0]
    heads = teacher_queries.shape[1] // HD
    kv_local = teacher_keys.shape[1] // HD
    group = heads * lax.axis_size("side") // kv_local
    width = student_hidden.shape[1]
    depth = proj.shape[0]
    capacity = student_hidden.shape[0]
    slots = capacity // n
    shared = n // plane
    held = shared * slots

    hidden = lax.dynamic_slice_in_dim(student_hidden, mine * held, held, 0).astype(F32)
    inverse_rms = lax.rsqrt(jnp.mean(hidden * hidden, axis=1, keepdims=True) + 1e-06)
    normed = (hidden * inverse_rms * norm_gain).astype(BF)
    normed_slots = lax.all_to_all(
        normed.reshape(held, n, depth).transpose(1, 0, 2), "seq", 0, 0, tiled=True
    )

    head = side * heads // group
    key_head = lax.dynamic_slice_in_dim(teacher_keys, head * HD, HD, 1)
    value_head = lax.dynamic_slice_in_dim(teacher_values, head * HD, HD, 1)
    small = jnp.stack([doc_ids, owner[:, 0]]).astype(BF)
    parcel = jnp.concatenate([key_head, value_head, jnp.pad(small, ((0, 14), (0, 0)))])
    parcel = lax.all_gather(parcel, "seq", axis=0, tiled=False)
    keys, values = parcel[:, :rows], parcel[:, rows : 2 * rows]
    docs = parcel[:, 2 * rows].astype(I32)
    owners = parcel[:, 2 * rows + 1].astype(I32)

    query_pos = me * rows + jnp.arange(rows, dtype=I32)
    key_pos = jnp.arange(n * rows, dtype=I32)
    allowed = (docs.reshape(-1)[None, :] == doc_ids[:, None]) & (
        key_pos[None, :] <= query_pos[:, None]
    )
    stacked = teacher_queries.reshape(rows, heads, HD).transpose(1, 0, 2)
    scores = jnp.einsum("hqd,kd->hqk", stacked, keys.reshape(-1, HD), preferred_element_type=F32)
    scores = jnp.where(allowed[None], scores * (1.0 / math.sqrt(HD)), -1e30)
    top = jnp.max(scores, axis=2, keepdims=True)
    probs = jnp.where(allowed[None], jnp.exp(scores - top), 0.0)
    totals = jnp.sum(probs, axis=2, keepdims=True)
    weighted = jnp.einsum(
        "hqk,kd->hqd", probs.astype(BF), values.reshape(-1, HD), preferred_element_type=F32
    )
    teacher_rows = (weighted / totals).astype(BF).transpose(1, 0, 2).reshape(rows, heads * HD)

    own_blocks = lax.dynamic_slice_in_dim(owners, mine * shared, shared, 0)
    order = jnp.arange(rows, dtype=I32)
    same = (own_blocks[:, :, None] == own_blocks[:, None, :]) & (order[:, None] > order[None, :])
    rank = jnp.sum(same.astype(I32), axis=2)
    spot = own_blocks * held + jnp.arange(shared, dtype=I32)[:, None] * slots + rank
    pick = (spot.reshape(-1)[:, None] == jnp.arange(n * held, dtype=I32)[None, :]).astype(BF)

    normed_own = dot(pick, normed_slots.reshape(n * held, depth)).astype(BF)
    normed_rows = lax.all_gather(normed_own, ("mp", "side"), axis=0, tiled=True)
    partial = dot(normed_rows, proj).astype(BF)
    predicted = lax.psum_scatter(partial, "seq", scatter_dimension=0, tiled=True).astype(F32)
    delta = (predicted - teacher_rows.astype(F32)).astype(BF)
    deltas = lax.all_gather(delta, "seq", axis=0, tiled=True)

    products = dot(deltas, proj, ((1,), (1,))).astype(BF)
    feature_rows = lax.psum_scatter(products, ("mp", "side"), scatter_dimension=0, tiled=True)
    feature_slots = dot(pick, feature_rows, ((0,), (0,))).astype(BF).reshape(n, held, depth)
    received = lax.all_to_all(feature_slots, "seq", 0, 0, tiled=True)
    feature_grad = received.transpose(1, 0, 2).reshape(held, width)

    gain_grad = feature_grad.astype(F32) * norm_gain
    mean_term = jnp.mean(gain_grad * hidden, axis=1, keepdims=True)
    grad_own = (inverse_rms * gain_grad - inverse_rms**3 * hidden * mean_term).astype(BF)
    grad_hidden = lax.all_gather(grad_own, ("mp", "side"), axis=0, tiled=True)

    grad_proj = dot(normed_rows, deltas, ((0,), (0,))) * (1.0 / math.sqrt(rows * n))
    return (grad_hidden, grad_proj)


def solution(mesh):
    sizes = mesh.shape
    paired = PAIRWISE and (sizes["seq"], sizes["mp"], sizes["side"]) == (4, 2, 2)
    return jax.shard_map(
        pairwise if paired else general,
        mesh=mesh,
        in_specs=(
            P(("groups", "seq"), ("mp", "side")),
            P(("groups", "seq"), "mp"),
            P(("groups", "seq"), "mp"),
            P(("groups", "seq")),
            P(("groups", "seq"), None),
            P(("groups", "seq"), None),
            P(),
            P("seq", ("mp", "side")),
        ),
        out_specs=(P(("groups", "seq"), None), P(("groups", "seq"), ("mp", "side"))),
        check_vma=False,
    )
```

```python
import functools
import math

import jax
import jax.numpy as jnp
from jax import lax
from jax.experimental import pallas as pl
from jax.experimental.pallas import tpu as pltpu
from jax.sharding import PartitionSpec as P

HD = 128
LANES = 128
BF = jnp.bfloat16
F32 = jnp.float32
I32 = jnp.int32
PARAMS = pltpu.CompilerParams(vmem_limit_bytes=16 * 1024 * 1024)
PAIRWISE = True


def dot(a, b, dims=((1,), (0,))):
    return lax.dot_general(a, b, (dims, ((), ())), preferred_element_type=F32)


def eye(size):
    return lax.broadcasted_iota(I32, (size, size), 0) == lax.broadcasted_iota(I32, (size, size), 1)


def to_row(column):
    return jnp.sum(jnp.where(eye(column.shape[0]), column, 0.0), axis=0, keepdims=True)


def to_column(row):
    return jnp.sum(jnp.where(eye(row.shape[1]), row, 0.0), axis=1, keepdims=True)


def indices():
    return lax.axis_index("seq"), lax.axis_index("mp") * 2 + lax.axis_index("side")


def call(kernel, shapes, args, flops, moved, transcendentals=0, **more):
    vmem = pl.BlockSpec(memory_space=pltpu.VMEM)
    options = dict(
        in_specs=[vmem] * len(args),
        out_specs=jax.tree.map(lambda s: vmem, shapes),
        compiler_params=PARAMS,
    )
    options.update(more)
    return pl.pallas_call(
        kernel,
        out_shape=shapes,
        cost_estimate=pl.CostEstimate(
            flops=flops, bytes_accessed=moved, transcendentals=transcendentals
        ),
        **options,
    )(*args)


def norm_kernel(student_ref, gain_ref, owner_ref, docs_ref, *refs):
    *pieces, inverse_ref, hidden_ref, arrived = refs
    me, mine = indices()
    copy = pltpu.make_async_copy(student_ref.at[mine], hidden_ref, arrived)
    copy.start()
    rows, width = hidden_ref.shape
    tiles = width // len(pieces) // LANES
    line = lax.broadcasted_iota(I32, (rows, LANES), 0)
    owner_row, docs_row = owner_ref[...].astype(F32), docs_ref[...].astype(F32)
    extra = jnp.where(line == 0, owner_row, jnp.where(line == 1, docs_row, 0.0)).astype(BF)
    for piece in pieces:
        piece[:, tiles * LANES :] = extra
    copy.wait()
    hidden = hidden_ref[...].astype(F32)
    inverse = lax.rsqrt(jnp.sum(hidden * hidden, axis=1, keepdims=True) / width + 1e-06)
    inverse_ref[...] = inverse
    for k, piece in enumerate(pieces):
        for tile in range(tiles):
            at = (me ^ k) * tiles + tile
            block = hidden_ref[:, pl.ds(pl.multiple_of(at * LANES, LANES), LANES)].astype(F32)
            normed = block * inverse * gain_ref[pl.ds(at, 1), :]
            piece[:, tile * LANES : (tile + 1) * LANES] = normed.astype(BF)


def norm_pieces(student, gain, owner, doc_ids):
    n, rows, width = student.shape
    piece = jax.ShapeDtypeStruct((rows, width // n + LANES), BF)
    vmem = pl.BlockSpec(memory_space=pltpu.VMEM)
    return call(
        norm_kernel,
        [piece] * n
        + [jax.ShapeDtypeStruct((rows, 1), F32), jax.ShapeDtypeStruct((rows, width), BF)],
        (student, gain, owner, doc_ids),
        6 * rows * width,
        6 * rows * width,
        in_specs=[pl.BlockSpec(memory_space=pl.ANY)] + [vmem] * 3,
        scratch_shapes=[pltpu.SemaphoreType.DMA],
        compiler_params=pltpu.CompilerParams(vmem_limit_bytes=60 * 1024 * 1024),
    )


def pick_kernel(*refs):
    *pieces, out_ref, drop_ref = refs
    me, mine = indices()
    tokens, depth = out_ref.shape
    slots = pieces[0].shape[0]
    spots = slots * len(pieces)
    owner_row = jnp.zeros((1, tokens), F32)
    for k, piece in enumerate(pieces):
        tile = piece[0:16, depth:].astype(F32)[0:1]
        owner_row = owner_row + jnp.where((me ^ mine) == k, tile, 0.0)
    owner = to_column(owner_row)
    earlier = lax.broadcasted_iota(I32, (tokens, tokens), 1) < lax.broadcasted_iota(
        I32, (tokens, tokens), 0
    )
    same = jnp.where(earlier & (owner == owner_row), 1.0, 0.0)
    rank = jnp.sum(same, axis=1, keepdims=True)
    peer = owner.astype(I32) ^ me
    spot = (peer * slots).astype(F32) + rank
    take = (lax.broadcasted_iota(I32, (tokens, spots), 1) == spot.astype(I32)).astype(F32)
    stacked = jnp.concatenate([piece[:, :depth] for piece in pieces], axis=0)
    out_ref[...] = dot(take.astype(BF), stacked).astype(BF)
    spot_row = to_row(spot).astype(I32)
    drop = (lax.broadcasted_iota(I32, (spots, tokens), 0) == spot_row).astype(F32)
    drop_ref[...] = drop.astype(BF)


def pick_rows(pieces, tokens):
    slots, wide = pieces[0].shape
    depth, spots = wide - LANES, slots * len(pieces)
    return call(
        pick_kernel,
        [jax.ShapeDtypeStruct((tokens, depth), BF), jax.ShapeDtypeStruct((spots, tokens), BF)],
        pieces,
        2 * tokens * spots * depth,
        4 * spots * depth,
    )


def attention_kernel(queries_ref, *refs):
    out_ref = refs[-1]
    n = (len(refs) - 1) // 2
    parcels, pieces = refs[:n], refs[n : 2 * n]
    tokens = queries_ref.shape[0]
    depth = pieces[0].shape[1] - LANES
    me, _ = indices()
    keys = jnp.concatenate([parcel[:tokens, :] for parcel in parcels], axis=0)
    values = jnp.concatenate([parcel[tokens:, :] for parcel in parcels], axis=0)
    docs = [piece[0:16, depth:].astype(F32)[1:2] for piece in pieces]
    doc_column = to_column(docs[0])
    query_pos = me * tokens + lax.broadcasted_iota(I32, (tokens, tokens), 0)
    within = lax.broadcasted_iota(I32, (tokens, tokens), 1)
    masks = []
    for k in range(n):
        near = (me ^ k) * tokens + within <= query_pos
        masks.append(jnp.where(near & (docs[k] == doc_column), 1.0, 0.0))
    allowed = jnp.concatenate(masks, axis=1) > 0.5
    scale_factor = 1.0 / math.sqrt(HD)
    for h in range(queries_ref.shape[1] // HD):
        columns = slice(h * HD, (h + 1) * HD)
        scores = dot(queries_ref[:, columns], keys, ((1,), (1,))) * scale_factor
        scores = jnp.where(allowed, scores, -1e30)
        top = jnp.max(scores, axis=1, keepdims=True)
        probs = jnp.where(allowed, jnp.exp(scores - top), 0.0)
        total = jnp.sum(probs, axis=1, keepdims=True)
        out_ref[:, columns] = (dot(probs.astype(BF), values) / total).astype(BF)


def attention_rows(queries, parcels, pieces):
    tokens, width = queries.shape
    n = len(parcels)
    return call(
        attention_kernel,
        jax.ShapeDtypeStruct((tokens, width), BF),
        (queries, *parcels, *pieces),
        0,
        4 * tokens * width,
    )


def route_kernel(first_ref, second_ref, third_ref, delta_ref, proj_ref, sent_ref, kept_ref, held):
    me, mine = indices()
    last = dot(delta_ref[...], proj_ref[...], ((1,), (1,))).astype(BF)
    for k, block in enumerate((first_ref[...], second_ref[...], third_ref[...], last)):
        held[k] = block
    off = me ^ mine
    kept_ref[0] = held[off]
    sent_ref[0] = held[off ^ 1]
    kept_ref[1] = held[off ^ 2]
    sent_ref[1] = held[off ^ 3]


def route_products(products, delta, proj):
    tokens, depth = products[0].shape
    pair = jax.ShapeDtypeStruct((2, tokens, depth), BF)
    return call(
        route_kernel,
        [pair, pair],
        (*products, delta, proj),
        2 * tokens * depth * proj.shape[1],
        2 * proj.size + 14 * tokens * depth,
        scratch_shapes=[pltpu.VMEM((4, tokens, depth), BF)],
    )


def rows_kernel(hidden_ref, gain_ref, inverse_ref, *refs):
    *pieces, out_ref = refs
    me, _ = indices()
    rows, width = hidden_ref.shape
    tiles = width // len(pieces) // LANES
    inverse = inverse_ref[...]
    total = jnp.zeros((rows, LANES), F32)
    for k, piece in enumerate(pieces):
        for tile in range(tiles):
            at = (me ^ k) * tiles + tile
            block = hidden_ref[:, pl.ds(pl.multiple_of(at * LANES, LANES), LANES)].astype(F32)
            grad = piece[:, tile * LANES : (tile + 1) * LANES].astype(F32)
            total = total + grad * gain_ref[pl.ds(at, 1), :] * block
    mean = jnp.sum(total, axis=1, keepdims=True) / width
    lean = inverse * inverse * inverse * mean
    for k, piece in enumerate(pieces):
        for tile in range(tiles):
            at = (me ^ k) * tiles + tile
            columns = pl.ds(pl.multiple_of(at * LANES, LANES), LANES)
            block = hidden_ref[:, columns].astype(F32)
            grad = piece[:, tile * LANES : (tile + 1) * LANES].astype(F32)
            grad = inverse * (grad * gain_ref[pl.ds(at, 1), :]) - lean * block
            out_ref[:, columns] = grad.astype(BF)


def grad_rows(hidden, gain, inverse, pieces):
    rows, width = hidden.shape
    return call(
        rows_kernel,
        jax.ShapeDtypeStruct((rows, width), BF),
        (hidden, gain, inverse, *pieces),
        12 * rows * width,
        6 * rows * width,
    )


def write_kernel(first, *refs):
    *blocks, out_ref, done = refs
    _, mine = indices()
    copies = [
        pltpu.make_async_copy(block, out_ref.at[mine ^ (first + q)], done.at[q])
        for q, block in enumerate(blocks)
    ]
    for copy in copies:
        copy.start()
    for copy in copies:
        copy.wait()


def write_rows(blocks, first, target=None):
    rows, width = blocks[0].shape
    hbm, vmem = pl.BlockSpec(memory_space=pltpu.HBM), pl.BlockSpec(memory_space=pltpu.VMEM)
    kernel = functools.partial(write_kernel, first)
    args, specs, aliases = tuple(blocks), [vmem] * len(blocks), {}
    if target is not None:
        kernel = lambda t, *refs: write_kernel(first, *refs)
        args, specs, aliases = (target, *args), [hbm] + specs, {0: 0}
    return call(
        kernel,
        jax.ShapeDtypeStruct((4, rows, width), BF),
        args,
        0,
        4 * len(blocks) * rows * width,
        in_specs=specs,
        out_specs=hbm,
        input_output_aliases=aliases,
        scratch_shapes=[pltpu.SemaphoreType.DMA((len(blocks),))],
    )


def swap(x, axis, k=1):
    return lax.ppermute(x, axis, [(i, i ^ k) for i in range(lax.axis_size(axis))])


def entry(entries, at):
    a, b, c, d = entries
    odd = at % 2 == 1
    return lax.optimization_barrier(
        jnp.where(at >= 2, jnp.where(odd, d, c), jnp.where(odd, b, a))
    )


def after(x, *others):
    return lax.optimization_barrier((x, *others))[0]


def pairwise(
    teacher_queries, teacher_keys, teacher_values, doc_ids, owner, student_hidden, norm_gain, proj
):
    n = 4
    me, mine = indices()
    side = lax.axis_index("side")
    rows = teacher_queries.shape[0]
    heads = teacher_queries.shape[1] // HD
    kv_local = teacher_keys.shape[1] // HD
    group = heads * 2 // kv_local
    capacity, width = student_hidden.shape
    slots = capacity // n
    off = mine ^ me
    student = student_hidden.reshape(n, slots, width)
    gain = norm_gain.reshape(width // LANES, LANES)

    *made, inverse, hidden = norm_pieces(student, gain, owner.T, doc_ids[None, :])
    pieces = [made[0]] + [swap(made[k], "seq", k) for k in range(1, n)]
    normed_own, drop = pick_rows(pieces, rows)

    mate = swap(normed_own, "side")
    far = swap(normed_own, "mp")
    far_mate = swap(far, "side")

    head = side * heads // group
    parcel = jnp.concatenate(
        [
            lax.dynamic_slice_in_dim(teacher_keys, head * HD, HD, 1),
            lax.dynamic_slice_in_dim(teacher_values, head * HD, HD, 1),
        ]
    )
    parcel = after(parcel, normed_own)
    parcels = [parcel] + [swap(parcel, "seq", k) for k in range(1, n)]
    far_mate = after(far_mate, *parcels)
    normed = [entry([normed_own, mate, far, far_mate], off ^ k) for k in range(n)]

    away = dot(normed[3], proj).astype(BF)
    over_own = lax.optimization_barrier(dot(after(normed[2], away), proj))
    beside = dot(after(normed[1], over_own), proj).astype(BF)
    got_over = after(swap(away, "seq", 1), over_own, beside)
    over = lax.optimization_barrier((over_own + got_over.astype(F32)).astype(BF))
    got_far = swap(over, "seq", 2)
    own = lax.optimization_barrier(dot(after(normed[0], over), proj))
    got_beside = swap(after(beside, own), "seq", 1)
    teacher_rows = attention_rows(after(teacher_queries, own), parcels, pieces)
    predicted = own + got_beside.astype(F32) + got_far.astype(F32)
    delta = (predicted - teacher_rows.astype(F32)).astype(BF)

    def product(block):
        return lax.optimization_barrier(dot(block, proj, ((1,), (1,))).astype(BF))

    delta_far = swap(delta, "seq", 2)
    own_product = product(delta)
    delta_beside = swap(after(delta, own_product), "seq", 1)
    delta_last = swap(delta_far, "seq", 1)
    deltas = [delta, delta_beside, delta_far, delta_last]
    products = [own_product, product(delta_beside), product(delta_far)]

    sent, kept = route_products(products, delta_last, proj)
    got = swap(sent, "side")
    cross = lax.optimization_barrier((kept[1].astype(F32) + got[1].astype(F32)).astype(BF))
    crossed = swap(cross, "mp")
    near = lax.optimization_barrier(kept[0].astype(F32) + after(got[0], cross).astype(F32))
    feature_rows = (near + crossed.astype(F32)).astype(BF)
    leaving = [dot(drop[k * slots : (k + 1) * slots], feature_rows).astype(BF) for k in range(n)]
    arrived = [leaving[0]] + [swap(leaving[k], "seq", k) for k in range(1, n)]
    grad_own = grad_rows(hidden, gain, inverse, arrived)

    grad_mate = swap(grad_own, "side")
    grad_far = swap(grad_own, "mp")
    grad_last = swap(grad_far, "side")
    grad_hidden = write_rows([grad_own, grad_mate, grad_far], 0)
    grad_hidden = write_rows([grad_last], 3, grad_hidden).reshape(capacity, width)

    factor = 1.0 / math.sqrt(rows * n)
    grad_proj = dot(jnp.concatenate(normed), jnp.concatenate(deltas), ((0,), (0,))) * factor
    return (grad_hidden, grad_proj)


def general(
    teacher_queries, teacher_keys, teacher_values, doc_ids, owner, student_hidden, norm_gain, proj
):
    n = lax.axis_size("seq")
    me = lax.axis_index("seq")
    side = lax.axis_index("side")
    plane = lax.axis_size("mp") * lax.axis_size("side")
    mine = lax.axis_index("mp") * lax.axis_size("side") + side
    rows = teacher_queries.shape[0]
    heads = teacher_queries.shape[1] // HD
    kv_local = teacher_keys.shape[1] // HD
    group = heads * lax.axis_size("side") // kv_local
    width = student_hidden.shape[1]
    depth = proj.shape[0]
    capacity = student_hidden.shape[0]
    slots = capacity // n
    shared = n // plane
    held = shared * slots

    hidden = lax.dynamic_slice_in_dim(student_hidden, mine * held, held, 0).astype(F32)
    inverse_rms = lax.rsqrt(jnp.mean(hidden * hidden, axis=1, keepdims=True) + 1e-06)
    normed = (hidden * inverse_rms * norm_gain).astype(BF)
    normed_slots = lax.all_to_all(
        normed.reshape(held, n, depth).transpose(1, 0, 2), "seq", 0, 0, tiled=True
    )

    head = side * heads // group
    key_head = lax.dynamic_slice_in_dim(teacher_keys, head * HD, HD, 1)
    value_head = lax.dynamic_slice_in_dim(teacher_values, head * HD, HD, 1)
    small = jnp.stack([doc_ids, owner[:, 0]]).astype(BF)
    parcel = jnp.concatenate([key_head, value_head, jnp.pad(small, ((0, 14), (0, 0)))])
    parcel = lax.all_gather(parcel, "seq", axis=0, tiled=False)
    keys, values = parcel[:, :rows], parcel[:, rows : 2 * rows]
    docs = parcel[:, 2 * rows].astype(I32)
    owners = parcel[:, 2 * rows + 1].astype(I32)

    query_pos = me * rows + jnp.arange(rows, dtype=I32)
    key_pos = jnp.arange(n * rows, dtype=I32)
    allowed = (docs.reshape(-1)[None, :] == doc_ids[:, None]) & (
        key_pos[None, :] <= query_pos[:, None]
    )
    stacked = teacher_queries.reshape(rows, heads, HD).transpose(1, 0, 2)
    scores = jnp.einsum("hqd,kd->hqk", stacked, keys.reshape(-1, HD), preferred_element_type=F32)
    scores = jnp.where(allowed[None], scores * (1.0 / math.sqrt(HD)), -1e30)
    top = jnp.max(scores, axis=2, keepdims=True)
    probs = jnp.where(allowed[None], jnp.exp(scores - top), 0.0)
    totals = jnp.sum(probs, axis=2, keepdims=True)
    weighted = jnp.einsum(
        "hqk,kd->hqd", probs.astype(BF), values.reshape(-1, HD), preferred_element_type=F32
    )
    teacher_rows = (weighted / totals).astype(BF).transpose(1, 0, 2).reshape(rows, heads * HD)

    own_blocks = lax.dynamic_slice_in_dim(owners, mine * shared, shared, 0)
    order = jnp.arange(rows, dtype=I32)
    same = (own_blocks[:, :, None] == own_blocks[:, None, :]) & (order[:, None] > order[None, :])
    rank = jnp.sum(same.astype(I32), axis=2)
    spot = own_blocks * held + jnp.arange(shared, dtype=I32)[:, None] * slots + rank
    pick = (spot.reshape(-1)[:, None] == jnp.arange(n * held, dtype=I32)[None, :]).astype(BF)

    normed_own = dot(pick, normed_slots.reshape(n * held, depth)).astype(BF)
    normed_rows = lax.all_gather(normed_own, ("mp", "side"), axis=0, tiled=True)
    partial = dot(normed_rows, proj).astype(BF)
    predicted = lax.psum_scatter(partial, "seq", scatter_dimension=0, tiled=True).astype(F32)
    delta = (predicted - teacher_rows.astype(F32)).astype(BF)
    deltas = lax.all_gather(delta, "seq", axis=0, tiled=True)

    products = dot(deltas, proj, ((1,), (1,))).astype(BF)
    feature_rows = lax.psum_scatter(products, ("mp", "side"), scatter_dimension=0, tiled=True)
    feature_slots = dot(pick, feature_rows, ((0,), (0,))).astype(BF).reshape(n, held, depth)
    received = lax.all_to_all(feature_slots, "seq", 0, 0, tiled=True)
    feature_grad = received.transpose(1, 0, 2).reshape(held, width)

    gain_grad = feature_grad.astype(F32) * norm_gain
    mean_term = jnp.mean(gain_grad * hidden, axis=1, keepdims=True)
    grad_own = (inverse_rms * gain_grad - inverse_rms**3 * hidden * mean_term).astype(BF)
    grad_hidden = lax.all_gather(grad_own, ("mp", "side"), axis=0, tiled=True)

    grad_proj = dot(normed_rows, deltas, ((0,), (0,))) * (1.0 / math.sqrt(rows * n))
    return (grad_hidden, grad_proj)


def solution(mesh):
    sizes = mesh.shape
    paired = PAIRWISE and (sizes["seq"], sizes["mp"], sizes["side"]) == (4, 2, 2)
    return jax.shard_map(
        pairwise if paired else general,
        mesh=mesh,
        in_specs=(
            P(("groups", "seq"), ("mp", "side")),
            P(("groups", "seq"), "mp"),
            P(("groups", "seq"), "mp"),
            P(("groups", "seq")),
            P(("groups", "seq"), None),
            P(("groups", "seq"), None),
            P(),
            P("seq", ("mp", "side")),
        ),
        out_specs=(P(("groups", "seq"), None), P(("groups", "seq"), ("mp", "side"))),
        check_vma=False,
    )
```

```python
import functools
import math

import jax
import jax.numpy as jnp
from jax import lax
from jax.experimental import pallas as pl
from jax.experimental.pallas import tpu as pltpu
from jax.sharding import PartitionSpec as P

HD = 128
LANES = 128
BF = jnp.bfloat16
F32 = jnp.float32
I32 = jnp.int32
PARAMS = pltpu.CompilerParams(vmem_limit_bytes=16 * 1024 * 1024)
PAIRWISE = True


def dot(a, b, dims=((1,), (0,))):
    return lax.dot_general(a, b, (dims, ((), ())), preferred_element_type=F32)


def eye(size):
    return lax.broadcasted_iota(I32, (size, size), 0) == lax.broadcasted_iota(I32, (size, size), 1)


def to_row(column):
    return jnp.sum(jnp.where(eye(column.shape[0]), column, 0.0), axis=0, keepdims=True)


def to_column(row):
    return jnp.sum(jnp.where(eye(row.shape[1]), row, 0.0), axis=1, keepdims=True)


def indices():
    return lax.axis_index("seq"), lax.axis_index("mp") * 2 + lax.axis_index("side")


def call(kernel, shapes, args, flops, moved, transcendentals=0, **more):
    vmem = pl.BlockSpec(memory_space=pltpu.VMEM)
    options = dict(
        in_specs=[vmem] * len(args),
        out_specs=jax.tree.map(lambda s: vmem, shapes),
        compiler_params=PARAMS,
    )
    options.update(more)
    return pl.pallas_call(
        kernel,
        out_shape=shapes,
        cost_estimate=pl.CostEstimate(
            flops=flops, bytes_accessed=moved, transcendentals=transcendentals
        ),
        **options,
    )(*args)


def norm_kernel(student_ref, gain_ref, owner_ref, docs_ref, *refs):
    *pieces, inverse_ref, hidden_ref = refs
    me, mine = indices()
    hidden_ref[...] = student_ref[mine]
    rows, width = hidden_ref.shape
    tiles = width // len(pieces) // LANES
    line = lax.broadcasted_iota(I32, (rows, LANES), 0)
    owner_row, docs_row = owner_ref[...].astype(F32), docs_ref[...].astype(F32)
    extra = jnp.where(line == 0, owner_row, jnp.where(line == 1, docs_row, 0.0)).astype(BF)
    for piece in pieces:
        piece[:, tiles * LANES :] = extra
    hidden = hidden_ref[...].astype(F32)
    inverse = lax.rsqrt(jnp.sum(hidden * hidden, axis=1, keepdims=True) / width + 1e-06)
    inverse_ref[...] = inverse
    for k, piece in enumerate(pieces):
        for tile in range(tiles):
            at = (me ^ k) * tiles + tile
            block = hidden_ref[:, pl.ds(pl.multiple_of(at * LANES, LANES), LANES)].astype(F32)
            normed = block * inverse * gain_ref[pl.ds(at, 1), :]
            piece[:, tile * LANES : (tile + 1) * LANES] = normed.astype(BF)


def norm_pieces(student, gain, owner, doc_ids):
    n, rows, width = student.shape
    piece = jax.ShapeDtypeStruct((rows, width // n + LANES), BF)
    return call(
        norm_kernel,
        [piece] * n
        + [jax.ShapeDtypeStruct((rows, 1), F32), jax.ShapeDtypeStruct((rows, width), BF)],
        (student, gain, owner, doc_ids),
        6 * rows * width,
        6 * rows * width,
    )


def pick_kernel(*refs):
    *pieces, out_ref, drop_ref = refs
    pieces = pieces[::-1]
    me, mine = indices()
    tokens, depth = out_ref.shape
    slots = pieces[0].shape[0]
    spots = slots * len(pieces)
    owner_row = jnp.zeros((1, tokens), F32)
    for k, piece in enumerate(pieces):
        tile = piece[0:16, depth:].astype(F32)[0:1]
        owner_row = owner_row + jnp.where((me ^ mine) == k, tile, 0.0)
    owner = to_column(owner_row)
    earlier = lax.broadcasted_iota(I32, (tokens, tokens), 1) < lax.broadcasted_iota(
        I32, (tokens, tokens), 0
    )
    same = jnp.where(earlier & (owner == owner_row), 1.0, 0.0)
    rank = jnp.sum(same, axis=1, keepdims=True)
    peer = owner.astype(I32) ^ me
    spot = (peer * slots).astype(F32) + rank
    take = (lax.broadcasted_iota(I32, (tokens, spots), 1) == spot.astype(I32)).astype(F32)
    stacked = jnp.concatenate([piece[:, :depth] for piece in pieces], axis=0)
    out_ref[...] = dot(take.astype(BF), stacked).astype(BF)
    spot_row = to_row(spot).astype(I32)
    drop = (lax.broadcasted_iota(I32, (spots, tokens), 0) == spot_row).astype(F32)
    drop_ref[...] = drop.astype(BF)


def pick_rows(pieces, tokens):
    slots, wide = pieces[0].shape
    depth, spots = wide - LANES, slots * len(pieces)
    return call(
        pick_kernel,
        [jax.ShapeDtypeStruct((tokens, depth), BF), jax.ShapeDtypeStruct((spots, tokens), BF)],
        pieces[::-1],
        2 * tokens * spots * depth,
        4 * spots * depth,
    )


def attention_kernel(queries_ref, *refs):
    out_ref = refs[-1]
    n = (len(refs) - 1) // 2
    parcels, pieces = refs[:n], refs[n : 2 * n]
    tokens = queries_ref.shape[0]
    depth = pieces[0].shape[1] - LANES
    me, _ = indices()
    keys = jnp.concatenate([parcel[:tokens, :] for parcel in parcels], axis=0)
    values = jnp.concatenate([parcel[tokens:, :] for parcel in parcels], axis=0)
    docs = [piece[0:16, depth:].astype(F32)[1:2] for piece in pieces]
    doc_column = to_column(docs[0])
    query_pos = me * tokens + lax.broadcasted_iota(I32, (tokens, tokens), 0)
    within = lax.broadcasted_iota(I32, (tokens, tokens), 1)
    masks = []
    for k in range(n):
        near = (me ^ k) * tokens + within <= query_pos
        masks.append(jnp.where(near & (docs[k] == doc_column), 1.0, 0.0))
    allowed = jnp.concatenate(masks, axis=1) > 0.5
    scale_factor = 1.0 / math.sqrt(HD)
    for h in range(queries_ref.shape[1] // HD):
        columns = slice(h * HD, (h + 1) * HD)
        scores = dot(queries_ref[:, columns], keys, ((1,), (1,))) * scale_factor
        scores = jnp.where(allowed, scores, -1e30)
        top = jnp.max(scores, axis=1, keepdims=True)
        probs = jnp.where(allowed, jnp.exp(scores - top), 0.0)
        total = jnp.sum(probs, axis=1, keepdims=True)
        out_ref[:, columns] = (dot(probs.astype(BF), values) / total).astype(BF)


def attention_rows(queries, parcels, pieces):
    tokens, width = queries.shape
    n = len(parcels)
    return call(
        attention_kernel,
        jax.ShapeDtypeStruct((tokens, width), BF),
        (queries, *parcels, *pieces),
        0,
        4 * tokens * width,
    )


def pick_entry(refs, at):
    d, c, b, a = (ref[...] for ref in refs)
    odd = at % 2 == 1
    return jnp.where(at >= 2, jnp.where(odd, d, c), jnp.where(odd, b, a))


def away_kernel(*refs):
    *entries, proj_ref, out_ref = refs
    me, mine = indices()
    block = pick_entry(entries, me ^ mine ^ 3)
    out_ref[...] = dot(block, proj_ref[...]).astype(BF)


def kept_kernel(*refs):
    *entries, proj_ref, own_ref, over_ref, normed_ref = refs
    me, mine = indices()
    rows = entries[0].shape[0]
    for k, spot in enumerate((0, 2, 1, 3)):
        normed_ref[spot * rows : (spot + 1) * rows, :] = pick_entry(entries, me ^ mine ^ k)
    columns = 256
    for first in range(0, proj_ref.shape[1], columns):
        part = slice(first, first + columns)
        product = dot(normed_ref[: 2 * rows, :], proj_ref[:, part])
        own_ref[:, part] = product[:rows]
        over_ref[:, part] = product[rows:]


def beside_kernel(normed_ref, proj_ref, out_ref):
    rows = out_ref.shape[0]
    out_ref[...] = dot(normed_ref[2 * rows : 3 * rows, :], proj_ref[...]).astype(BF)


def away_partial(entries, proj):
    rows, depth = entries[0].shape
    out = jax.ShapeDtypeStruct((rows, proj.shape[1]), BF)
    return call(away_kernel, out, (*entries, proj), 0, 0)


def kept_partials(entries, proj):
    rows, depth = entries[0].shape
    out = jax.ShapeDtypeStruct((rows, proj.shape[1]), F32)
    shapes = [out, out, jax.ShapeDtypeStruct((4 * rows, depth), BF)]
    return call(kept_kernel, shapes, (*entries, proj), 0, 0)


def beside_partial(normed, proj):
    out = jax.ShapeDtypeStruct((normed.shape[0] // 4, proj.shape[1]), BF)
    return call(beside_kernel, out, (normed, proj), 0, 0)


def product_kernel(delta_ref, proj_ref, out_ref):
    out_ref[...] = dot(delta_ref[...], proj_ref[...], ((1,), (1,))).astype(BF)


def product(delta, proj):
    out = jax.ShapeDtypeStruct((delta.shape[0], proj.shape[0]), BF)
    return call(product_kernel, out, (delta, proj), 0, 0)


def route_kernel(first_ref, second_ref, third_ref, delta_ref, proj_ref, sent_ref, kept_ref, held):
    me, mine = indices()
    last = dot(delta_ref[...], proj_ref[...], ((1,), (1,))).astype(BF)
    for k, block in enumerate((first_ref[...], second_ref[...], third_ref[...], last)):
        held[k] = block
    off = me ^ mine
    kept_ref[0] = held[off]
    sent_ref[0] = held[off ^ 1]
    kept_ref[1] = held[off ^ 2]
    sent_ref[1] = held[off ^ 3]


def route_products(products, delta, proj):
    tokens, depth = products[0].shape
    pair = jax.ShapeDtypeStruct((2, tokens, depth), BF)
    return call(
        route_kernel,
        [pair, pair],
        (*products, delta, proj),
        0,
        0,
        scratch_shapes=[pltpu.VMEM((4, tokens, depth), BF)],
    )


def rows_kernel(hidden_ref, gain_ref, inverse_ref, *refs):
    *pieces, out_ref = refs
    me, _ = indices()
    rows, width = hidden_ref.shape
    tiles = width // len(pieces) // LANES
    inverse = inverse_ref[...]
    total = jnp.zeros((rows, LANES), F32)
    for k, piece in enumerate(pieces):
        for tile in range(tiles):
            at = (me ^ k) * tiles + tile
            block = hidden_ref[:, pl.ds(pl.multiple_of(at * LANES, LANES), LANES)].astype(F32)
            grad = piece[:, tile * LANES : (tile + 1) * LANES].astype(F32)
            total = total + grad * gain_ref[pl.ds(at, 1), :] * block
    mean = jnp.sum(total, axis=1, keepdims=True) / width
    lean = inverse * inverse * inverse * mean
    for k, piece in enumerate(pieces):
        for tile in range(tiles):
            at = (me ^ k) * tiles + tile
            columns = pl.ds(pl.multiple_of(at * LANES, LANES), LANES)
            block = hidden_ref[:, columns].astype(F32)
            grad = piece[:, tile * LANES : (tile + 1) * LANES].astype(F32)
            grad = inverse * (grad * gain_ref[pl.ds(at, 1), :]) - lean * block
            out_ref[:, columns] = grad.astype(BF)


def grad_rows(hidden, gain, inverse, pieces):
    rows, width = hidden.shape
    return call(
        rows_kernel,
        jax.ShapeDtypeStruct((rows, width), BF),
        (hidden, gain, inverse, *pieces),
        12 * rows * width,
        6 * rows * width,
    )


def write_kernel(first, *refs):
    *blocks, out_ref, done = refs
    _, mine = indices()
    copies = [
        pltpu.make_async_copy(block, out_ref.at[mine ^ (first + q)], done.at[q])
        for q, block in enumerate(blocks)
    ]
    for copy in copies:
        copy.start()
    for copy in copies:
        copy.wait()


def write_rows(blocks, first, target=None):
    rows, width = blocks[0].shape
    hbm, vmem = pl.BlockSpec(memory_space=pltpu.HBM), pl.BlockSpec(memory_space=pltpu.VMEM)
    kernel = functools.partial(write_kernel, first)
    args, specs, aliases = tuple(blocks), [vmem] * len(blocks), {}
    if target is not None:
        kernel = lambda t, *refs: write_kernel(first, *refs)
        args, specs, aliases = (target, *args), [hbm] + specs, {0: 0}
    return call(
        kernel,
        jax.ShapeDtypeStruct((4, rows, width), BF),
        args,
        0,
        4 * len(blocks) * rows * width,
        in_specs=specs,
        out_specs=hbm,
        input_output_aliases=aliases,
        scratch_shapes=[pltpu.SemaphoreType.DMA((len(blocks),))],
    )


def swap(x, axis, k=1):
    return lax.ppermute(x, axis, [(i, i ^ k) for i in range(lax.axis_size(axis))])


def exchange(blocks):
    got = {k: swap(blocks[k], "seq", k) for k in reversed(range(1, len(blocks)))}
    return [got[k] for k in range(1, len(blocks))]


def after(x, *others):
    return lax.optimization_barrier((x, *others))[0]


def pairwise(
    teacher_queries, teacher_keys, teacher_values, doc_ids, owner, student_hidden, norm_gain, proj
):
    n = 4
    me, mine = indices()
    side = lax.axis_index("side")
    rows = teacher_queries.shape[0]
    heads = teacher_queries.shape[1] // HD
    kv_local = teacher_keys.shape[1] // HD
    group = heads * 2 // kv_local
    capacity, width = student_hidden.shape
    slots = capacity // n
    student = student_hidden.reshape(n, slots, width)
    gain = norm_gain.reshape(width // LANES, LANES)

    *made, inverse, hidden = norm_pieces(student, gain, owner.T, doc_ids[None, :])
    pieces = [made[0]] + exchange(made)
    normed_own, drop = pick_rows(pieces, rows)

    head = side * heads // group
    parcel = jnp.concatenate(
        [
            lax.dynamic_slice_in_dim(teacher_keys, head * HD, HD, 1),
            lax.dynamic_slice_in_dim(teacher_values, head * HD, HD, 1),
        ]
    )
    parcel = after(lax.optimization_barrier(parcel), normed_own)

    far = swap(normed_own, "mp")
    mate = swap(after(normed_own, parcel), "side")
    parcels = [parcel] + exchange([parcel] * n)
    far_mate = swap(after(far, mate, *parcels), "side")
    entries = [far_mate, far, mate, normed_own]

    away = away_partial(entries, proj)
    own, over_own, normed = kept_partials([after(e, away) for e in entries], proj)
    got_over = after(swap(away, "seq", 1), over_own)
    over = lax.optimization_barrier((over_own + got_over.astype(F32)).astype(BF))
    got_far = swap(over, "seq", 2)
    got_beside = swap(beside_partial(after(normed, over), proj), "seq", 1)
    teacher_rows = attention_rows(after(teacher_queries, over), parcels, pieces)
    predicted = lax.optimization_barrier(own + got_far.astype(F32)) + got_beside.astype(F32)
    delta = (predicted - teacher_rows.astype(F32)).astype(BF)

    delta_far = swap(delta, "seq", 2)
    own_product = product(delta, proj)
    delta_beside = swap(after(delta, own_product), "seq", 1)
    delta_last = swap(delta_far, "seq", 1)
    deltas = [delta, delta_beside, delta_far, delta_last]
    products = [own_product, product(delta_beside, proj), product(delta_far, proj)]

    sent, kept = route_products(products, delta_last, proj)
    got = swap(sent, "side")
    cross = lax.optimization_barrier((kept[1].astype(F32) + got[1].astype(F32)).astype(BF))
    crossed = swap(cross, "mp")
    near = lax.optimization_barrier(kept[0].astype(F32) + after(got[0], cross).astype(F32))
    feature_rows = (near + crossed.astype(F32)).astype(BF)
    leaving = [dot(drop[k * slots : (k + 1) * slots], feature_rows).astype(BF) for k in range(n)]
    arrived = [leaving[0]] + exchange(leaving)
    grad_own = grad_rows(hidden, gain, inverse, arrived)

    factor = 1.0 / math.sqrt(rows * n)
    deltas = jnp.concatenate([deltas[k] for k in (0, 2, 1, 3)])
    grad_proj = lax.optimization_barrier(dot(normed, after(deltas, cross), ((0,), (0,))) * factor)

    grad_mate = swap(grad_own, "side")
    grad_far = swap(grad_own, "mp")
    grad_last = swap(after(grad_far, grad_proj), "side")
    grad_hidden = write_rows([grad_own, grad_mate, grad_far], 0)
    grad_hidden = write_rows([grad_last], 3, grad_hidden).reshape(capacity, width)
    return (grad_hidden, grad_proj)


def general(
    teacher_queries, teacher_keys, teacher_values, doc_ids, owner, student_hidden, norm_gain, proj
):
    n = lax.axis_size("seq")
    me = lax.axis_index("seq")
    side = lax.axis_index("side")
    plane = lax.axis_size("mp") * lax.axis_size("side")
    mine = lax.axis_index("mp") * lax.axis_size("side") + side
    rows = teacher_queries.shape[0]
    heads = teacher_queries.shape[1] // HD
    kv_local = teacher_keys.shape[1] // HD
    group = heads * lax.axis_size("side") // kv_local
    width = student_hidden.shape[1]
    depth = proj.shape[0]
    capacity = student_hidden.shape[0]
    slots = capacity // n
    shared = n // plane
    held = shared * slots

    hidden = lax.dynamic_slice_in_dim(student_hidden, mine * held, held, 0).astype(F32)
    inverse_rms = lax.rsqrt(jnp.mean(hidden * hidden, axis=1, keepdims=True) + 1e-06)
    normed = (hidden * inverse_rms * norm_gain).astype(BF)
    normed_slots = lax.all_to_all(
        normed.reshape(held, n, depth).transpose(1, 0, 2), "seq", 0, 0, tiled=True
    )

    head = side * heads // group
    key_head = lax.dynamic_slice_in_dim(teacher_keys, head * HD, HD, 1)
    value_head = lax.dynamic_slice_in_dim(teacher_values, head * HD, HD, 1)
    small = jnp.stack([doc_ids, owner[:, 0]]).astype(BF)
    parcel = jnp.concatenate([key_head, value_head, jnp.pad(small, ((0, 14), (0, 0)))])
    parcel = lax.all_gather(parcel, "seq", axis=0, tiled=False)
    keys, values = parcel[:, :rows], parcel[:, rows : 2 * rows]
    docs = parcel[:, 2 * rows].astype(I32)
    owners = parcel[:, 2 * rows + 1].astype(I32)

    query_pos = me * rows + jnp.arange(rows, dtype=I32)
    key_pos = jnp.arange(n * rows, dtype=I32)
    allowed = (docs.reshape(-1)[None, :] == doc_ids[:, None]) & (
        key_pos[None, :] <= query_pos[:, None]
    )
    stacked = teacher_queries.reshape(rows, heads, HD).transpose(1, 0, 2)
    scores = jnp.einsum("hqd,kd->hqk", stacked, keys.reshape(-1, HD), preferred_element_type=F32)
    scores = jnp.where(allowed[None], scores * (1.0 / math.sqrt(HD)), -1e30)
    top = jnp.max(scores, axis=2, keepdims=True)
    probs = jnp.where(allowed[None], jnp.exp(scores - top), 0.0)
    totals = jnp.sum(probs, axis=2, keepdims=True)
    weighted = jnp.einsum(
        "hqk,kd->hqd", probs.astype(BF), values.reshape(-1, HD), preferred_element_type=F32
    )
    teacher_rows = (weighted / totals).astype(BF).transpose(1, 0, 2).reshape(rows, heads * HD)

    own_blocks = lax.dynamic_slice_in_dim(owners, mine * shared, shared, 0)
    order = jnp.arange(rows, dtype=I32)
    same = (own_blocks[:, :, None] == own_blocks[:, None, :]) & (order[:, None] > order[None, :])
    rank = jnp.sum(same.astype(I32), axis=2)
    spot = own_blocks * held + jnp.arange(shared, dtype=I32)[:, None] * slots + rank
    pick = (spot.reshape(-1)[:, None] == jnp.arange(n * held, dtype=I32)[None, :]).astype(BF)

    normed_own = dot(pick, normed_slots.reshape(n * held, depth)).astype(BF)
    normed_rows = lax.all_gather(normed_own, ("mp", "side"), axis=0, tiled=True)
    partial = dot(normed_rows, proj).astype(BF)
    predicted = lax.psum_scatter(partial, "seq", scatter_dimension=0, tiled=True).astype(F32)
    delta = (predicted - teacher_rows.astype(F32)).astype(BF)
    deltas = lax.all_gather(delta, "seq", axis=0, tiled=True)

    products = dot(deltas, proj, ((1,), (1,))).astype(BF)
    feature_rows = lax.psum_scatter(products, ("mp", "side"), scatter_dimension=0, tiled=True)
    feature_slots = dot(pick, feature_rows, ((0,), (0,))).astype(BF).reshape(n, held, depth)
    received = lax.all_to_all(feature_slots, "seq", 0, 0, tiled=True)
    feature_grad = received.transpose(1, 0, 2).reshape(held, width)

    gain_grad = feature_grad.astype(F32) * norm_gain
    mean_term = jnp.mean(gain_grad * hidden, axis=1, keepdims=True)
    grad_own = (inverse_rms * gain_grad - inverse_rms**3 * hidden * mean_term).astype(BF)
    grad_hidden = lax.all_gather(grad_own, ("mp", "side"), axis=0, tiled=True)

    grad_proj = dot(normed_rows, deltas, ((0,), (0,))) * (1.0 / math.sqrt(rows * n))
    return (grad_hidden, grad_proj)


def solution(mesh):
    sizes = mesh.shape
    paired = PAIRWISE and (sizes["seq"], sizes["mp"], sizes["side"]) == (4, 2, 2)
    return jax.shard_map(
        pairwise if paired else general,
        mesh=mesh,
        in_specs=(
            P(("groups", "seq"), ("mp", "side")),
            P(("groups", "seq"), "mp"),
            P(("groups", "seq"), "mp"),
            P(("groups", "seq")),
            P(("groups", "seq"), None),
            P(("groups", "seq"), None),
            P(),
            P("seq", ("mp", "side")),
        ),
        out_specs=(P(("groups", "seq"), None), P(("groups", "seq"), ("mp", "side"))),
        check_vma=False,
    )
```

```python
import functools
import math

import jax
import jax.numpy as jnp
from jax import lax
from jax.experimental import pallas as pl
from jax.experimental.pallas import tpu as pltpu
from jax.sharding import PartitionSpec as P

HD = 128
LANES = 128
BF = jnp.bfloat16
F32 = jnp.float32
I32 = jnp.int32
PARAMS = pltpu.CompilerParams(vmem_limit_bytes=16 * 1024 * 1024)
NORM_MB = 52
PAIRWISE = True


def dot(a, b, dims=((1,), (0,))):
    return lax.dot_general(a, b, (dims, ((), ())), preferred_element_type=F32)


def eye(size):
    return lax.broadcasted_iota(I32, (size, size), 0) == lax.broadcasted_iota(I32, (size, size), 1)


def to_row(column):
    return jnp.sum(jnp.where(eye(column.shape[0]), column, 0.0), axis=0, keepdims=True)


def to_column(row):
    return jnp.sum(jnp.where(eye(row.shape[1]), row, 0.0), axis=1, keepdims=True)


def indices():
    return lax.axis_index("seq"), lax.axis_index("mp") * 2 + lax.axis_index("side")


def call(kernel, shapes, args, flops, moved, transcendentals=0, **more):
    vmem = pl.BlockSpec(memory_space=pltpu.VMEM)
    options = dict(
        in_specs=[vmem] * len(args),
        out_specs=jax.tree.map(lambda s: vmem, shapes),
        compiler_params=PARAMS,
    )
    options.update(more)
    return pl.pallas_call(
        kernel,
        out_shape=shapes,
        cost_estimate=pl.CostEstimate(
            flops=flops, bytes_accessed=moved, transcendentals=transcendentals
        ),
        **options,
    )(*args)


def inverse_rms(hidden):
    width = hidden.shape[1]
    return lax.rsqrt(jnp.sum(hidden * hidden, axis=1, keepdims=True) / width + 1e-06)


def norm_kernel(student_any, small_ref, *refs):
    *pieces, hidden_ref, arrived = refs
    me, mine = indices()
    copies = [
        pltpu.make_async_copy(student_any.at[mine ^ (2 * i)], hidden_ref.at[i], arrived.at[i])
        for i in range(2)
    ]
    for copy in copies:
        copy.start()
    _, rows, width = hidden_ref.shape
    tiles = width // len(pieces) // LANES
    line = lax.broadcasted_iota(I32, (rows, LANES), 0)
    last = width // LANES
    owner_row, docs_row = small_ref[last : last + 1, :], small_ref[last + 1 : last + 2, :]
    extra = jnp.where(line == 0, owner_row, jnp.where(line == 1, docs_row, 0.0)).astype(BF)
    for piece in pieces:
        piece[:, tiles * LANES :] = extra
    copies[0].wait()
    inverse = inverse_rms(hidden_ref[0].astype(F32))
    for k, piece in enumerate(pieces):
        for tile in range(tiles):
            at = (me ^ k) * tiles + tile
            columns = pl.ds(pl.multiple_of(at * LANES, LANES), LANES)
            block = hidden_ref[0, :, columns].astype(F32)
            normed = block * inverse * small_ref[pl.ds(at, 1), :]
            piece[:, tile * LANES : (tile + 1) * LANES] = normed.astype(BF)
    copies[1].wait()


def norm_pieces(student, small):
    n, rows, width = student.shape
    piece = jax.ShapeDtypeStruct((rows, width // n + LANES), BF)
    return call(
        norm_kernel,
        [piece] * n + [jax.ShapeDtypeStruct((2, rows, width), BF)],
        (student, small),
        6 * rows * width,
        8 * rows * width,
        in_specs=[pl.BlockSpec(memory_space=pl.ANY), pl.BlockSpec(memory_space=pltpu.VMEM)],
        scratch_shapes=[pltpu.SemaphoreType.DMA((2,))],
        compiler_params=pltpu.CompilerParams(vmem_limit_bytes=NORM_MB * 1024 * 1024),
    )


def pick_kernel(*refs):
    *pieces, out_ref, drop_ref = refs
    pieces = pieces[::-1]
    me, mine = indices()
    tokens, depth = out_ref.shape
    slots = pieces[0].shape[0]
    spots = slots * len(pieces)
    owner_row = jnp.zeros((1, tokens), F32)
    for k, piece in enumerate(pieces):
        tile = piece[0:16, depth:].astype(F32)[0:1]
        owner_row = owner_row + jnp.where((me ^ mine) == k, tile, 0.0)
    owner = to_column(owner_row)
    earlier = lax.broadcasted_iota(I32, (tokens, tokens), 1) < lax.broadcasted_iota(
        I32, (tokens, tokens), 0
    )
    same = jnp.where(earlier & (owner == owner_row), 1.0, 0.0)
    rank = jnp.sum(same, axis=1, keepdims=True)
    peer = owner.astype(I32) ^ me
    spot = (peer * slots).astype(F32) + rank
    take = (lax.broadcasted_iota(I32, (tokens, spots), 1) == spot.astype(I32)).astype(F32)
    stacked = jnp.concatenate([piece[:, :depth] for piece in pieces], axis=0)
    out_ref[...] = dot(take.astype(BF), stacked).astype(BF)
    spot_row = to_row(spot).astype(I32)
    drop = (lax.broadcasted_iota(I32, (spots, tokens), 0) == spot_row).astype(F32)
    drop_ref[...] = drop.astype(BF)


def pick_rows(pieces, tokens):
    slots, wide = pieces[0].shape
    depth, spots = wide - LANES, slots * len(pieces)
    return call(
        pick_kernel,
        [jax.ShapeDtypeStruct((tokens, depth), BF), jax.ShapeDtypeStruct((spots, tokens), BF)],
        pieces[::-1],
        2 * tokens * spots * depth,
        4 * spots * depth,
    )


def attention_kernel(queries_ref, *refs):
    out_ref = refs[-1]
    n = (len(refs) - 1) // 2
    parcels, pieces = refs[:n], refs[n : 2 * n]
    tokens = queries_ref.shape[0]
    depth = pieces[0].shape[1] - LANES
    me, _ = indices()
    keys = jnp.concatenate([parcel[:tokens, :] for parcel in parcels], axis=0)
    values = jnp.concatenate([parcel[tokens:, :] for parcel in parcels], axis=0)
    docs = [piece[0:16, depth:].astype(F32)[1:2] for piece in pieces]
    doc_column = to_column(docs[0])
    query_pos = me * tokens + lax.broadcasted_iota(I32, (tokens, tokens), 0)
    within = lax.broadcasted_iota(I32, (tokens, tokens), 1)
    masks = []
    for k in range(n):
        near = (me ^ k) * tokens + within <= query_pos
        masks.append(jnp.where(near & (docs[k] == doc_column), 1.0, 0.0))
    allowed = jnp.concatenate(masks, axis=1) > 0.5
    scale_factor = 1.0 / math.sqrt(HD)
    for h in range(queries_ref.shape[1] // HD):
        columns = slice(h * HD, (h + 1) * HD)
        scores = dot(queries_ref[:, columns], keys, ((1,), (1,))) * scale_factor
        scores = jnp.where(allowed, scores, -1e30)
        top = jnp.max(scores, axis=1, keepdims=True)
        probs = jnp.where(allowed, jnp.exp(scores - top), 0.0)
        total = jnp.sum(probs, axis=1, keepdims=True)
        out_ref[:, columns] = (dot(probs.astype(BF), values) / total).astype(BF)


def attention_rows(queries, parcels, pieces):
    tokens, width = queries.shape
    n = len(parcels)
    return call(
        attention_kernel,
        jax.ShapeDtypeStruct((tokens, width), BF),
        (queries, *parcels, *pieces),
        0,
        4 * tokens * width,
    )


def pick_entry(refs, at):
    d, c, b, a = (ref[...] for ref in refs)
    odd = at % 2 == 1
    return jnp.where(at >= 2, jnp.where(odd, d, c), jnp.where(odd, b, a))


def away_kernel(*refs):
    *entries, proj_ref, out_ref = refs
    me, mine = indices()
    block = pick_entry(entries, me ^ mine ^ 3)
    out_ref[...] = dot(block, proj_ref[...]).astype(BF)


def kept_kernel(*refs):
    *entries, proj_ref, own_ref, over_ref, normed_ref = refs
    me, mine = indices()
    rows = entries[0].shape[0]
    for k, spot in enumerate((0, 2, 1, 3)):
        normed_ref[spot * rows : (spot + 1) * rows, :] = pick_entry(entries, me ^ mine ^ k)
    columns = 256
    for first in range(0, proj_ref.shape[1], columns):
        part = slice(first, first + columns)
        product = dot(normed_ref[: 2 * rows, :], proj_ref[:, part])
        own_ref[:, part] = product[:rows]
        over_ref[:, part] = product[rows:]


def beside_kernel(normed_ref, proj_ref, out_ref):
    rows = out_ref.shape[0]
    out_ref[...] = dot(normed_ref[2 * rows : 3 * rows, :], proj_ref[...]).astype(BF)


def away_partial(entries, proj):
    rows, depth = entries[0].shape
    out = jax.ShapeDtypeStruct((rows, proj.shape[1]), BF)
    return call(away_kernel, out, (*entries, proj), 0, 0)


def kept_partials(entries, proj):
    rows, depth = entries[0].shape
    out = jax.ShapeDtypeStruct((rows, proj.shape[1]), F32)
    shapes = [out, out, jax.ShapeDtypeStruct((4 * rows, depth), BF)]
    return call(kept_kernel, shapes, (*entries, proj), 0, 0)


def beside_partial(normed, proj):
    out = jax.ShapeDtypeStruct((normed.shape[0] // 4, proj.shape[1]), BF)
    return call(beside_kernel, out, (normed, proj), 0, 0)


def product_kernel(delta_ref, proj_ref, out_ref):
    out_ref[...] = dot(delta_ref[...], proj_ref[...], ((1,), (1,))).astype(BF)


def product(delta, proj):
    out = jax.ShapeDtypeStruct((delta.shape[0], proj.shape[0]), BF)
    return call(product_kernel, out, (delta, proj), 0, 0)


def route_kernel(first_ref, second_ref, third_ref, delta_ref, proj_ref, sent_ref, kept_ref, held):
    me, mine = indices()
    last = dot(delta_ref[...], proj_ref[...], ((1,), (1,))).astype(BF)
    for k, block in enumerate((first_ref[...], second_ref[...], third_ref[...], last)):
        held[k] = block
    off = me ^ mine
    kept_ref[0] = held[off]
    sent_ref[0] = held[off ^ 1]
    kept_ref[1] = held[off ^ 2]
    sent_ref[1] = held[off ^ 3]


def route_products(products, delta, proj):
    tokens, depth = products[0].shape
    pair = jax.ShapeDtypeStruct((2, tokens, depth), BF)
    return call(
        route_kernel,
        [pair, pair],
        (*products, delta, proj),
        0,
        0,
        scratch_shapes=[pltpu.VMEM((4, tokens, depth), BF)],
    )


def rows_kernel(hidden_ref, small_ref, *refs):
    *pieces, out_ref = refs
    me, _ = indices()
    blocks, rows, width = hidden_ref.shape
    n = len(pieces) // blocks
    tiles = width // n // LANES
    for i in range(blocks):
        inverse = inverse_rms(hidden_ref[i].astype(F32))
        spots = [
            (piece, tile, (me ^ k) * tiles + tile)
            for k, piece in enumerate(pieces[i * n : (i + 1) * n])
            for tile in range(tiles)
        ]
        total = jnp.zeros((rows, LANES), F32)
        for piece, tile, at in spots:
            columns = pl.ds(pl.multiple_of(at * LANES, LANES), LANES)
            block = hidden_ref[i, :, columns].astype(F32)
            grad = piece[:, tile * LANES : (tile + 1) * LANES].astype(F32)
            total = total + grad * small_ref[pl.ds(at, 1), :] * block
        mean = jnp.sum(total, axis=1, keepdims=True) / width
        lean = inverse * inverse * inverse * mean
        for piece, tile, at in spots:
            columns = pl.ds(pl.multiple_of(at * LANES, LANES), LANES)
            block = hidden_ref[i, :, columns].astype(F32)
            grad = piece[:, tile * LANES : (tile + 1) * LANES].astype(F32)
            grad = inverse * (grad * small_ref[pl.ds(at, 1), :]) - lean * block
            out_ref[i, :, columns] = grad.astype(BF)


def grad_rows(hidden, small, pieces):
    return call(
        rows_kernel,
        jax.ShapeDtypeStruct(hidden.shape, BF),
        (hidden, small, *pieces),
        14 * hidden.size,
        6 * hidden.size,
    )


def write_kernel(first, pair_ref, out_ref, done):
    _, mine = indices()
    copies = [
        pltpu.make_async_copy(pair_ref.at[i], out_ref.at[mine ^ first ^ (2 * i)], done.at[i])
        for i in range(2)
    ]
    for copy in copies:
        copy.start()
    for copy in copies:
        copy.wait()


def write_rows(pair, first, target=None):
    _, rows, width = pair.shape
    hbm, vmem = pl.BlockSpec(memory_space=pltpu.HBM), pl.BlockSpec(memory_space=pltpu.VMEM)
    kernel = functools.partial(write_kernel, first)
    args, specs, aliases = (pair,), [vmem], {}
    if target is not None:
        kernel = lambda t, *refs: write_kernel(first, *refs)
        args, specs, aliases = (target, pair), [hbm, vmem], {0: 0}
    return call(
        kernel,
        jax.ShapeDtypeStruct((4, rows, width), BF),
        args,
        0,
        4 * pair.size,
        in_specs=specs,
        out_specs=hbm,
        input_output_aliases=aliases,
        scratch_shapes=[pltpu.SemaphoreType.DMA((2,))],
    )


def swap(x, axis, k=1):
    return lax.ppermute(x, axis, [(i, i ^ k) for i in range(lax.axis_size(axis))])


def exchange(blocks):
    got = {k: swap(blocks[k], "seq", k) for k in reversed(range(1, len(blocks)))}
    return [got[k] for k in range(1, len(blocks))]


def after(x, *others):
    return lax.optimization_barrier((x, *others))[0]


def pairwise(
    teacher_queries, teacher_keys, teacher_values, doc_ids, owner, student_hidden, norm_gain, proj
):
    n = 4
    me, mine = indices()
    side = lax.axis_index("side")
    rows = teacher_queries.shape[0]
    heads = teacher_queries.shape[1] // HD
    kv_local = teacher_keys.shape[1] // HD
    group = heads * 2 // kv_local
    capacity, width = student_hidden.shape
    slots = capacity // n
    student = student_hidden.reshape(n, slots, width)
    tiles = width // LANES
    line = lax.broadcasted_iota(I32, (tiles + 2, LANES), 0)
    ids = jnp.where(line == tiles, owner[:, 0][None, :], doc_ids[None, :]).astype(F32)
    gain = jnp.pad(norm_gain.reshape(tiles, LANES), ((0, 2), (0, 0)))
    small = jnp.where(line < tiles, gain, ids)

    *made, hidden = norm_pieces(student, small)
    pieces = [made[0]] + exchange(made)
    normed_own, drop = pick_rows(pieces, rows)

    head = side * heads // group
    parcel = jnp.concatenate(
        [
            lax.dynamic_slice_in_dim(teacher_keys, head * HD, HD, 1),
            lax.dynamic_slice_in_dim(teacher_values, head * HD, HD, 1),
        ]
    )
    parcel = after(lax.optimization_barrier(parcel), normed_own)

    far = swap(normed_own, "mp")
    mate = swap(after(normed_own, parcel), "side")
    parcels = [parcel] + exchange([parcel] * n)
    far_mate = lax.ppermute(normed_own, ("mp", "side"), [(j, j ^ 3) for j in range(n)])
    entries = [far_mate, far, mate, normed_own]

    away = away_partial([after(e, *parcels) for e in entries], proj)
    own, over_own, normed = kept_partials([after(e, away) for e in entries], proj)
    got_over = after(swap(away, "seq", 1), over_own)
    over = lax.optimization_barrier((over_own + got_over.astype(F32)).astype(BF))
    got_far = swap(over, "seq", 2)
    got_beside = swap(beside_partial(after(normed, over), proj), "seq", 1)
    teacher_rows = attention_rows(after(teacher_queries, over), parcels, pieces)
    predicted = lax.optimization_barrier(own + got_far.astype(F32)) + got_beside.astype(F32)
    delta = (predicted - teacher_rows.astype(F32)).astype(BF)

    delta_far = swap(delta, "seq", 2)
    own_product = product(delta, proj)
    delta_beside = swap(after(delta, own_product), "seq", 1)
    delta_last = swap(delta_far, "seq", 1)
    deltas = [delta, delta_beside, delta_far, delta_last]
    products = [own_product, product(delta_beside, proj), product(delta_far, proj)]

    sent, kept = route_products(products, delta_last, proj)
    got = swap(sent, "side")
    cross = lax.optimization_barrier((kept[1].astype(F32) + got[1].astype(F32)).astype(BF))
    crossed = swap(cross, "mp")
    near = lax.optimization_barrier(kept[0].astype(F32) + after(got[0], cross).astype(F32))

    factor = 1.0 / math.sqrt(rows * n)
    deltas = after(jnp.concatenate([deltas[k] for k in (0, 2, 1, 3)]), cross)
    grad_proj = lax.optimization_barrier(dot(normed, deltas, ((0,), (0,))) * factor)
    feature_rows = (near + after(crossed, grad_proj).astype(F32)).astype(BF)

    leaving = [dot(drop[k * slots : (k + 1) * slots], feature_rows).astype(BF) for k in range(n)]
    arrived = [leaving[0]] + exchange(leaving)
    across = [swap(block, "mp") for block in arrived]
    grad_pair = grad_rows(hidden, small, arrived + across)
    grad_mates = swap(grad_pair, "side")
    grad_hidden = write_rows(grad_mates, 1, write_rows(grad_pair, 0)).reshape(capacity, width)
    return (grad_hidden, grad_proj)


def general(
    teacher_queries, teacher_keys, teacher_values, doc_ids, owner, student_hidden, norm_gain, proj
):
    n = lax.axis_size("seq")
    me = lax.axis_index("seq")
    side = lax.axis_index("side")
    plane = lax.axis_size("mp") * lax.axis_size("side")
    mine = lax.axis_index("mp") * lax.axis_size("side") + side
    rows = teacher_queries.shape[0]
    heads = teacher_queries.shape[1] // HD
    kv_local = teacher_keys.shape[1] // HD
    group = heads * lax.axis_size("side") // kv_local
    width = student_hidden.shape[1]
    depth = proj.shape[0]
    capacity = student_hidden.shape[0]
    slots = capacity // n
    shared = n // plane
    held = shared * slots

    hidden = lax.dynamic_slice_in_dim(student_hidden, mine * held, held, 0).astype(F32)
    inverse_rms = lax.rsqrt(jnp.mean(hidden * hidden, axis=1, keepdims=True) + 1e-06)
    normed = (hidden * inverse_rms * norm_gain).astype(BF)
    normed_slots = lax.all_to_all(
        normed.reshape(held, n, depth).transpose(1, 0, 2), "seq", 0, 0, tiled=True
    )

    head = side * heads // group
    key_head = lax.dynamic_slice_in_dim(teacher_keys, head * HD, HD, 1)
    value_head = lax.dynamic_slice_in_dim(teacher_values, head * HD, HD, 1)
    small = jnp.stack([doc_ids, owner[:, 0]]).astype(BF)
    parcel = jnp.concatenate([key_head, value_head, jnp.pad(small, ((0, 14), (0, 0)))])
    parcel = lax.all_gather(parcel, "seq", axis=0, tiled=False)
    keys, values = parcel[:, :rows], parcel[:, rows : 2 * rows]
    docs = parcel[:, 2 * rows].astype(I32)
    owners = parcel[:, 2 * rows + 1].astype(I32)

    query_pos = me * rows + jnp.arange(rows, dtype=I32)
    key_pos = jnp.arange(n * rows, dtype=I32)
    allowed = (docs.reshape(-1)[None, :] == doc_ids[:, None]) & (
        key_pos[None, :] <= query_pos[:, None]
    )
    stacked = teacher_queries.reshape(rows, heads, HD).transpose(1, 0, 2)
    scores = jnp.einsum("hqd,kd->hqk", stacked, keys.reshape(-1, HD), preferred_element_type=F32)
    scores = jnp.where(allowed[None], scores * (1.0 / math.sqrt(HD)), -1e30)
    top = jnp.max(scores, axis=2, keepdims=True)
    probs = jnp.where(allowed[None], jnp.exp(scores - top), 0.0)
    totals = jnp.sum(probs, axis=2, keepdims=True)
    weighted = jnp.einsum(
        "hqk,kd->hqd", probs.astype(BF), values.reshape(-1, HD), preferred_element_type=F32
    )
    teacher_rows = (weighted / totals).astype(BF).transpose(1, 0, 2).reshape(rows, heads * HD)

    own_blocks = lax.dynamic_slice_in_dim(owners, mine * shared, shared, 0)
    order = jnp.arange(rows, dtype=I32)
    same = (own_blocks[:, :, None] == own_blocks[:, None, :]) & (order[:, None] > order[None, :])
    rank = jnp.sum(same.astype(I32), axis=2)
    spot = own_blocks * held + jnp.arange(shared, dtype=I32)[:, None] * slots + rank
    pick = (spot.reshape(-1)[:, None] == jnp.arange(n * held, dtype=I32)[None, :]).astype(BF)

    normed_own = dot(pick, normed_slots.reshape(n * held, depth)).astype(BF)
    normed_rows = lax.all_gather(normed_own, ("mp", "side"), axis=0, tiled=True)
    partial = dot(normed_rows, proj).astype(BF)
    predicted = lax.psum_scatter(partial, "seq", scatter_dimension=0, tiled=True).astype(F32)
    delta = (predicted - teacher_rows.astype(F32)).astype(BF)
    deltas = lax.all_gather(delta, "seq", axis=0, tiled=True)

    products = dot(deltas, proj, ((1,), (1,))).astype(BF)
    feature_rows = lax.psum_scatter(products, ("mp", "side"), scatter_dimension=0, tiled=True)
    feature_slots = dot(pick, feature_rows, ((0,), (0,))).astype(BF).reshape(n, held, depth)
    received = lax.all_to_all(feature_slots, "seq", 0, 0, tiled=True)
    feature_grad = received.transpose(1, 0, 2).reshape(held, width)

    gain_grad = feature_grad.astype(F32) * norm_gain
    mean_term = jnp.mean(gain_grad * hidden, axis=1, keepdims=True)
    grad_own = (inverse_rms * gain_grad - inverse_rms**3 * hidden * mean_term).astype(BF)
    grad_hidden = lax.all_gather(grad_own, ("mp", "side"), axis=0, tiled=True)

    grad_proj = dot(normed_rows, deltas, ((0,), (0,))) * (1.0 / math.sqrt(rows * n))
    return (grad_hidden, grad_proj)


def solution(mesh):
    sizes = mesh.shape
    paired = PAIRWISE and (sizes["seq"], sizes["mp"], sizes["side"]) == (4, 2, 2)
    return jax.shard_map(
        pairwise if paired else general,
        mesh=mesh,
        in_specs=(
            P(("groups", "seq"), ("mp", "side")),
            P(("groups", "seq"), "mp"),
            P(("groups", "seq"), "mp"),
            P(("groups", "seq")),
            P(("groups", "seq"), None),
            P(("groups", "seq"), None),
            P(),
            P("seq", ("mp", "side")),
        ),
        out_specs=(P(("groups", "seq"), None), P(("groups", "seq"), ("mp", "side"))),
        check_vma=False,
    )
```

```python
import functools
import math

import jax
import jax.numpy as jnp
from jax import lax
from jax.experimental import pallas as pl
from jax.experimental.pallas import tpu as pltpu
from jax.sharding import PartitionSpec as P

HD = 128
LANES = 128
BF = jnp.bfloat16
F32 = jnp.float32
I32 = jnp.int32
PARAMS = pltpu.CompilerParams(vmem_limit_bytes=16 * 1024 * 1024)
NORM_MB = 52
PAIRWISE = True


def dot(a, b, dims=((1,), (0,))):
    return lax.dot_general(a, b, (dims, ((), ())), preferred_element_type=F32)


def eye(size):
    return lax.broadcasted_iota(I32, (size, size), 0) == lax.broadcasted_iota(I32, (size, size), 1)


def to_row(column):
    return jnp.sum(jnp.where(eye(column.shape[0]), column, 0.0), axis=0, keepdims=True)


def to_column(row):
    return jnp.sum(jnp.where(eye(row.shape[1]), row, 0.0), axis=1, keepdims=True)


def indices():
    return lax.axis_index("seq"), lax.axis_index("mp") * 2 + lax.axis_index("side")


def call(kernel, shapes, args, flops, moved, transcendentals=0, **more):
    vmem = pl.BlockSpec(memory_space=pltpu.VMEM)
    options = dict(
        in_specs=[vmem] * len(args),
        out_specs=jax.tree.map(lambda s: vmem, shapes),
        compiler_params=PARAMS,
    )
    options.update(more)
    return pl.pallas_call(
        kernel,
        out_shape=shapes,
        cost_estimate=pl.CostEstimate(
            flops=flops, bytes_accessed=moved, transcendentals=transcendentals
        ),
        **options,
    )(*args)


def inverse_rms(hidden):
    width = hidden.shape[1]
    return lax.rsqrt(jnp.sum(hidden * hidden, axis=1, keepdims=True) / width + 1e-06)


def norm_kernel(student_any, small_ref, *refs):
    *pieces, hidden_ref, arrived = refs
    me, mine = indices()
    copies = [
        pltpu.make_async_copy(student_any.at[mine ^ (2 * i)], hidden_ref.at[i], arrived.at[i])
        for i in range(2)
    ]
    for copy in copies:
        copy.start()
    _, rows, width = hidden_ref.shape
    tiles = width // len(pieces) // LANES
    line = lax.broadcasted_iota(I32, (rows, LANES), 0)
    last = width // LANES
    owner_row, docs_row = small_ref[last : last + 1, :], small_ref[last + 1 : last + 2, :]
    extra = jnp.where(line == 0, owner_row, jnp.where(line == 1, docs_row, 0.0)).astype(BF)
    for piece in pieces:
        piece[:, tiles * LANES :] = extra
    copies[0].wait()
    inverse = inverse_rms(hidden_ref[0].astype(F32))
    for k, piece in enumerate(pieces):
        for tile in range(tiles):
            at = (me ^ k) * tiles + tile
            columns = pl.ds(pl.multiple_of(at * LANES, LANES), LANES)
            block = hidden_ref[0, :, columns].astype(F32)
            normed = block * inverse * small_ref[pl.ds(at, 1), :]
            piece[:, tile * LANES : (tile + 1) * LANES] = normed.astype(BF)
    copies[1].wait()


def norm_pieces(student, small):
    n, rows, width = student.shape
    piece = jax.ShapeDtypeStruct((rows, width // n + LANES), BF)
    return call(
        norm_kernel,
        [piece] * n + [jax.ShapeDtypeStruct((2, rows, width), BF)],
        (student, small),
        6 * rows * width,
        8 * rows * width,
        in_specs=[pl.BlockSpec(memory_space=pl.ANY), pl.BlockSpec(memory_space=pltpu.VMEM)],
        scratch_shapes=[pltpu.SemaphoreType.DMA((2,))],
        compiler_params=pltpu.CompilerParams(vmem_limit_bytes=NORM_MB * 1024 * 1024),
    )


def pick_kernel(*refs):
    *pieces, out_ref, drop_ref = refs
    pieces = pieces[::-1]
    me, mine = indices()
    tokens, depth = out_ref.shape
    slots = pieces[0].shape[0]
    spots = slots * len(pieces)
    owner_row = jnp.zeros((1, tokens), F32)
    for k, piece in enumerate(pieces):
        tile = piece[0:16, depth:].astype(F32)[0:1]
        owner_row = owner_row + jnp.where((me ^ mine) == k, tile, 0.0)
    owner = to_column(owner_row)
    earlier = lax.broadcasted_iota(I32, (tokens, tokens), 1) < lax.broadcasted_iota(
        I32, (tokens, tokens), 0
    )
    same = jnp.where(earlier & (owner == owner_row), 1.0, 0.0)
    rank = jnp.sum(same, axis=1, keepdims=True)
    peer = owner.astype(I32) ^ me
    spot = (peer * slots).astype(F32) + rank
    take = (lax.broadcasted_iota(I32, (tokens, spots), 1) == spot.astype(I32)).astype(F32)
    stacked = jnp.concatenate([piece[:, :depth] for piece in pieces], axis=0)
    out_ref[...] = dot(take.astype(BF), stacked).astype(BF)
    spot_row = to_row(spot).astype(I32)
    drop = (lax.broadcasted_iota(I32, (spots, tokens), 0) == spot_row).astype(F32)
    drop_ref[...] = drop.astype(BF)


def pick_rows(pieces, tokens):
    slots, wide = pieces[0].shape
    depth, spots = wide - LANES, slots * len(pieces)
    return call(
        pick_kernel,
        [jax.ShapeDtypeStruct((tokens, depth), BF), jax.ShapeDtypeStruct((spots, tokens), BF)],
        pieces[::-1],
        2 * tokens * spots * depth,
        4 * spots * depth,
    )


def attention_kernel(queries_ref, *refs):
    out_ref = refs[-1]
    n = (len(refs) - 1) // 2
    parcels, pieces = refs[:n], refs[n : 2 * n]
    tokens = queries_ref.shape[0]
    depth = pieces[0].shape[1] - LANES
    me, _ = indices()
    keys = jnp.concatenate([parcel[:tokens, :] for parcel in parcels], axis=0)
    values = jnp.concatenate([parcel[tokens:, :] for parcel in parcels], axis=0)
    docs = [piece[0:16, depth:].astype(F32)[1:2] for piece in pieces]
    doc_column = to_column(docs[0])
    query_pos = me * tokens + lax.broadcasted_iota(I32, (tokens, tokens), 0)
    within = lax.broadcasted_iota(I32, (tokens, tokens), 1)
    masks = []
    for k in range(n):
        block = (me - k + n) % n
        doc_row = sum(jnp.where((me ^ block) == i, docs[i], 0.0) for i in range(n))
        near = block * tokens + within <= query_pos
        masks.append(jnp.where(near & (doc_row == doc_column), 1.0, 0.0))
    allowed = jnp.concatenate(masks, axis=1) > 0.5
    scale_factor = 1.0 / math.sqrt(HD)
    for h in range(queries_ref.shape[1] // HD):
        columns = slice(h * HD, (h + 1) * HD)
        scores = dot(queries_ref[:, columns], keys, ((1,), (1,))) * scale_factor
        scores = jnp.where(allowed, scores, -1e30)
        top = jnp.max(scores, axis=1, keepdims=True)
        probs = jnp.where(allowed, jnp.exp(scores - top), 0.0)
        total = jnp.sum(probs, axis=1, keepdims=True)
        out_ref[:, columns] = (dot(probs.astype(BF), values) / total).astype(BF)


def attention_rows(queries, parcels, pieces):
    tokens, width = queries.shape
    n = len(parcels)
    return call(
        attention_kernel,
        jax.ShapeDtypeStruct((tokens, width), BF),
        (queries, *parcels, *pieces),
        0,
        4 * tokens * width,
    )


def pick_entry(refs, at):
    d, c, b, a = (ref[...] for ref in refs)
    odd = at % 2 == 1
    return jnp.where(at >= 2, jnp.where(odd, d, c), jnp.where(odd, b, a))


def away_kernel(*refs):
    *entries, proj_ref, out_ref = refs
    me, mine = indices()
    block = pick_entry(entries, me ^ mine ^ 3)
    out_ref[...] = dot(block, proj_ref[...]).astype(BF)


def kept_kernel(*refs):
    *entries, proj_ref, own_ref, over_ref, normed_ref = refs
    me, mine = indices()
    rows = entries[0].shape[0]
    for k, spot in enumerate((0, 2, 1, 3)):
        normed_ref[spot * rows : (spot + 1) * rows, :] = pick_entry(entries, me ^ mine ^ k)
    columns = 256
    for first in range(0, proj_ref.shape[1], columns):
        part = slice(first, first + columns)
        product = dot(normed_ref[: 2 * rows, :], proj_ref[:, part])
        own_ref[:, part] = product[:rows]
        over_ref[:, part] = product[rows:]


def beside_kernel(normed_ref, proj_ref, out_ref):
    rows = out_ref.shape[0]
    out_ref[...] = dot(normed_ref[2 * rows : 3 * rows, :], proj_ref[...]).astype(BF)


def away_partial(entries, proj):
    rows, depth = entries[0].shape
    out = jax.ShapeDtypeStruct((rows, proj.shape[1]), BF)
    return call(away_kernel, out, (*entries, proj), 0, 0)


def kept_partials(entries, proj):
    rows, depth = entries[0].shape
    out = jax.ShapeDtypeStruct((rows, proj.shape[1]), F32)
    shapes = [out, out, jax.ShapeDtypeStruct((4 * rows, depth), BF)]
    return call(kept_kernel, shapes, (*entries, proj), 0, 0)


def beside_partial(normed, proj):
    out = jax.ShapeDtypeStruct((normed.shape[0] // 4, proj.shape[1]), BF)
    return call(beside_kernel, out, (normed, proj), 0, 0)


def product_kernel(delta_ref, proj_ref, out_ref):
    out_ref[...] = dot(delta_ref[...], proj_ref[...], ((1,), (1,))).astype(BF)


def product(delta, proj):
    out = jax.ShapeDtypeStruct((delta.shape[0], proj.shape[0]), BF)
    return call(product_kernel, out, (delta, proj), 0, 0)


def route_kernel(first_ref, second_ref, third_ref, delta_ref, proj_ref, sent_ref, kept_ref, held):
    me, mine = indices()
    last = dot(delta_ref[...], proj_ref[...], ((1,), (1,))).astype(BF)
    for k, block in enumerate((first_ref[...], second_ref[...], third_ref[...], last)):
        held[k] = block
    off = me ^ mine
    kept_ref[0] = held[off]
    sent_ref[0] = held[off ^ 1]
    kept_ref[1] = held[off ^ 2]
    sent_ref[1] = held[off ^ 3]


def route_products(products, delta, proj):
    tokens, depth = products[0].shape
    pair = jax.ShapeDtypeStruct((2, tokens, depth), BF)
    return call(
        route_kernel,
        [pair, pair],
        (*products, delta, proj),
        0,
        0,
        scratch_shapes=[pltpu.VMEM((4, tokens, depth), BF)],
    )


def rows_kernel(hidden_ref, small_ref, *refs):
    *pieces, out_ref = refs
    me, _ = indices()
    blocks, rows, width = hidden_ref.shape
    n = len(pieces) // blocks
    tiles = width // n // LANES
    for i in range(blocks):
        inverse = inverse_rms(hidden_ref[i].astype(F32))
        spots = [
            (piece, tile, (me ^ k) * tiles + tile)
            for k, piece in enumerate(pieces[i * n : (i + 1) * n])
            for tile in range(tiles)
        ]
        total = jnp.zeros((rows, LANES), F32)
        for piece, tile, at in spots:
            columns = pl.ds(pl.multiple_of(at * LANES, LANES), LANES)
            block = hidden_ref[i, :, columns].astype(F32)
            grad = piece[:, tile * LANES : (tile + 1) * LANES].astype(F32)
            total = total + grad * small_ref[pl.ds(at, 1), :] * block
        mean = jnp.sum(total, axis=1, keepdims=True) / width
        lean = inverse * inverse * inverse * mean
        for piece, tile, at in spots:
            columns = pl.ds(pl.multiple_of(at * LANES, LANES), LANES)
            block = hidden_ref[i, :, columns].astype(F32)
            grad = piece[:, tile * LANES : (tile + 1) * LANES].astype(F32)
            grad = inverse * (grad * small_ref[pl.ds(at, 1), :]) - lean * block
            out_ref[i, :, columns] = grad.astype(BF)


def grad_rows(hidden, small, pieces):
    return call(
        rows_kernel,
        jax.ShapeDtypeStruct(hidden.shape, BF),
        (hidden, small, *pieces),
        14 * hidden.size,
        6 * hidden.size,
    )


def write_kernel(first, pair_ref, out_ref, done):
    _, mine = indices()
    copies = [
        pltpu.make_async_copy(pair_ref.at[i], out_ref.at[mine ^ first ^ (2 * i)], done.at[i])
        for i in range(2)
    ]
    for copy in copies:
        copy.start()
    for copy in copies:
        copy.wait()


def write_rows(pair, first, target=None):
    _, rows, width = pair.shape
    hbm, vmem = pl.BlockSpec(memory_space=pltpu.HBM), pl.BlockSpec(memory_space=pltpu.VMEM)
    kernel = functools.partial(write_kernel, first)
    args, specs, aliases = (pair,), [vmem], {}
    if target is not None:
        kernel = lambda t, *refs: write_kernel(first, *refs)
        args, specs, aliases = (target, pair), [hbm, vmem], {0: 0}
    return call(
        kernel,
        jax.ShapeDtypeStruct((4, rows, width), BF),
        args,
        0,
        4 * pair.size,
        in_specs=specs,
        out_specs=hbm,
        input_output_aliases=aliases,
        scratch_shapes=[pltpu.SemaphoreType.DMA((2,))],
    )


def swap(x, axis, k=1):
    return lax.ppermute(x, axis, [(i, i ^ k) for i in range(lax.axis_size(axis))])


def onward(x):
    return lax.ppermute(x, "seq", [(i, i + 1) for i in range(lax.axis_size("seq") - 1)])


def exchange(blocks):
    got = {k: swap(blocks[k], "seq", k) for k in reversed(range(1, len(blocks)))}
    return [got[k] for k in range(1, len(blocks))]


def after(x, *others):
    return lax.optimization_barrier((x, *others))[0]


def pairwise(
    teacher_queries, teacher_keys, teacher_values, doc_ids, owner, student_hidden, norm_gain, proj
):
    n = 4
    me, mine = indices()
    side = lax.axis_index("side")
    rows = teacher_queries.shape[0]
    heads = teacher_queries.shape[1] // HD
    kv_local = teacher_keys.shape[1] // HD
    group = heads * 2 // kv_local
    capacity, width = student_hidden.shape
    slots = capacity // n
    student = student_hidden.reshape(n, slots, width)
    tiles = width // LANES
    line = lax.broadcasted_iota(I32, (tiles + 2, LANES), 0)
    ids = jnp.where(line == tiles, owner[:, 0][None, :], doc_ids[None, :]).astype(F32)
    gain = jnp.pad(norm_gain.reshape(tiles, LANES), ((0, 2), (0, 0)))
    small = jnp.where(line < tiles, gain, ids)

    *made, hidden = norm_pieces(student, small)
    pieces = [made[0]] + exchange(made)
    normed_own, drop = pick_rows(pieces, rows)

    head = side * heads // group
    parcel = jnp.concatenate(
        [
            lax.dynamic_slice_in_dim(teacher_keys, head * HD, HD, 1),
            lax.dynamic_slice_in_dim(teacher_values, head * HD, HD, 1),
        ]
    )
    parcel = after(lax.optimization_barrier(parcel), normed_own)

    far = swap(normed_own, "mp")
    mate = swap(after(normed_own, parcel), "side")
    parcels = [parcel, onward(parcel)]
    far_mate = swap(after(far, mate, parcels[1]), "side")
    entries = [far_mate, far, mate, normed_own]

    away = away_partial(entries, proj)
    own, over_own, normed = kept_partials([after(e, away) for e in entries], proj)
    parcels.append(onward(after(parcels[1], away)))
    got_over = after(swap(away, "seq", 1), over_own, parcels[2])
    over = lax.optimization_barrier((over_own + got_over.astype(F32)).astype(BF))
    got_far = swap(over, "seq", 2)
    got_beside = swap(beside_partial(after(normed, over), proj), "seq", 1)
    parcels.append(onward(after(parcels[2], over)))
    teacher_rows = attention_rows(after(teacher_queries, over), parcels, pieces)
    predicted = lax.optimization_barrier(own + got_far.astype(F32)) + got_beside.astype(F32)
    delta = (predicted - teacher_rows.astype(F32)).astype(BF)

    delta_far = swap(delta, "seq", 2)
    own_product = product(delta, proj)
    delta_beside = swap(after(delta, own_product), "seq", 1)
    delta_last = swap(delta_far, "seq", 1)
    deltas = [delta, delta_beside, delta_far, delta_last]
    products = [own_product, product(delta_beside, proj), product(delta_far, proj)]

    sent, kept = route_products(products, delta_last, proj)
    got = swap(sent, "side")
    cross = lax.optimization_barrier((kept[1].astype(F32) + got[1].astype(F32)).astype(BF))
    crossed = swap(cross, "mp")
    near = lax.optimization_barrier(kept[0].astype(F32) + after(got[0], cross).astype(F32))

    factor = 1.0 / math.sqrt(rows * n)
    deltas = after(jnp.concatenate([deltas[k] for k in (0, 2, 1, 3)]), cross)
    grad_proj = lax.optimization_barrier(dot(normed, deltas, ((0,), (0,))) * factor)
    feature_rows = (near + after(crossed, grad_proj).astype(F32)).astype(BF)

    leaving = [dot(drop[k * slots : (k + 1) * slots], feature_rows).astype(BF) for k in range(n)]
    arrived = [leaving[0]] + exchange(leaving)
    across = [swap(block, "mp") for block in arrived]
    grad_pair = grad_rows(hidden, small, arrived + across)
    grad_mates = swap(grad_pair, "side")
    grad_hidden = write_rows(grad_mates, 1, write_rows(grad_pair, 0)).reshape(capacity, width)
    return (grad_hidden, grad_proj)


def general(
    teacher_queries, teacher_keys, teacher_values, doc_ids, owner, student_hidden, norm_gain, proj
):
    n = lax.axis_size("seq")
    me = lax.axis_index("seq")
    side = lax.axis_index("side")
    plane = lax.axis_size("mp") * lax.axis_size("side")
    mine = lax.axis_index("mp") * lax.axis_size("side") + side
    rows = teacher_queries.shape[0]
    heads = teacher_queries.shape[1] // HD
    kv_local = teacher_keys.shape[1] // HD
    group = heads * lax.axis_size("side") // kv_local
    width = student_hidden.shape[1]
    depth = proj.shape[0]
    capacity = student_hidden.shape[0]
    slots = capacity // n
    shared = n // plane
    held = shared * slots

    hidden = lax.dynamic_slice_in_dim(student_hidden, mine * held, held, 0).astype(F32)
    inverse_rms = lax.rsqrt(jnp.mean(hidden * hidden, axis=1, keepdims=True) + 1e-06)
    normed = (hidden * inverse_rms * norm_gain).astype(BF)
    normed_slots = lax.all_to_all(
        normed.reshape(held, n, depth).transpose(1, 0, 2), "seq", 0, 0, tiled=True
    )

    head = side * heads // group
    key_head = lax.dynamic_slice_in_dim(teacher_keys, head * HD, HD, 1)
    value_head = lax.dynamic_slice_in_dim(teacher_values, head * HD, HD, 1)
    small = jnp.stack([doc_ids, owner[:, 0]]).astype(BF)
    parcel = jnp.concatenate([key_head, value_head, jnp.pad(small, ((0, 14), (0, 0)))])
    parcel = lax.all_gather(parcel, "seq", axis=0, tiled=False)
    keys, values = parcel[:, :rows], parcel[:, rows : 2 * rows]
    docs = parcel[:, 2 * rows].astype(I32)
    owners = parcel[:, 2 * rows + 1].astype(I32)

    query_pos = me * rows + jnp.arange(rows, dtype=I32)
    key_pos = jnp.arange(n * rows, dtype=I32)
    allowed = (docs.reshape(-1)[None, :] == doc_ids[:, None]) & (
        key_pos[None, :] <= query_pos[:, None]
    )
    stacked = teacher_queries.reshape(rows, heads, HD).transpose(1, 0, 2)
    scores = jnp.einsum("hqd,kd->hqk", stacked, keys.reshape(-1, HD), preferred_element_type=F32)
    scores = jnp.where(allowed[None], scores * (1.0 / math.sqrt(HD)), -1e30)
    top = jnp.max(scores, axis=2, keepdims=True)
    probs = jnp.where(allowed[None], jnp.exp(scores - top), 0.0)
    totals = jnp.sum(probs, axis=2, keepdims=True)
    weighted = jnp.einsum(
        "hqk,kd->hqd", probs.astype(BF), values.reshape(-1, HD), preferred_element_type=F32
    )
    teacher_rows = (weighted / totals).astype(BF).transpose(1, 0, 2).reshape(rows, heads * HD)

    own_blocks = lax.dynamic_slice_in_dim(owners, mine * shared, shared, 0)
    order = jnp.arange(rows, dtype=I32)
    same = (own_blocks[:, :, None] == own_blocks[:, None, :]) & (order[:, None] > order[None, :])
    rank = jnp.sum(same.astype(I32), axis=2)
    spot = own_blocks * held + jnp.arange(shared, dtype=I32)[:, None] * slots + rank
    pick = (spot.reshape(-1)[:, None] == jnp.arange(n * held, dtype=I32)[None, :]).astype(BF)

    normed_own = dot(pick, normed_slots.reshape(n * held, depth)).astype(BF)
    normed_rows = lax.all_gather(normed_own, ("mp", "side"), axis=0, tiled=True)
    partial = dot(normed_rows, proj).astype(BF)
    predicted = lax.psum_scatter(partial, "seq", scatter_dimension=0, tiled=True).astype(F32)
    delta = (predicted - teacher_rows.astype(F32)).astype(BF)
    deltas = lax.all_gather(delta, "seq", axis=0, tiled=True)

    products = dot(deltas, proj, ((1,), (1,))).astype(BF)
    feature_rows = lax.psum_scatter(products, ("mp", "side"), scatter_dimension=0, tiled=True)
    feature_slots = dot(pick, feature_rows, ((0,), (0,))).astype(BF).reshape(n, held, depth)
    received = lax.all_to_all(feature_slots, "seq", 0, 0, tiled=True)
    feature_grad = received.transpose(1, 0, 2).reshape(held, width)

    gain_grad = feature_grad.astype(F32) * norm_gain
    mean_term = jnp.mean(gain_grad * hidden, axis=1, keepdims=True)
    grad_own = (inverse_rms * gain_grad - inverse_rms**3 * hidden * mean_term).astype(BF)
    grad_hidden = lax.all_gather(grad_own, ("mp", "side"), axis=0, tiled=True)

    grad_proj = dot(normed_rows, deltas, ((0,), (0,))) * (1.0 / math.sqrt(rows * n))
    return (grad_hidden, grad_proj)


def solution(mesh):
    sizes = mesh.shape
    paired = PAIRWISE and (sizes["seq"], sizes["mp"], sizes["side"]) == (4, 2, 2)
    return jax.shard_map(
        pairwise if paired else general,
        mesh=mesh,
        in_specs=(
            P(("groups", "seq"), ("mp", "side")),
            P(("groups", "seq"), "mp"),
            P(("groups", "seq"), "mp"),
            P(("groups", "seq")),
            P(("groups", "seq"), None),
            P(("groups", "seq"), None),
            P(),
            P("seq", ("mp", "side")),
        ),
        out_specs=(P(("groups", "seq"), None), P(("groups", "seq"), ("mp", "side"))),
        check_vma=False,
    )
```

```python
import functools
import math

import jax
import jax.numpy as jnp
from jax import lax
from jax.experimental import pallas as pl
from jax.experimental.pallas import tpu as pltpu
from jax.sharding import PartitionSpec as P

HD = 128
LANES = 128
BF = jnp.bfloat16
F32 = jnp.float32
I32 = jnp.int32
PARAMS = pltpu.CompilerParams(vmem_limit_bytes=16 * 1024 * 1024)
NORM_MB = 52
PAIRWISE = True


def dot(a, b, dims=((1,), (0,))):
    return lax.dot_general(a, b, (dims, ((), ())), preferred_element_type=F32)


def eye(size):
    return lax.broadcasted_iota(I32, (size, size), 0) == lax.broadcasted_iota(I32, (size, size), 1)


def to_row(column):
    return jnp.sum(jnp.where(eye(column.shape[0]), column, 0.0), axis=0, keepdims=True)


def to_column(row):
    return jnp.sum(jnp.where(eye(row.shape[1]), row, 0.0), axis=1, keepdims=True)


def indices():
    return lax.axis_index("seq"), lax.axis_index("mp") * 2 + lax.axis_index("side")


def call(kernel, shapes, args, flops, moved, transcendentals=0, **more):
    vmem = pl.BlockSpec(memory_space=pltpu.VMEM)
    options = dict(
        in_specs=[vmem] * len(args),
        out_specs=jax.tree.map(lambda s: vmem, shapes),
        compiler_params=PARAMS,
    )
    options.update(more)
    return pl.pallas_call(
        kernel,
        out_shape=shapes,
        cost_estimate=pl.CostEstimate(
            flops=flops, bytes_accessed=moved, transcendentals=transcendentals
        ),
        **options,
    )(*args)


def inverse_rms(hidden):
    width = hidden.shape[1]
    return lax.rsqrt(jnp.sum(hidden * hidden, axis=1, keepdims=True) / width + 1e-06)


def norm_kernel(student_any, small_ref, *refs):
    *pieces, hidden_ref, arrived = refs
    me, mine = indices()
    copies = [
        pltpu.make_async_copy(student_any.at[mine ^ (2 * i)], hidden_ref.at[i], arrived.at[i])
        for i in range(2)
    ]
    for copy in copies:
        copy.start()
    _, rows, width = hidden_ref.shape
    tiles = width // len(pieces) // LANES
    line = lax.broadcasted_iota(I32, (rows, LANES), 0)
    last = width // LANES
    owner_row, docs_row = small_ref[last : last + 1, :], small_ref[last + 1 : last + 2, :]
    extra = jnp.where(line == 0, owner_row, jnp.where(line == 1, docs_row, 0.0)).astype(BF)
    for piece in pieces:
        piece[:, tiles * LANES :] = extra
    copies[0].wait()
    inverse = inverse_rms(hidden_ref[0].astype(F32))
    for k, piece in enumerate(pieces):
        for tile in range(tiles):
            at = (me ^ k) * tiles + tile
            columns = pl.ds(pl.multiple_of(at * LANES, LANES), LANES)
            block = hidden_ref[0, :, columns].astype(F32)
            normed = block * inverse * small_ref[pl.ds(at, 1), :]
            piece[:, tile * LANES : (tile + 1) * LANES] = normed.astype(BF)
    copies[1].wait()


def norm_pieces(student, small):
    n, rows, width = student.shape
    piece = jax.ShapeDtypeStruct((rows, width // n + LANES), BF)
    return call(
        norm_kernel,
        [piece] * n + [jax.ShapeDtypeStruct((2, rows, width), BF)],
        (student, small),
        6 * rows * width,
        8 * rows * width,
        in_specs=[pl.BlockSpec(memory_space=pl.ANY), pl.BlockSpec(memory_space=pltpu.VMEM)],
        scratch_shapes=[pltpu.SemaphoreType.DMA((2,))],
        compiler_params=pltpu.CompilerParams(vmem_limit_bytes=NORM_MB * 1024 * 1024),
    )


def pick_kernel(*refs):
    *pieces, out_ref, drop_ref = refs
    pieces = pieces[::-1]
    me, mine = indices()
    tokens, depth = out_ref.shape
    slots = pieces[0].shape[0]
    spots = slots * len(pieces)
    owner_row = jnp.zeros((1, tokens), F32)
    for k, piece in enumerate(pieces):
        tile = piece[0:16, depth:].astype(F32)[0:1]
        owner_row = owner_row + jnp.where((me ^ mine) == k, tile, 0.0)
    owner = to_column(owner_row)
    earlier = lax.broadcasted_iota(I32, (tokens, tokens), 1) < lax.broadcasted_iota(
        I32, (tokens, tokens), 0
    )
    same = jnp.where(earlier & (owner == owner_row), 1.0, 0.0)
    rank = jnp.sum(same, axis=1, keepdims=True)
    peer = owner.astype(I32) ^ me
    spot = (peer * slots).astype(F32) + rank
    take = (lax.broadcasted_iota(I32, (tokens, spots), 1) == spot.astype(I32)).astype(F32)
    stacked = jnp.concatenate([piece[:, :depth] for piece in pieces], axis=0)
    out_ref[...] = dot(take.astype(BF), stacked).astype(BF)
    spot_row = to_row(spot).astype(I32)
    drop = (lax.broadcasted_iota(I32, (spots, tokens), 0) == spot_row).astype(F32)
    drop_ref[...] = drop.astype(BF)


def pick_rows(pieces, tokens):
    slots, wide = pieces[0].shape
    depth, spots = wide - LANES, slots * len(pieces)
    return call(
        pick_kernel,
        [jax.ShapeDtypeStruct((tokens, depth), BF), jax.ShapeDtypeStruct((spots, tokens), BF)],
        pieces[::-1],
        2 * tokens * spots * depth,
        4 * spots * depth,
    )


def attention_kernel(queries_ref, near_ref, far_ref, *refs):
    *pieces, out_ref = refs
    n = len(pieces)
    tokens = queries_ref.shape[0]
    depth = pieces[0].shape[1] - LANES
    me, _ = indices()
    parcels = [(pair, 2 * tokens * i) for pair in (near_ref, far_ref) for i in range(2)]
    keys = jnp.concatenate([pair[at : at + tokens, :] for pair, at in parcels], axis=0)
    values = jnp.concatenate(
        [pair[at + tokens : at + 2 * tokens, :] for pair, at in parcels], axis=0
    )
    docs = [piece[0:16, depth:].astype(F32)[1:2] for piece in pieces]
    doc_column = to_column(docs[0])
    query_pos = me * tokens + lax.broadcasted_iota(I32, (tokens, tokens), 0)
    within = lax.broadcasted_iota(I32, (tokens, tokens), 1)
    masks = []
    for k in range(n):
        block = (me - k + n) % n
        doc_row = sum(jnp.where((me ^ block) == i, docs[i], 0.0) for i in range(n))
        near = block * tokens + within <= query_pos
        masks.append(jnp.where(near & (doc_row == doc_column), 1.0, 0.0))
    allowed = jnp.concatenate(masks, axis=1) > 0.5
    scale_factor = 1.0 / math.sqrt(HD)
    for h in range(queries_ref.shape[1] // HD):
        columns = slice(h * HD, (h + 1) * HD)
        scores = dot(queries_ref[:, columns], keys, ((1,), (1,))) * scale_factor
        scores = jnp.where(allowed, scores, -1e30)
        top = jnp.max(scores, axis=1, keepdims=True)
        probs = jnp.where(allowed, jnp.exp(scores - top), 0.0)
        total = jnp.sum(probs, axis=1, keepdims=True)
        out_ref[:, columns] = (dot(probs.astype(BF), values) / total).astype(BF)


def attention_rows(queries, pairs, pieces):
    tokens, width = queries.shape
    return call(
        attention_kernel,
        jax.ShapeDtypeStruct((tokens, width), BF),
        (queries, *pairs, *pieces),
        0,
        4 * tokens * width,
    )


def pick_entry(refs, at):
    d, c, b, a = (ref[...] for ref in refs)
    odd = at % 2 == 1
    return jnp.where(at >= 2, jnp.where(odd, d, c), jnp.where(odd, b, a))


def away_kernel(*refs):
    *entries, proj_ref, out_ref = refs
    me, mine = indices()
    block = pick_entry(entries, me ^ mine ^ 3)
    out_ref[...] = dot(block, proj_ref[...]).astype(BF)


def kept_kernel(*refs):
    *entries, proj_ref, own_ref, over_ref, normed_ref = refs
    me, mine = indices()
    rows = entries[0].shape[0]
    for k, spot in enumerate((0, 2, 1, 3)):
        normed_ref[spot * rows : (spot + 1) * rows, :] = pick_entry(entries, me ^ mine ^ k)
    columns = 256
    for first in range(0, proj_ref.shape[1], columns):
        part = slice(first, first + columns)
        product = dot(normed_ref[: 2 * rows, :], proj_ref[:, part])
        own_ref[:, part] = product[:rows]
        over_ref[:, part] = product[rows:]


def beside_kernel(normed_ref, proj_ref, out_ref):
    rows = out_ref.shape[0]
    out_ref[...] = dot(normed_ref[2 * rows : 3 * rows, :], proj_ref[...]).astype(BF)


def away_partial(entries, proj):
    rows, depth = entries[0].shape
    out = jax.ShapeDtypeStruct((rows, proj.shape[1]), BF)
    return call(away_kernel, out, (*entries, proj), 0, 0)


def kept_partials(entries, proj):
    rows, depth = entries[0].shape
    out = jax.ShapeDtypeStruct((rows, proj.shape[1]), F32)
    shapes = [out, out, jax.ShapeDtypeStruct((4 * rows, depth), BF)]
    return call(kept_kernel, shapes, (*entries, proj), 0, 0)


def beside_partial(normed, proj):
    out = jax.ShapeDtypeStruct((normed.shape[0] // 4, proj.shape[1]), BF)
    return call(beside_kernel, out, (normed, proj), 0, 0)


def product_kernel(delta_ref, proj_ref, out_ref):
    out_ref[...] = dot(delta_ref[...], proj_ref[...], ((1,), (1,))).astype(BF)


def product(delta, proj):
    out = jax.ShapeDtypeStruct((delta.shape[0], proj.shape[0]), BF)
    return call(product_kernel, out, (delta, proj), 0, 0)


def route_kernel(first_ref, second_ref, third_ref, delta_ref, proj_ref, sent_ref, kept_ref, held):
    me, mine = indices()
    last = dot(delta_ref[...], proj_ref[...], ((1,), (1,))).astype(BF)
    for k, block in enumerate((first_ref[...], second_ref[...], third_ref[...], last)):
        held[k] = block
    off = me ^ mine
    kept_ref[0] = held[off]
    sent_ref[0] = held[off ^ 1]
    kept_ref[1] = held[off ^ 2]
    sent_ref[1] = held[off ^ 3]


def route_products(products, delta, proj):
    tokens, depth = products[0].shape
    pair = jax.ShapeDtypeStruct((2, tokens, depth), BF)
    return call(
        route_kernel,
        [pair, pair],
        (*products, delta, proj),
        0,
        0,
        scratch_shapes=[pltpu.VMEM((4, tokens, depth), BF)],
    )


def rows_kernel(hidden_ref, small_ref, *refs):
    *pieces, out_ref = refs
    me, _ = indices()
    blocks, rows, width = hidden_ref.shape
    n = len(pieces) // blocks
    tiles = width // n // LANES
    for i in range(blocks):
        inverse = inverse_rms(hidden_ref[i].astype(F32))
        spots = [
            (piece, tile, (me ^ k) * tiles + tile)
            for k, piece in enumerate(pieces[i * n : (i + 1) * n])
            for tile in range(tiles)
        ]
        total = jnp.zeros((rows, LANES), F32)
        for piece, tile, at in spots:
            columns = pl.ds(pl.multiple_of(at * LANES, LANES), LANES)
            block = hidden_ref[i, :, columns].astype(F32)
            grad = piece[:, tile * LANES : (tile + 1) * LANES].astype(F32)
            total = total + grad * small_ref[pl.ds(at, 1), :] * block
        mean = jnp.sum(total, axis=1, keepdims=True) / width
        lean = inverse * inverse * inverse * mean
        for piece, tile, at in spots:
            columns = pl.ds(pl.multiple_of(at * LANES, LANES), LANES)
            block = hidden_ref[i, :, columns].astype(F32)
            grad = piece[:, tile * LANES : (tile + 1) * LANES].astype(F32)
            grad = inverse * (grad * small_ref[pl.ds(at, 1), :]) - lean * block
            out_ref[i, :, columns] = grad.astype(BF)


def grad_rows(hidden, small, pieces):
    return call(
        rows_kernel,
        jax.ShapeDtypeStruct(hidden.shape, BF),
        (hidden, small, *pieces),
        14 * hidden.size,
        6 * hidden.size,
    )


def write_kernel(first, pair_ref, out_ref, done):
    _, mine = indices()
    copies = [
        pltpu.make_async_copy(pair_ref.at[i], out_ref.at[mine ^ first ^ (2 * i)], done.at[i])
        for i in range(2)
    ]
    for copy in copies:
        copy.start()
    for copy in copies:
        copy.wait()


def write_rows(pair, first, target=None):
    _, rows, width = pair.shape
    hbm, vmem = pl.BlockSpec(memory_space=pltpu.HBM), pl.BlockSpec(memory_space=pltpu.VMEM)
    kernel = functools.partial(write_kernel, first)
    args, specs, aliases = (pair,), [vmem], {}
    if target is not None:
        kernel = lambda t, *refs: write_kernel(first, *refs)
        args, specs, aliases = (target, pair), [hbm, vmem], {0: 0}
    return call(
        kernel,
        jax.ShapeDtypeStruct((4, rows, width), BF),
        args,
        0,
        4 * pair.size,
        in_specs=specs,
        out_specs=hbm,
        input_output_aliases=aliases,
        scratch_shapes=[pltpu.SemaphoreType.DMA((2,))],
    )


def swap(x, axis, k=1):
    return lax.ppermute(x, axis, [(i, i ^ k) for i in range(lax.axis_size(axis))])


def onward(x, step):
    n = lax.axis_size("seq")
    return lax.ppermute(x, "seq", [(i, i + step) for i in range(n - step)])


def exchange(blocks):
    got = {k: swap(blocks[k], "seq", k) for k in reversed(range(1, len(blocks)))}
    return [got[k] for k in range(1, len(blocks))]


def after(x, *others):
    return lax.optimization_barrier((x, *others))[0]


def pairwise(
    teacher_queries, teacher_keys, teacher_values, doc_ids, owner, student_hidden, norm_gain, proj
):
    n = 4
    me, mine = indices()
    side = lax.axis_index("side")
    rows = teacher_queries.shape[0]
    heads = teacher_queries.shape[1] // HD
    kv_local = teacher_keys.shape[1] // HD
    group = heads * 2 // kv_local
    capacity, width = student_hidden.shape
    slots = capacity // n
    student = student_hidden.reshape(n, slots, width)
    tiles = width // LANES
    line = lax.broadcasted_iota(I32, (tiles + 2, LANES), 0)
    ids = jnp.where(line == tiles, owner[:, 0][None, :], doc_ids[None, :]).astype(F32)
    gain = jnp.pad(norm_gain.reshape(tiles, LANES), ((0, 2), (0, 0)))
    small = jnp.where(line < tiles, gain, ids)

    *made, hidden = norm_pieces(student, small)
    pieces = [made[0]] + exchange(made)
    normed_own, drop = pick_rows(pieces, rows)

    head = side * heads // group
    parcel = jnp.concatenate(
        [
            lax.dynamic_slice_in_dim(teacher_keys, head * HD, HD, 1),
            lax.dynamic_slice_in_dim(teacher_values, head * HD, HD, 1),
        ]
    )
    parcel = after(lax.optimization_barrier(parcel), normed_own)

    far = swap(normed_own, "mp")
    mate = swap(after(normed_own, parcel), "side")
    before = onward(parcel, 1)
    far_mate = swap(after(far, mate, before), "side")
    entries = [far_mate, far, mate, normed_own]

    away = away_partial(entries, proj)
    own, over_own, normed = kept_partials([after(e, away) for e in entries], proj)
    near_pair = lax.optimization_barrier(jnp.concatenate([parcel, before]))
    far_pair = onward(after(near_pair, away), 2)
    got_over = after(swap(away, "seq", 1), over_own, far_pair)
    over = lax.optimization_barrier((over_own + got_over.astype(F32)).astype(BF))
    got_far = swap(over, "seq", 2)
    got_beside = swap(beside_partial(after(normed, over), proj), "seq", 1)
    teacher_rows = attention_rows(after(teacher_queries, over), [near_pair, far_pair], pieces)
    predicted = lax.optimization_barrier(own + got_far.astype(F32)) + got_beside.astype(F32)
    delta = (predicted - teacher_rows.astype(F32)).astype(BF)

    delta_far = swap(delta, "seq", 2)
    own_product = product(delta, proj)
    delta_beside = swap(after(delta, own_product), "seq", 1)
    delta_last = swap(delta_far, "seq", 1)
    deltas = [delta, delta_beside, delta_far, delta_last]
    products = [own_product, product(delta_beside, proj), product(delta_far, proj)]

    sent, kept = route_products(products, delta_last, proj)
    got = swap(sent, "side")
    cross = lax.optimization_barrier((kept[1].astype(F32) + got[1].astype(F32)).astype(BF))
    crossed = swap(cross, "mp")
    near = lax.optimization_barrier(kept[0].astype(F32) + after(got[0], cross).astype(F32))

    factor = 1.0 / math.sqrt(rows * n)
    deltas = after(jnp.concatenate([deltas[k] for k in (0, 2, 1, 3)]), cross)
    grad_proj = lax.optimization_barrier(dot(normed, deltas, ((0,), (0,))) * factor)
    feature_rows = (near + after(crossed, grad_proj).astype(F32)).astype(BF)

    leaving = [dot(drop[k * slots : (k + 1) * slots], feature_rows).astype(BF) for k in range(n)]
    arrived = [leaving[0]] + exchange(leaving)
    across = [swap(block, "mp") for block in arrived]
    grad_pair = grad_rows(hidden, small, arrived + across)
    grad_mates = swap(grad_pair, "side")
    grad_hidden = write_rows(grad_mates, 1, write_rows(grad_pair, 0)).reshape(capacity, width)
    return (grad_hidden, grad_proj)


def general(
    teacher_queries, teacher_keys, teacher_values, doc_ids, owner, student_hidden, norm_gain, proj
):
    n = lax.axis_size("seq")
    me = lax.axis_index("seq")
    side = lax.axis_index("side")
    plane = lax.axis_size("mp") * lax.axis_size("side")
    mine = lax.axis_index("mp") * lax.axis_size("side") + side
    rows = teacher_queries.shape[0]
    heads = teacher_queries.shape[1] // HD
    kv_local = teacher_keys.shape[1] // HD
    group = heads * lax.axis_size("side") // kv_local
    width = student_hidden.shape[1]
    depth = proj.shape[0]
    capacity = student_hidden.shape[0]
    slots = capacity // n
    shared = n // plane
    held = shared * slots

    hidden = lax.dynamic_slice_in_dim(student_hidden, mine * held, held, 0).astype(F32)
    inverse_rms = lax.rsqrt(jnp.mean(hidden * hidden, axis=1, keepdims=True) + 1e-06)
    normed = (hidden * inverse_rms * norm_gain).astype(BF)
    normed_slots = lax.all_to_all(
        normed.reshape(held, n, depth).transpose(1, 0, 2), "seq", 0, 0, tiled=True
    )

    head = side * heads // group
    key_head = lax.dynamic_slice_in_dim(teacher_keys, head * HD, HD, 1)
    value_head = lax.dynamic_slice_in_dim(teacher_values, head * HD, HD, 1)
    small = jnp.stack([doc_ids, owner[:, 0]]).astype(BF)
    parcel = jnp.concatenate([key_head, value_head, jnp.pad(small, ((0, 14), (0, 0)))])
    parcel = lax.all_gather(parcel, "seq", axis=0, tiled=False)
    keys, values = parcel[:, :rows], parcel[:, rows : 2 * rows]
    docs = parcel[:, 2 * rows].astype(I32)
    owners = parcel[:, 2 * rows + 1].astype(I32)

    query_pos = me * rows + jnp.arange(rows, dtype=I32)
    key_pos = jnp.arange(n * rows, dtype=I32)
    allowed = (docs.reshape(-1)[None, :] == doc_ids[:, None]) & (
        key_pos[None, :] <= query_pos[:, None]
    )
    stacked = teacher_queries.reshape(rows, heads, HD).transpose(1, 0, 2)
    scores = jnp.einsum("hqd,kd->hqk", stacked, keys.reshape(-1, HD), preferred_element_type=F32)
    scores = jnp.where(allowed[None], scores * (1.0 / math.sqrt(HD)), -1e30)
    top = jnp.max(scores, axis=2, keepdims=True)
    probs = jnp.where(allowed[None], jnp.exp(scores - top), 0.0)
    totals = jnp.sum(probs, axis=2, keepdims=True)
    weighted = jnp.einsum(
        "hqk,kd->hqd", probs.astype(BF), values.reshape(-1, HD), preferred_element_type=F32
    )
    teacher_rows = (weighted / totals).astype(BF).transpose(1, 0, 2).reshape(rows, heads * HD)

    own_blocks = lax.dynamic_slice_in_dim(owners, mine * shared, shared, 0)
    order = jnp.arange(rows, dtype=I32)
    same = (own_blocks[:, :, None] == own_blocks[:, None, :]) & (order[:, None] > order[None, :])
    rank = jnp.sum(same.astype(I32), axis=2)
    spot = own_blocks * held + jnp.arange(shared, dtype=I32)[:, None] * slots + rank
    pick = (spot.reshape(-1)[:, None] == jnp.arange(n * held, dtype=I32)[None, :]).astype(BF)

    normed_own = dot(pick, normed_slots.reshape(n * held, depth)).astype(BF)
    normed_rows = lax.all_gather(normed_own, ("mp", "side"), axis=0, tiled=True)
    partial = dot(normed_rows, proj).astype(BF)
    predicted = lax.psum_scatter(partial, "seq", scatter_dimension=0, tiled=True).astype(F32)
    delta = (predicted - teacher_rows.astype(F32)).astype(BF)
    deltas = lax.all_gather(delta, "seq", axis=0, tiled=True)

    products = dot(deltas, proj, ((1,), (1,))).astype(BF)
    feature_rows = lax.psum_scatter(products, ("mp", "side"), scatter_dimension=0, tiled=True)
    feature_slots = dot(pick, feature_rows, ((0,), (0,))).astype(BF).reshape(n, held, depth)
    received = lax.all_to_all(feature_slots, "seq", 0, 0, tiled=True)
    feature_grad = received.transpose(1, 0, 2).reshape(held, width)

    gain_grad = feature_grad.astype(F32) * norm_gain
    mean_term = jnp.mean(gain_grad * hidden, axis=1, keepdims=True)
    grad_own = (inverse_rms * gain_grad - inverse_rms**3 * hidden * mean_term).astype(BF)
    grad_hidden = lax.all_gather(grad_own, ("mp", "side"), axis=0, tiled=True)

    grad_proj = dot(normed_rows, deltas, ((0,), (0,))) * (1.0 / math.sqrt(rows * n))
    return (grad_hidden, grad_proj)


def solution(mesh):
    sizes = mesh.shape
    paired = PAIRWISE and (sizes["seq"], sizes["mp"], sizes["side"]) == (4, 2, 2)
    return jax.shard_map(
        pairwise if paired else general,
        mesh=mesh,
        in_specs=(
            P(("groups", "seq"), ("mp", "side")),
            P(("groups", "seq"), "mp"),
            P(("groups", "seq"), "mp"),
            P(("groups", "seq")),
            P(("groups", "seq"), None),
            P(("groups", "seq"), None),
            P(),
            P("seq", ("mp", "side")),
        ),
        out_specs=(P(("groups", "seq"), None), P(("groups", "seq"), ("mp", "side"))),
        check_vma=False,
    )
```

```python
import functools
import math

import jax
import jax.numpy as jnp
from jax import lax
from jax.experimental import pallas as pl
from jax.experimental.pallas import tpu as pltpu
from jax.sharding import PartitionSpec as P

HD = 128
LANES = 128
BF = jnp.bfloat16
F32 = jnp.float32
I32 = jnp.int32
PARAMS = pltpu.CompilerParams(vmem_limit_bytes=16 * 1024 * 1024)
NORM_MB = 52
PAIRWISE = True


def dot(a, b, dims=((1,), (0,))):
    return lax.dot_general(a, b, (dims, ((), ())), preferred_element_type=F32)


def eye(size):
    return lax.broadcasted_iota(I32, (size, size), 0) == lax.broadcasted_iota(I32, (size, size), 1)


def to_row(column):
    return jnp.sum(jnp.where(eye(column.shape[0]), column, 0.0), axis=0, keepdims=True)


def to_column(row):
    return jnp.sum(jnp.where(eye(row.shape[1]), row, 0.0), axis=1, keepdims=True)


def indices():
    return lax.axis_index("seq"), lax.axis_index("mp") * 2 + lax.axis_index("side")


def call(kernel, shapes, args, flops, moved, transcendentals=0, **more):
    vmem = pl.BlockSpec(memory_space=pltpu.VMEM)
    options = dict(
        in_specs=[vmem] * len(args),
        out_specs=jax.tree.map(lambda s: vmem, shapes),
        compiler_params=PARAMS,
    )
    options.update(more)
    return pl.pallas_call(
        kernel,
        out_shape=shapes,
        cost_estimate=pl.CostEstimate(
            flops=flops, bytes_accessed=moved, transcendentals=transcendentals
        ),
        **options,
    )(*args)


def inverse_rms(hidden):
    width = hidden.shape[1]
    return lax.rsqrt(jnp.sum(hidden * hidden, axis=1, keepdims=True) / width + 1e-06)


def norm_kernel(student_any, small_ref, *refs):
    *pieces, hidden_ref, arrived = refs
    me, mine = indices()
    copies = [
        pltpu.make_async_copy(student_any.at[mine ^ (2 * i)], hidden_ref.at[i], arrived.at[i])
        for i in range(2)
    ]
    for copy in copies:
        copy.start()
    _, rows, width = hidden_ref.shape
    tiles = width // len(pieces) // LANES
    line = lax.broadcasted_iota(I32, (rows, LANES), 0)
    last = width // LANES
    owner_row, docs_row = small_ref[last : last + 1, :], small_ref[last + 1 : last + 2, :]
    extra = jnp.where(line == 0, owner_row, jnp.where(line == 1, docs_row, 0.0)).astype(BF)
    for piece in pieces:
        piece[:, tiles * LANES :] = extra
    copies[0].wait()
    inverse = inverse_rms(hidden_ref[0].astype(F32))
    for k, piece in enumerate(pieces):
        for tile in range(tiles):
            at = (me ^ k) * tiles + tile
            columns = pl.ds(pl.multiple_of(at * LANES, LANES), LANES)
            block = hidden_ref[0, :, columns].astype(F32)
            normed = block * inverse * small_ref[pl.ds(at, 1), :]
            piece[:, tile * LANES : (tile + 1) * LANES] = normed.astype(BF)
    copies[1].wait()


def norm_pieces(student, small):
    n, rows, width = student.shape
    piece = jax.ShapeDtypeStruct((rows, width // n + LANES), BF)
    return call(
        norm_kernel,
        [piece] * n + [jax.ShapeDtypeStruct((2, rows, width), BF)],
        (student, small),
        6 * rows * width,
        8 * rows * width,
        in_specs=[pl.BlockSpec(memory_space=pl.ANY), pl.BlockSpec(memory_space=pltpu.VMEM)],
        scratch_shapes=[pltpu.SemaphoreType.DMA((2,))],
        compiler_params=pltpu.CompilerParams(vmem_limit_bytes=NORM_MB * 1024 * 1024),
    )


def pick_kernel(*refs):
    *pieces, out_ref, drop_ref = refs
    pieces = pieces[::-1]
    me, mine = indices()
    tokens, depth = out_ref.shape
    slots = pieces[0].shape[0]
    spots = slots * len(pieces)
    owner_row = jnp.zeros((1, tokens), F32)
    for k, piece in enumerate(pieces):
        tile = piece[0:16, depth:].astype(F32)[0:1]
        owner_row = owner_row + jnp.where((me ^ mine) == k, tile, 0.0)
    owner = to_column(owner_row)
    earlier = lax.broadcasted_iota(I32, (tokens, tokens), 1) < lax.broadcasted_iota(
        I32, (tokens, tokens), 0
    )
    same = jnp.where(earlier & (owner == owner_row), 1.0, 0.0)
    rank = jnp.sum(same, axis=1, keepdims=True)
    peer = owner.astype(I32) ^ me
    spot = (peer * slots).astype(F32) + rank
    take = (lax.broadcasted_iota(I32, (tokens, spots), 1) == spot.astype(I32)).astype(F32)
    stacked = jnp.concatenate([piece[:, :depth] for piece in pieces], axis=0)
    out_ref[...] = dot(take.astype(BF), stacked).astype(BF)
    spot_row = to_row(spot).astype(I32)
    drop = (lax.broadcasted_iota(I32, (spots, tokens), 0) == spot_row).astype(F32)
    drop_ref[...] = drop.astype(BF)


def pick_rows(pieces, tokens):
    slots, wide = pieces[0].shape
    depth, spots = wide - LANES, slots * len(pieces)
    return call(
        pick_kernel,
        [jax.ShapeDtypeStruct((tokens, depth), BF), jax.ShapeDtypeStruct((spots, tokens), BF)],
        pieces[::-1],
        2 * tokens * spots * depth,
        4 * spots * depth,
    )


def attention_kernel(queries_ref, *refs):
    out_ref = refs[-1]
    n = (len(refs) - 1) // 2
    parcels, pieces = refs[:n], refs[n : 2 * n]
    tokens = queries_ref.shape[0]
    depth = pieces[0].shape[1] - LANES
    me, _ = indices()
    keys = jnp.concatenate([parcel[:tokens, :] for parcel in parcels], axis=0)
    values = jnp.concatenate([parcel[tokens:, :] for parcel in parcels], axis=0)
    docs = [piece[0:16, depth:].astype(F32)[1:2] for piece in pieces]
    doc_column = to_column(docs[0])
    query_pos = me * tokens + lax.broadcasted_iota(I32, (tokens, tokens), 0)
    within = lax.broadcasted_iota(I32, (tokens, tokens), 1)
    masks = []
    for k in range(n):
        block = (me - k + n) % n
        doc_row = sum(jnp.where((me ^ block) == i, docs[i], 0.0) for i in range(n))
        near = block * tokens + within <= query_pos
        masks.append(jnp.where(near & (doc_row == doc_column), 1.0, 0.0))
    allowed = jnp.concatenate(masks, axis=1) > 0.5
    scale_factor = 1.0 / math.sqrt(HD)
    for h in range(queries_ref.shape[1] // HD):
        columns = slice(h * HD, (h + 1) * HD)
        scores = dot(queries_ref[:, columns], keys, ((1,), (1,))) * scale_factor
        scores = jnp.where(allowed, scores, -1e30)
        top = jnp.max(scores, axis=1, keepdims=True)
        probs = jnp.where(allowed, jnp.exp(scores - top), 0.0)
        total = jnp.sum(probs, axis=1, keepdims=True)
        out_ref[:, columns] = (dot(probs.astype(BF), values) / total).astype(BF)


def attention_rows(queries, parcels, pieces):
    tokens, width = queries.shape
    return call(
        attention_kernel,
        jax.ShapeDtypeStruct((tokens, width), BF),
        (queries, *parcels, *pieces),
        0,
        4 * tokens * width,
    )


def pick_entry(refs, at):
    d, c, b, a = (ref[...] for ref in refs)
    odd = at % 2 == 1
    return jnp.where(at >= 2, jnp.where(odd, d, c), jnp.where(odd, b, a))


def away_kernel(*refs):
    *entries, proj_ref, out_ref = refs
    me, mine = indices()
    block = pick_entry(entries, me ^ mine ^ 3)
    out_ref[...] = dot(block, proj_ref[...]).astype(BF)


def kept_kernel(*refs):
    *entries, proj_ref, own_ref, over_ref, normed_ref = refs
    me, mine = indices()
    rows = entries[0].shape[0]
    for k, spot in enumerate((0, 2, 1, 3)):
        normed_ref[spot * rows : (spot + 1) * rows, :] = pick_entry(entries, me ^ mine ^ k)
    columns = 256
    for first in range(0, proj_ref.shape[1], columns):
        part = slice(first, first + columns)
        product = dot(normed_ref[: 2 * rows, :], proj_ref[:, part])
        own_ref[:, part] = product[:rows]
        over_ref[:, part] = product[rows:]


def beside_kernel(normed_ref, proj_ref, out_ref):
    rows = out_ref.shape[0]
    out_ref[...] = dot(normed_ref[2 * rows : 3 * rows, :], proj_ref[...]).astype(BF)


def away_partial(entries, proj):
    rows, depth = entries[0].shape
    out = jax.ShapeDtypeStruct((rows, proj.shape[1]), BF)
    return call(away_kernel, out, (*entries, proj), 0, 0)


def kept_partials(entries, proj):
    rows, depth = entries[0].shape
    out = jax.ShapeDtypeStruct((rows, proj.shape[1]), F32)
    shapes = [out, out, jax.ShapeDtypeStruct((4 * rows, depth), BF)]
    return call(kept_kernel, shapes, (*entries, proj), 0, 0)


def beside_partial(normed, proj):
    out = jax.ShapeDtypeStruct((normed.shape[0] // 4, proj.shape[1]), BF)
    return call(beside_kernel, out, (normed, proj), 0, 0)


def product_kernel(delta_ref, proj_ref, out_ref):
    out_ref[...] = dot(delta_ref[...], proj_ref[...], ((1,), (1,))).astype(BF)


def product(delta, proj):
    out = jax.ShapeDtypeStruct((delta.shape[0], proj.shape[0]), BF)
    return call(product_kernel, out, (delta, proj), 0, 0)


def route_kernel(first_ref, second_ref, third_ref, delta_ref, proj_ref, sent_ref, kept_ref, held):
    me, mine = indices()
    last = dot(delta_ref[...], proj_ref[...], ((1,), (1,))).astype(BF)
    for k, block in enumerate((first_ref[...], second_ref[...], third_ref[...], last)):
        held[k] = block
    off = me ^ mine
    kept_ref[0] = held[off]
    sent_ref[0] = held[off ^ 1]
    kept_ref[1] = held[off ^ 2]
    sent_ref[1] = held[off ^ 3]


def route_products(products, delta, proj):
    tokens, depth = products[0].shape
    pair = jax.ShapeDtypeStruct((2, tokens, depth), BF)
    return call(
        route_kernel,
        [pair, pair],
        (*products, delta, proj),
        0,
        0,
        scratch_shapes=[pltpu.VMEM((4, tokens, depth), BF)],
    )


def leave_kernel(peers, drop_ref, kept_ref, got_ref, crossed_ref, *outs):
    near = kept_ref[0].astype(F32) + got_ref[0].astype(F32)
    rows = (near + crossed_ref[...].astype(F32)).astype(BF)
    slots = outs[0].shape[0]
    for k, out in zip(peers, outs):
        out[...] = dot(drop_ref[k * slots : (k + 1) * slots, :], rows).astype(BF)


def leaving_rows(peers, drop, kept, got, crossed):
    out = jax.ShapeDtypeStruct((drop.shape[0] // 4, crossed.shape[1]), BF)
    kernel = functools.partial(leave_kernel, peers)
    return call(kernel, [out] * len(peers), (drop, kept, got, crossed), 0, 0)


def rows_kernel(hidden_ref, small_ref, *refs):
    *pieces, out_ref = refs
    me, _ = indices()
    blocks, rows, width = hidden_ref.shape
    n = len(pieces) // blocks
    tiles = width // n // LANES
    for i in range(blocks):
        inverse = inverse_rms(hidden_ref[i].astype(F32))
        spots = [
            (piece, tile, (me ^ k) * tiles + tile)
            for k, piece in enumerate(pieces[i * n : (i + 1) * n])
            for tile in range(tiles)
        ]
        total = jnp.zeros((rows, LANES), F32)
        for piece, tile, at in spots:
            columns = pl.ds(pl.multiple_of(at * LANES, LANES), LANES)
            block = hidden_ref[i, :, columns].astype(F32)
            grad = piece[:, tile * LANES : (tile + 1) * LANES].astype(F32)
            total = total + grad * small_ref[pl.ds(at, 1), :] * block
        mean = jnp.sum(total, axis=1, keepdims=True) / width
        lean = inverse * inverse * inverse * mean
        for piece, tile, at in spots:
            columns = pl.ds(pl.multiple_of(at * LANES, LANES), LANES)
            block = hidden_ref[i, :, columns].astype(F32)
            grad = piece[:, tile * LANES : (tile + 1) * LANES].astype(F32)
            grad = inverse * (grad * small_ref[pl.ds(at, 1), :]) - lean * block
            out_ref[i, :, columns] = grad.astype(BF)


def grad_rows(hidden, small, pieces):
    return call(
        rows_kernel,
        jax.ShapeDtypeStruct(hidden.shape, BF),
        (hidden, small, *pieces),
        14 * hidden.size,
        6 * hidden.size,
    )


def write_kernel(first, pair_ref, out_ref, done):
    _, mine = indices()
    copies = [
        pltpu.make_async_copy(pair_ref.at[i], out_ref.at[mine ^ first ^ (2 * i)], done.at[i])
        for i in range(2)
    ]
    for copy in copies:
        copy.start()
    for copy in copies:
        copy.wait()


def write_rows(pair, first, target=None):
    _, rows, width = pair.shape
    hbm, vmem = pl.BlockSpec(memory_space=pltpu.HBM), pl.BlockSpec(memory_space=pltpu.VMEM)
    kernel = functools.partial(write_kernel, first)
    args, specs, aliases = (pair,), [vmem], {}
    if target is not None:
        kernel = lambda t, *refs: write_kernel(first, *refs)
        args, specs, aliases = (target, pair), [hbm, vmem], {0: 0}
    return call(
        kernel,
        jax.ShapeDtypeStruct((4, rows, width), BF),
        args,
        0,
        4 * pair.size,
        in_specs=specs,
        out_specs=hbm,
        input_output_aliases=aliases,
        scratch_shapes=[pltpu.SemaphoreType.DMA((2,))],
    )


def swap(x, axis, k=1):
    return lax.ppermute(x, axis, [(i, i ^ k) for i in range(lax.axis_size(axis))])


def onward(x):
    return lax.ppermute(x, "seq", [(i, i + 1) for i in range(lax.axis_size("seq") - 1)])


def exchange(blocks):
    got = {k: swap(blocks[k], "seq", k) for k in reversed(range(1, len(blocks)))}
    return [got[k] for k in range(1, len(blocks))]


def after(x, *others):
    return lax.optimization_barrier((x, *others))[0]


def pairwise(
    teacher_queries, teacher_keys, teacher_values, doc_ids, owner, student_hidden, norm_gain, proj
):
    n = 4
    me, mine = indices()
    side = lax.axis_index("side")
    rows = teacher_queries.shape[0]
    heads = teacher_queries.shape[1] // HD
    kv_local = teacher_keys.shape[1] // HD
    group = heads * 2 // kv_local
    capacity, width = student_hidden.shape
    slots = capacity // n
    student = student_hidden.reshape(n, slots, width)
    tiles = width // LANES
    line = lax.broadcasted_iota(I32, (tiles + 2, LANES), 0)
    ids = jnp.where(line == tiles, owner[:, 0][None, :], doc_ids[None, :]).astype(F32)
    gain = jnp.pad(norm_gain.reshape(tiles, LANES), ((0, 2), (0, 0)))
    small = jnp.where(line < tiles, gain, ids)

    *made, hidden = norm_pieces(student, small)
    pieces = [made[0]] + exchange(made)

    head = side * heads // group
    parcel = jnp.concatenate(
        [
            lax.dynamic_slice_in_dim(teacher_keys, head * HD, HD, 1),
            lax.dynamic_slice_in_dim(teacher_values, head * HD, HD, 1),
        ]
    )
    parcels = [after(lax.optimization_barrier(parcel), made[0])]
    parcels.append(onward(parcels[0]))
    normed_own, drop = pick_rows([after(piece, parcels[1]) for piece in pieces], rows)

    far = swap(normed_own, "mp")
    mate = swap(normed_own, "side")
    parcels.append(onward(after(parcels[1], normed_own)))
    far_mate = swap(after(far, mate, parcels[2]), "side")
    entries = [far_mate, far, mate, normed_own]

    away = away_partial(entries, proj)
    own, over_own, normed = kept_partials([after(e, away) for e in entries], proj)
    parcels.append(onward(after(parcels[2], away)))
    got_over = after(swap(away, "seq", 1), over_own, parcels[3])
    over = lax.optimization_barrier((over_own + got_over.astype(F32)).astype(BF))
    got_far = swap(over, "seq", 2)
    got_beside = swap(beside_partial(after(normed, over), proj), "seq", 1)
    teacher_rows = attention_rows(after(teacher_queries, over), parcels, pieces)
    predicted = lax.optimization_barrier(own + got_far.astype(F32)) + got_beside.astype(F32)
    delta = (predicted - teacher_rows.astype(F32)).astype(BF)

    delta_far = swap(delta, "seq", 2)
    own_product = product(delta, proj)
    delta_beside = swap(after(delta, own_product), "seq", 1)
    delta_last = swap(delta_far, "seq", 1)
    deltas = [delta, delta_beside, delta_far, delta_last]
    products = [own_product, product(delta_beside, proj), product(delta_far, proj)]

    sent, kept = route_products(products, delta_last, proj)
    got = swap(sent, "side")
    cross = lax.optimization_barrier((kept[1].astype(F32) + got[1].astype(F32)).astype(BF))
    crossed = swap(cross, "mp")

    factor = 1.0 / math.sqrt(rows * n)
    deltas = after(jnp.concatenate([deltas[k] for k in (0, 2, 1, 3)]), cross)
    grad_proj = lax.optimization_barrier(dot(normed, deltas, ((0,), (0,))) * factor)
    crossed = after(crossed, grad_proj)
    leaving = leaving_rows(range(n), drop, kept, got, crossed)

    arrived = [leaving[0]] + exchange(leaving)
    across = [swap(block, "mp") for block in arrived]
    grad_pair = grad_rows(hidden, small, arrived + across)
    grad_mates = swap(grad_pair, "side")
    grad_hidden = write_rows(grad_mates, 1, write_rows(grad_pair, 0)).reshape(capacity, width)
    return (grad_hidden, grad_proj)


def general(
    teacher_queries, teacher_keys, teacher_values, doc_ids, owner, student_hidden, norm_gain, proj
):
    n = lax.axis_size("seq")
    me = lax.axis_index("seq")
    side = lax.axis_index("side")
    plane = lax.axis_size("mp") * lax.axis_size("side")
    mine = lax.axis_index("mp") * lax.axis_size("side") + side
    rows = teacher_queries.shape[0]
    heads = teacher_queries.shape[1] // HD
    kv_local = teacher_keys.shape[1] // HD
    group = heads * lax.axis_size("side") // kv_local
    width = student_hidden.shape[1]
    depth = proj.shape[0]
    capacity = student_hidden.shape[0]
    slots = capacity // n
    shared = n // plane
    held = shared * slots

    hidden = lax.dynamic_slice_in_dim(student_hidden, mine * held, held, 0).astype(F32)
    inverse_rms = lax.rsqrt(jnp.mean(hidden * hidden, axis=1, keepdims=True) + 1e-06)
    normed = (hidden * inverse_rms * norm_gain).astype(BF)
    normed_slots = lax.all_to_all(
        normed.reshape(held, n, depth).transpose(1, 0, 2), "seq", 0, 0, tiled=True
    )

    head = side * heads // group
    key_head = lax.dynamic_slice_in_dim(teacher_keys, head * HD, HD, 1)
    value_head = lax.dynamic_slice_in_dim(teacher_values, head * HD, HD, 1)
    small = jnp.stack([doc_ids, owner[:, 0]]).astype(BF)
    parcel = jnp.concatenate([key_head, value_head, jnp.pad(small, ((0, 14), (0, 0)))])
    parcel = lax.all_gather(parcel, "seq", axis=0, tiled=False)
    keys, values = parcel[:, :rows], parcel[:, rows : 2 * rows]
    docs = parcel[:, 2 * rows].astype(I32)
    owners = parcel[:, 2 * rows + 1].astype(I32)

    query_pos = me * rows + jnp.arange(rows, dtype=I32)
    key_pos = jnp.arange(n * rows, dtype=I32)
    allowed = (docs.reshape(-1)[None, :] == doc_ids[:, None]) & (
        key_pos[None, :] <= query_pos[:, None]
    )
    stacked = teacher_queries.reshape(rows, heads, HD).transpose(1, 0, 2)
    scores = jnp.einsum("hqd,kd->hqk", stacked, keys.reshape(-1, HD), preferred_element_type=F32)
    scores = jnp.where(allowed[None], scores * (1.0 / math.sqrt(HD)), -1e30)
    top = jnp.max(scores, axis=2, keepdims=True)
    probs = jnp.where(allowed[None], jnp.exp(scores - top), 0.0)
    totals = jnp.sum(probs, axis=2, keepdims=True)
    weighted = jnp.einsum(
        "hqk,kd->hqd", probs.astype(BF), values.reshape(-1, HD), preferred_element_type=F32
    )
    teacher_rows = (weighted / totals).astype(BF).transpose(1, 0, 2).reshape(rows, heads * HD)

    own_blocks = lax.dynamic_slice_in_dim(owners, mine * shared, shared, 0)
    order = jnp.arange(rows, dtype=I32)
    same = (own_blocks[:, :, None] == own_blocks[:, None, :]) & (order[:, None] > order[None, :])
    rank = jnp.sum(same.astype(I32), axis=2)
    spot = own_blocks * held + jnp.arange(shared, dtype=I32)[:, None] * slots + rank
    pick = (spot.reshape(-1)[:, None] == jnp.arange(n * held, dtype=I32)[None, :]).astype(BF)

    normed_own = dot(pick, normed_slots.reshape(n * held, depth)).astype(BF)
    normed_rows = lax.all_gather(normed_own, ("mp", "side"), axis=0, tiled=True)
    partial = dot(normed_rows, proj).astype(BF)
    predicted = lax.psum_scatter(partial, "seq", scatter_dimension=0, tiled=True).astype(F32)
    delta = (predicted - teacher_rows.astype(F32)).astype(BF)
    deltas = lax.all_gather(delta, "seq", axis=0, tiled=True)

    products = dot(deltas, proj, ((1,), (1,))).astype(BF)
    feature_rows = lax.psum_scatter(products, ("mp", "side"), scatter_dimension=0, tiled=True)
    feature_slots = dot(pick, feature_rows, ((0,), (0,))).astype(BF).reshape(n, held, depth)
    received = lax.all_to_all(feature_slots, "seq", 0, 0, tiled=True)
    feature_grad = received.transpose(1, 0, 2).reshape(held, width)

    gain_grad = feature_grad.astype(F32) * norm_gain
    mean_term = jnp.mean(gain_grad * hidden, axis=1, keepdims=True)
    grad_own = (inverse_rms * gain_grad - inverse_rms**3 * hidden * mean_term).astype(BF)
    grad_hidden = lax.all_gather(grad_own, ("mp", "side"), axis=0, tiled=True)

    grad_proj = dot(normed_rows, deltas, ((0,), (0,))) * (1.0 / math.sqrt(rows * n))
    return (grad_hidden, grad_proj)


def solution(mesh):
    sizes = mesh.shape
    paired = PAIRWISE and (sizes["seq"], sizes["mp"], sizes["side"]) == (4, 2, 2)
    return jax.shard_map(
        pairwise if paired else general,
        mesh=mesh,
        in_specs=(
            P(("groups", "seq"), ("mp", "side")),
            P(("groups", "seq"), "mp"),
            P(("groups", "seq"), "mp"),
            P(("groups", "seq")),
            P(("groups", "seq"), None),
            P(("groups", "seq"), None),
            P(),
            P("seq", ("mp", "side")),
        ),
        out_specs=(P(("groups", "seq"), None), P(("groups", "seq"), ("mp", "side"))),
        check_vma=False,
    )
```

```python
import functools
import math

import jax
import jax.numpy as jnp
from jax import lax
from jax.experimental import pallas as pl
from jax.experimental.pallas import tpu as pltpu
from jax.sharding import PartitionSpec as P

HD = 128
LANES = 128
BF = jnp.bfloat16
F32 = jnp.float32
I32 = jnp.int32
PARAMS = pltpu.CompilerParams(vmem_limit_bytes=16 * 1024 * 1024)
NORM_MB = 52
PAIRWISE = True


def dot(a, b, dims=((1,), (0,))):
    return lax.dot_general(a, b, (dims, ((), ())), preferred_element_type=F32)


def eye(size):
    return lax.broadcasted_iota(I32, (size, size), 0) == lax.broadcasted_iota(I32, (size, size), 1)


def to_row(column):
    return jnp.sum(jnp.where(eye(column.shape[0]), column, 0.0), axis=0, keepdims=True)


def to_column(row):
    return jnp.sum(jnp.where(eye(row.shape[1]), row, 0.0), axis=1, keepdims=True)


def indices():
    return lax.axis_index("seq"), lax.axis_index("mp") * 2 + lax.axis_index("side")


def call(kernel, shapes, args, flops, moved, transcendentals=0, **more):
    vmem = pl.BlockSpec(memory_space=pltpu.VMEM)
    options = dict(
        in_specs=[vmem] * len(args),
        out_specs=jax.tree.map(lambda s: vmem, shapes),
        compiler_params=PARAMS,
    )
    options.update(more)
    return pl.pallas_call(
        kernel,
        out_shape=shapes,
        cost_estimate=pl.CostEstimate(
            flops=flops, bytes_accessed=moved, transcendentals=transcendentals
        ),
        **options,
    )(*args)


def inverse_rms(hidden):
    width = hidden.shape[1]
    return lax.rsqrt(jnp.sum(hidden * hidden, axis=1, keepdims=True) / width + 1e-06)


def norm_kernel(student_any, small_ref, *refs):
    *pieces, hidden_ref, arrived = refs
    me, mine = indices()
    copies = [
        pltpu.make_async_copy(student_any.at[mine ^ (2 * i)], hidden_ref.at[i], arrived.at[i])
        for i in range(2)
    ]
    for copy in copies:
        copy.start()
    _, rows, width = hidden_ref.shape
    tiles = width // len(pieces) // LANES
    line = lax.broadcasted_iota(I32, (rows, LANES), 0)
    last = width // LANES
    owner_row, docs_row = small_ref[last : last + 1, :], small_ref[last + 1 : last + 2, :]
    extra = jnp.where(line == 0, owner_row, jnp.where(line == 1, docs_row, 0.0)).astype(BF)
    for piece in pieces:
        piece[:, tiles * LANES :] = extra
    copies[0].wait()
    inverse = inverse_rms(hidden_ref[0].astype(F32))
    for k, piece in enumerate(pieces):
        for tile in range(tiles):
            at = (me ^ k) * tiles + tile
            columns = pl.ds(pl.multiple_of(at * LANES, LANES), LANES)
            block = hidden_ref[0, :, columns].astype(F32)
            normed = block * inverse * small_ref[pl.ds(at, 1), :]
            piece[:, tile * LANES : (tile + 1) * LANES] = normed.astype(BF)
    copies[1].wait()


def norm_pieces(student, small):
    n, rows, width = student.shape
    piece = jax.ShapeDtypeStruct((rows, width // n + LANES), BF)
    return call(
        norm_kernel,
        [piece] * n + [jax.ShapeDtypeStruct((2, rows, width), BF)],
        (student, small),
        6 * rows * width,
        8 * rows * width,
        in_specs=[pl.BlockSpec(memory_space=pl.ANY), pl.BlockSpec(memory_space=pltpu.VMEM)],
        scratch_shapes=[pltpu.SemaphoreType.DMA((2,))],
        compiler_params=pltpu.CompilerParams(vmem_limit_bytes=NORM_MB * 1024 * 1024),
    )


def pick_kernel(*refs):
    *pieces, out_ref, drop_ref = refs
    pieces = pieces[::-1]
    me, mine = indices()
    tokens, depth = out_ref.shape
    slots = pieces[0].shape[0]
    spots = slots * len(pieces)
    owner_row = jnp.zeros((1, tokens), F32)
    for k, piece in enumerate(pieces):
        tile = piece[0:16, depth:].astype(F32)[0:1]
        owner_row = owner_row + jnp.where((me ^ mine) == k, tile, 0.0)
    owner = to_column(owner_row)
    earlier = lax.broadcasted_iota(I32, (tokens, tokens), 1) < lax.broadcasted_iota(
        I32, (tokens, tokens), 0
    )
    same = jnp.where(earlier & (owner == owner_row), 1.0, 0.0)
    rank = jnp.sum(same, axis=1, keepdims=True)
    peer = owner.astype(I32) ^ me
    spot = (peer * slots).astype(F32) + rank
    take = (lax.broadcasted_iota(I32, (tokens, spots), 1) == spot.astype(I32)).astype(F32)
    stacked = jnp.concatenate([piece[:, :depth] for piece in pieces], axis=0)
    out_ref[...] = dot(take.astype(BF), stacked).astype(BF)
    spot_row = to_row(spot).astype(I32)
    drop = (lax.broadcasted_iota(I32, (spots, tokens), 0) == spot_row).astype(F32)
    drop_ref[...] = drop.astype(BF)


def pick_rows(pieces, tokens):
    slots, wide = pieces[0].shape
    depth, spots = wide - LANES, slots * len(pieces)
    return call(
        pick_kernel,
        [jax.ShapeDtypeStruct((tokens, depth), BF), jax.ShapeDtypeStruct((spots, tokens), BF)],
        pieces[::-1],
        2 * tokens * spots * depth,
        4 * spots * depth,
    )


def attention_kernel(queries_ref, *refs):
    out_ref = refs[-1]
    n = (len(refs) - 1) // 2
    parcels, pieces = refs[:n], refs[n : 2 * n]
    tokens = queries_ref.shape[0]
    depth = pieces[0].shape[1] - LANES
    me, _ = indices()
    keys = jnp.concatenate([parcel[:tokens, :] for parcel in parcels], axis=0)
    values = jnp.concatenate([parcel[tokens:, :] for parcel in parcels], axis=0)
    docs = [piece[0:16, depth:].astype(F32)[1:2] for piece in pieces]
    doc_column = to_column(docs[0])
    query_pos = me * tokens + lax.broadcasted_iota(I32, (tokens, tokens), 0)
    within = lax.broadcasted_iota(I32, (tokens, tokens), 1)
    masks = []
    for k in range(n):
        block = (me - k + n) % n
        doc_row = sum(jnp.where((me ^ block) == i, docs[i], 0.0) for i in range(n))
        near = block * tokens + within <= query_pos
        masks.append(jnp.where(near & (doc_row == doc_column), 1.0, 0.0))
    allowed = jnp.concatenate(masks, axis=1) > 0.5
    scale_factor = 1.0 / math.sqrt(HD)
    for h in range(queries_ref.shape[1] // HD):
        columns = slice(h * HD, (h + 1) * HD)
        scores = dot(queries_ref[:, columns], keys, ((1,), (1,))) * scale_factor
        scores = jnp.where(allowed, scores, -1e30)
        top = jnp.max(scores, axis=1, keepdims=True)
        probs = jnp.where(allowed, jnp.exp(scores - top), 0.0)
        total = jnp.sum(probs, axis=1, keepdims=True)
        out_ref[:, columns] = (dot(probs.astype(BF), values) / total).astype(BF)


def attention_rows(queries, parcels, pieces):
    tokens, width = queries.shape
    return call(
        attention_kernel,
        jax.ShapeDtypeStruct((tokens, width), BF),
        (queries, *parcels, *pieces),
        0,
        4 * tokens * width,
    )


def pick_entry(refs, at):
    d, c, b, a = (ref[...] for ref in refs)
    odd = at % 2 == 1
    return jnp.where(at >= 2, jnp.where(odd, d, c), jnp.where(odd, b, a))


def away_kernel(*refs):
    *entries, proj_ref, out_ref = refs
    me, mine = indices()
    block = pick_entry(entries, me ^ mine ^ 3)
    out_ref[...] = dot(block, proj_ref[...]).astype(BF)


def kept_kernel(*refs):
    *entries, proj_ref, own_ref, over_ref, normed_ref = refs
    me, mine = indices()
    rows = entries[0].shape[0]
    for k, spot in enumerate((0, 2, 1, 3)):
        normed_ref[spot * rows : (spot + 1) * rows, :] = pick_entry(entries, me ^ mine ^ k)
    columns = 256
    for first in range(0, proj_ref.shape[1], columns):
        part = slice(first, first + columns)
        product = dot(normed_ref[: 2 * rows, :], proj_ref[:, part])
        own_ref[:, part] = product[:rows]
        over_ref[:, part] = product[rows:]


def beside_kernel(normed_ref, proj_ref, out_ref):
    rows = out_ref.shape[0]
    out_ref[...] = dot(normed_ref[2 * rows : 3 * rows, :], proj_ref[...]).astype(BF)


def away_partial(entries, proj):
    rows, depth = entries[0].shape
    out = jax.ShapeDtypeStruct((rows, proj.shape[1]), BF)
    return call(away_kernel, out, (*entries, proj), 0, 0)


def kept_partials(entries, proj):
    rows, depth = entries[0].shape
    out = jax.ShapeDtypeStruct((rows, proj.shape[1]), F32)
    shapes = [out, out, jax.ShapeDtypeStruct((4 * rows, depth), BF)]
    return call(kept_kernel, shapes, (*entries, proj), 0, 0)


def beside_partial(normed, proj):
    out = jax.ShapeDtypeStruct((normed.shape[0] // 4, proj.shape[1]), BF)
    return call(beside_kernel, out, (normed, proj), 0, 0)


def product_kernel(delta_ref, proj_ref, out_ref):
    out_ref[...] = dot(delta_ref[...], proj_ref[...], ((1,), (1,))).astype(BF)


def product(delta, proj):
    out = jax.ShapeDtypeStruct((delta.shape[0], proj.shape[0]), BF)
    return call(product_kernel, out, (delta, proj), 0, 0)


def route_kernel(first_ref, second_ref, third_ref, delta_ref, proj_ref, sent_ref, kept_ref, held):
    me, mine = indices()
    last = dot(delta_ref[...], proj_ref[...], ((1,), (1,))).astype(BF)
    for k, block in enumerate((first_ref[...], second_ref[...], third_ref[...], last)):
        held[k] = block
    off = me ^ mine
    kept_ref[0] = held[off]
    sent_ref[0] = held[off ^ 1]
    kept_ref[1] = held[off ^ 2]
    sent_ref[1] = held[off ^ 3]


def route_products(products, delta, proj):
    tokens, depth = products[0].shape
    pair = jax.ShapeDtypeStruct((2, tokens, depth), BF)
    return call(
        route_kernel,
        [pair, pair],
        (*products, delta, proj),
        0,
        0,
        scratch_shapes=[pltpu.VMEM((4, tokens, depth), BF)],
    )


def leave_kernel(peers, drop_ref, kept_ref, got_ref, crossed_ref, *outs):
    near = kept_ref[0].astype(F32) + got_ref[0].astype(F32)
    rows = (near + crossed_ref[...].astype(F32)).astype(BF)
    slots = outs[0].shape[0]
    for k, out in zip(peers, outs):
        out[...] = dot(drop_ref[k * slots : (k + 1) * slots, :], rows).astype(BF)


def leaving_rows(peers, drop, kept, got, crossed):
    out = jax.ShapeDtypeStruct((drop.shape[0] // 4, crossed.shape[1]), BF)
    kernel = functools.partial(leave_kernel, peers)
    return call(kernel, [out] * len(peers), (drop, kept, got, crossed), 0, 0)


def rows_kernel(hidden_ref, small_ref, *refs):
    *pieces, out_ref = refs
    me, _ = indices()
    blocks, rows, width = hidden_ref.shape
    n = len(pieces) // blocks
    tiles = width // n // LANES
    for i in range(blocks):
        inverse = inverse_rms(hidden_ref[i].astype(F32))
        spots = [
            (piece, tile, (me ^ k) * tiles + tile)
            for k, piece in enumerate(pieces[i * n : (i + 1) * n])
            for tile in range(tiles)
        ]
        total = jnp.zeros((rows, LANES), F32)
        for piece, tile, at in spots:
            columns = pl.ds(pl.multiple_of(at * LANES, LANES), LANES)
            block = hidden_ref[i, :, columns].astype(F32)
            grad = piece[:, tile * LANES : (tile + 1) * LANES].astype(F32)
            total = total + grad * small_ref[pl.ds(at, 1), :] * block
        mean = jnp.sum(total, axis=1, keepdims=True) / width
        lean = inverse * inverse * inverse * mean
        for piece, tile, at in spots:
            columns = pl.ds(pl.multiple_of(at * LANES, LANES), LANES)
            block = hidden_ref[i, :, columns].astype(F32)
            grad = piece[:, tile * LANES : (tile + 1) * LANES].astype(F32)
            grad = inverse * (grad * small_ref[pl.ds(at, 1), :]) - lean * block
            out_ref[i, :, columns] = grad.astype(BF)


def grad_rows(hidden, small, pieces):
    return call(
        rows_kernel,
        jax.ShapeDtypeStruct(hidden.shape, BF),
        (hidden, small, *pieces),
        14 * hidden.size,
        6 * hidden.size,
    )


def write_kernel(first, pair_ref, out_ref, done):
    _, mine = indices()
    copies = [
        pltpu.make_async_copy(pair_ref.at[i], out_ref.at[mine ^ first ^ (2 * i)], done.at[i])
        for i in range(2)
    ]
    for copy in copies:
        copy.start()
    for copy in copies:
        copy.wait()


def write_rows(pair, first, target=None):
    _, rows, width = pair.shape
    hbm, vmem = pl.BlockSpec(memory_space=pltpu.HBM), pl.BlockSpec(memory_space=pltpu.VMEM)
    kernel = functools.partial(write_kernel, first)
    args, specs, aliases = (pair,), [vmem], {}
    if target is not None:
        kernel = lambda t, *refs: write_kernel(first, *refs)
        args, specs, aliases = (target, pair), [hbm, vmem], {0: 0}
    return call(
        kernel,
        jax.ShapeDtypeStruct((4, rows, width), BF),
        args,
        0,
        4 * pair.size,
        in_specs=specs,
        out_specs=hbm,
        input_output_aliases=aliases,
        scratch_shapes=[pltpu.SemaphoreType.DMA((2,))],
    )


def swap(x, axis, k=1):
    return lax.ppermute(x, axis, [(i, i ^ k) for i in range(lax.axis_size(axis))])


def onward(x, step):
    n = lax.axis_size("seq")
    return lax.ppermute(x, "seq", [(i, i + step) for i in range(n - step)])


def exchange(blocks):
    got = {k: swap(blocks[k], "seq", k) for k in reversed(range(1, len(blocks)))}
    return [got[k] for k in range(1, len(blocks))]


def after(x, *others):
    return lax.optimization_barrier((x, *others))[0]


def pairwise(
    teacher_queries, teacher_keys, teacher_values, doc_ids, owner, student_hidden, norm_gain, proj
):
    n = 4
    me, mine = indices()
    side = lax.axis_index("side")
    rows = teacher_queries.shape[0]
    heads = teacher_queries.shape[1] // HD
    kv_local = teacher_keys.shape[1] // HD
    group = heads * 2 // kv_local
    capacity, width = student_hidden.shape
    slots = capacity // n
    student = student_hidden.reshape(n, slots, width)
    tiles = width // LANES
    line = lax.broadcasted_iota(I32, (tiles + 2, LANES), 0)
    ids = jnp.where(line == tiles, owner[:, 0][None, :], doc_ids[None, :]).astype(F32)
    gain = jnp.pad(norm_gain.reshape(tiles, LANES), ((0, 2), (0, 0)))
    small = jnp.where(line < tiles, gain, ids)

    *made, hidden = norm_pieces(student, small)
    pieces = [made[0]] + exchange(made)

    head = side * heads // group
    parcel = jnp.concatenate(
        [
            lax.dynamic_slice_in_dim(teacher_keys, head * HD, HD, 1),
            lax.dynamic_slice_in_dim(teacher_values, head * HD, HD, 1),
        ]
    )
    parcels = [after(lax.optimization_barrier(parcel), made[0])]
    parcels.append(onward(parcels[0], 1))
    normed_own, drop = pick_rows([after(piece, parcels[1]) for piece in pieces], rows)

    far = swap(normed_own, "mp")
    mate = swap(normed_own, "side")
    parcels += [onward(after(parcels[0], normed_own), step) for step in (2, 3)]
    far_mate = swap(after(far, mate, *parcels[2:]), "side")
    entries = [far_mate, far, mate, normed_own]

    away = away_partial(entries, proj)
    own, over_own, normed = kept_partials([after(e, away) for e in entries], proj)
    got_over = after(swap(away, "seq", 1), over_own)
    over = lax.optimization_barrier((over_own + got_over.astype(F32)).astype(BF))
    got_far = swap(over, "seq", 2)
    got_beside = swap(beside_partial(after(normed, over), proj), "seq", 1)
    teacher_rows = attention_rows(after(teacher_queries, over), parcels, pieces)
    predicted = lax.optimization_barrier(own + got_far.astype(F32)) + got_beside.astype(F32)
    delta = (predicted - teacher_rows.astype(F32)).astype(BF)

    delta_far = swap(delta, "seq", 2)
    own_product = product(delta, proj)
    delta_beside = swap(after(delta, own_product), "seq", 1)
    delta_last = swap(delta_far, "seq", 1)
    deltas = [delta, delta_beside, delta_far, delta_last]
    products = [own_product, product(delta_beside, proj), product(delta_far, proj)]

    sent, kept = route_products(products, delta_last, proj)
    got = swap(sent, "side")
    cross = lax.optimization_barrier((kept[1].astype(F32) + got[1].astype(F32)).astype(BF))
    crossed = swap(cross, "mp")

    factor = 1.0 / math.sqrt(rows * n)
    deltas = after(jnp.concatenate([deltas[k] for k in (0, 2, 1, 3)]), cross)
    grad_proj = lax.optimization_barrier(dot(normed, deltas, ((0,), (0,))) * factor)
    crossed = after(crossed, grad_proj)
    leaving = leaving_rows(range(n), drop, kept, got, crossed)

    arrived = [leaving[0]] + exchange(leaving)
    across = [swap(block, "mp") for block in arrived]
    grad_pair = grad_rows(hidden, small, arrived + across)
    grad_mates = swap(grad_pair, "side")
    grad_hidden = write_rows(grad_mates, 1, write_rows(grad_pair, 0)).reshape(capacity, width)
    return (grad_hidden, grad_proj)


def general(
    teacher_queries, teacher_keys, teacher_values, doc_ids, owner, student_hidden, norm_gain, proj
):
    n = lax.axis_size("seq")
    me = lax.axis_index("seq")
    side = lax.axis_index("side")
    plane = lax.axis_size("mp") * lax.axis_size("side")
    mine = lax.axis_index("mp") * lax.axis_size("side") + side
    rows = teacher_queries.shape[0]
    heads = teacher_queries.shape[1] // HD
    kv_local = teacher_keys.shape[1] // HD
    group = heads * lax.axis_size("side") // kv_local
    width = student_hidden.shape[1]
    depth = proj.shape[0]
    capacity = student_hidden.shape[0]
    slots = capacity // n
    shared = n // plane
    held = shared * slots

    hidden = lax.dynamic_slice_in_dim(student_hidden, mine * held, held, 0).astype(F32)
    inverse_rms = lax.rsqrt(jnp.mean(hidden * hidden, axis=1, keepdims=True) + 1e-06)
    normed = (hidden * inverse_rms * norm_gain).astype(BF)
    normed_slots = lax.all_to_all(
        normed.reshape(held, n, depth).transpose(1, 0, 2), "seq", 0, 0, tiled=True
    )

    head = side * heads // group
    key_head = lax.dynamic_slice_in_dim(teacher_keys, head * HD, HD, 1)
    value_head = lax.dynamic_slice_in_dim(teacher_values, head * HD, HD, 1)
    small = jnp.stack([doc_ids, owner[:, 0]]).astype(BF)
    parcel = jnp.concatenate([key_head, value_head, jnp.pad(small, ((0, 14), (0, 0)))])
    parcel = lax.all_gather(parcel, "seq", axis=0, tiled=False)
    keys, values = parcel[:, :rows], parcel[:, rows : 2 * rows]
    docs = parcel[:, 2 * rows].astype(I32)
    owners = parcel[:, 2 * rows + 1].astype(I32)

    query_pos = me * rows + jnp.arange(rows, dtype=I32)
    key_pos = jnp.arange(n * rows, dtype=I32)
    allowed = (docs.reshape(-1)[None, :] == doc_ids[:, None]) & (
        key_pos[None, :] <= query_pos[:, None]
    )
    stacked = teacher_queries.reshape(rows, heads, HD).transpose(1, 0, 2)
    scores = jnp.einsum("hqd,kd->hqk", stacked, keys.reshape(-1, HD), preferred_element_type=F32)
    scores = jnp.where(allowed[None], scores * (1.0 / math.sqrt(HD)), -1e30)
    top = jnp.max(scores, axis=2, keepdims=True)
    probs = jnp.where(allowed[None], jnp.exp(scores - top), 0.0)
    totals = jnp.sum(probs, axis=2, keepdims=True)
    weighted = jnp.einsum(
        "hqk,kd->hqd", probs.astype(BF), values.reshape(-1, HD), preferred_element_type=F32
    )
    teacher_rows = (weighted / totals).astype(BF).transpose(1, 0, 2).reshape(rows, heads * HD)

    own_blocks = lax.dynamic_slice_in_dim(owners, mine * shared, shared, 0)
    order = jnp.arange(rows, dtype=I32)
    same = (own_blocks[:, :, None] == own_blocks[:, None, :]) & (order[:, None] > order[None, :])
    rank = jnp.sum(same.astype(I32), axis=2)
    spot = own_blocks * held + jnp.arange(shared, dtype=I32)[:, None] * slots + rank
    pick = (spot.reshape(-1)[:, None] == jnp.arange(n * held, dtype=I32)[None, :]).astype(BF)

    normed_own = dot(pick, normed_slots.reshape(n * held, depth)).astype(BF)
    normed_rows = lax.all_gather(normed_own, ("mp", "side"), axis=0, tiled=True)
    partial = dot(normed_rows, proj).astype(BF)
    predicted = lax.psum_scatter(partial, "seq", scatter_dimension=0, tiled=True).astype(F32)
    delta = (predicted - teacher_rows.astype(F32)).astype(BF)
    deltas = lax.all_gather(delta, "seq", axis=0, tiled=True)

    products = dot(deltas, proj, ((1,), (1,))).astype(BF)
    feature_rows = lax.psum_scatter(products, ("mp", "side"), scatter_dimension=0, tiled=True)
    feature_slots = dot(pick, feature_rows, ((0,), (0,))).astype(BF).reshape(n, held, depth)
    received = lax.all_to_all(feature_slots, "seq", 0, 0, tiled=True)
    feature_grad = received.transpose(1, 0, 2).reshape(held, width)

    gain_grad = feature_grad.astype(F32) * norm_gain
    mean_term = jnp.mean(gain_grad * hidden, axis=1, keepdims=True)
    grad_own = (inverse_rms * gain_grad - inverse_rms**3 * hidden * mean_term).astype(BF)
    grad_hidden = lax.all_gather(grad_own, ("mp", "side"), axis=0, tiled=True)

    grad_proj = dot(normed_rows, deltas, ((0,), (0,))) * (1.0 / math.sqrt(rows * n))
    return (grad_hidden, grad_proj)


def solution(mesh):
    sizes = mesh.shape
    paired = PAIRWISE and (sizes["seq"], sizes["mp"], sizes["side"]) == (4, 2, 2)
    return jax.shard_map(
        pairwise if paired else general,
        mesh=mesh,
        in_specs=(
            P(("groups", "seq"), ("mp", "side")),
            P(("groups", "seq"), "mp"),
            P(("groups", "seq"), "mp"),
            P(("groups", "seq")),
            P(("groups", "seq"), None),
            P(("groups", "seq"), None),
            P(),
            P("seq", ("mp", "side")),
        ),
        out_specs=(P(("groups", "seq"), None), P(("groups", "seq"), ("mp", "side"))),
        check_vma=False,
    )
```

```python
import functools
import math

import jax
import jax.numpy as jnp
from jax import lax
from jax.experimental import pallas as pl
from jax.experimental.pallas import tpu as pltpu
from jax.sharding import PartitionSpec as P

HD = 128
LANES = 128
BF = jnp.bfloat16
F32 = jnp.float32
I32 = jnp.int32
PARAMS = pltpu.CompilerParams(vmem_limit_bytes=16 * 1024 * 1024)
NORM_MB = 52
PAIRWISE = True


def dot(a, b, dims=((1,), (0,))):
    return lax.dot_general(a, b, (dims, ((), ())), preferred_element_type=F32)


def eye(size):
    return lax.broadcasted_iota(I32, (size, size), 0) == lax.broadcasted_iota(I32, (size, size), 1)


def to_row(column):
    return jnp.sum(jnp.where(eye(column.shape[0]), column, 0.0), axis=0, keepdims=True)


def to_column(row):
    return jnp.sum(jnp.where(eye(row.shape[1]), row, 0.0), axis=1, keepdims=True)


def indices():
    return lax.axis_index("seq"), lax.axis_index("mp") * 2 + lax.axis_index("side")


def call(kernel, shapes, args, flops, moved, transcendentals=0, **more):
    vmem = pl.BlockSpec(memory_space=pltpu.VMEM)
    options = dict(
        in_specs=[vmem] * len(args),
        out_specs=jax.tree.map(lambda s: vmem, shapes),
        compiler_params=PARAMS,
    )
    options.update(more)
    return pl.pallas_call(
        kernel,
        out_shape=shapes,
        cost_estimate=pl.CostEstimate(
            flops=flops, bytes_accessed=moved, transcendentals=transcendentals
        ),
        **options,
    )(*args)


def inverse_rms(hidden):
    width = hidden.shape[1]
    return lax.rsqrt(jnp.sum(hidden * hidden, axis=1, keepdims=True) / width + 1e-06)


def norm_kernel(student_any, small_ref, *refs):
    *pieces, hidden_ref, arrived = refs
    me, mine = indices()
    copies = [
        pltpu.make_async_copy(student_any.at[mine ^ (2 * i)], hidden_ref.at[i], arrived.at[i])
        for i in range(2)
    ]
    for copy in copies:
        copy.start()
    _, rows, width = hidden_ref.shape
    tiles = width // len(pieces) // LANES
    line = lax.broadcasted_iota(I32, (rows, LANES), 0)
    last = width // LANES
    owner_row, docs_row = small_ref[last : last + 1, :], small_ref[last + 1 : last + 2, :]
    extra = jnp.where(line == 0, owner_row, jnp.where(line == 1, docs_row, 0.0)).astype(BF)
    for piece in pieces:
        piece[:, tiles * LANES :] = extra
    copies[0].wait()
    inverse = inverse_rms(hidden_ref[0].astype(F32))
    for k, piece in enumerate(pieces):
        for tile in range(tiles):
            at = (me ^ k) * tiles + tile
            columns = pl.ds(pl.multiple_of(at * LANES, LANES), LANES)
            block = hidden_ref[0, :, columns].astype(F32)
            normed = block * inverse * small_ref[pl.ds(at, 1), :]
            piece[:, tile * LANES : (tile + 1) * LANES] = normed.astype(BF)
    copies[1].wait()


def norm_pieces(student, small):
    n, rows, width = student.shape
    piece = jax.ShapeDtypeStruct((rows, width // n + LANES), BF)
    return call(
        norm_kernel,
        [piece] * n + [jax.ShapeDtypeStruct((2, rows, width), BF)],
        (student, small),
        6 * rows * width,
        8 * rows * width,
        in_specs=[pl.BlockSpec(memory_space=pl.ANY), pl.BlockSpec(memory_space=pltpu.VMEM)],
        scratch_shapes=[pltpu.SemaphoreType.DMA((2,))],
        compiler_params=pltpu.CompilerParams(vmem_limit_bytes=NORM_MB * 1024 * 1024),
    )


def pick_kernel(*refs):
    *pieces, out_ref, drop_ref = refs
    pieces = pieces[::-1]
    me, mine = indices()
    tokens, depth = out_ref.shape
    slots = pieces[0].shape[0]
    spots = slots * len(pieces)
    owner_row = jnp.zeros((1, tokens), F32)
    for k, piece in enumerate(pieces):
        tile = piece[0:16, depth:].astype(F32)[0:1]
        owner_row = owner_row + jnp.where((me ^ mine) == k, tile, 0.0)
    owner = to_column(owner_row)
    earlier = lax.broadcasted_iota(I32, (tokens, tokens), 1) < lax.broadcasted_iota(
        I32, (tokens, tokens), 0
    )
    same = jnp.where(earlier & (owner == owner_row), 1.0, 0.0)
    rank = jnp.sum(same, axis=1, keepdims=True)
    peer = owner.astype(I32) ^ me
    spot = (peer * slots).astype(F32) + rank
    take = (lax.broadcasted_iota(I32, (tokens, spots), 1) == spot.astype(I32)).astype(F32)
    stacked = jnp.concatenate([piece[:, :depth] for piece in pieces], axis=0)
    out_ref[...] = dot(take.astype(BF), stacked).astype(BF)
    spot_row = to_row(spot).astype(I32)
    drop = (lax.broadcasted_iota(I32, (spots, tokens), 0) == spot_row).astype(F32)
    drop_ref[...] = drop.astype(BF)


def pick_rows(pieces, tokens):
    slots, wide = pieces[0].shape
    depth, spots = wide - LANES, slots * len(pieces)
    return call(
        pick_kernel,
        [jax.ShapeDtypeStruct((tokens, depth), BF), jax.ShapeDtypeStruct((spots, tokens), BF)],
        pieces[::-1],
        2 * tokens * spots * depth,
        4 * spots * depth,
    )


def attention_kernel(queries_ref, *refs):
    out_ref = refs[-1]
    n = (len(refs) - 1) // 2
    parcels, pieces = refs[:n], refs[n : 2 * n]
    tokens = queries_ref.shape[0]
    depth = pieces[0].shape[1] - LANES
    me, _ = indices()
    keys = jnp.concatenate([parcel[:tokens, :] for parcel in parcels], axis=0)
    values = jnp.concatenate([parcel[tokens:, :] for parcel in parcels], axis=0)
    docs = [piece[0:16, depth:].astype(F32)[1:2] for piece in pieces]
    doc_column = to_column(docs[0])
    query_pos = me * tokens + lax.broadcasted_iota(I32, (tokens, tokens), 0)
    within = lax.broadcasted_iota(I32, (tokens, tokens), 1)
    masks = []
    for k in range(n):
        block = (me - k + n) % n
        doc_row = sum(jnp.where((me ^ block) == i, docs[i], 0.0) for i in range(n))
        near = block * tokens + within <= query_pos
        masks.append(jnp.where(near & (doc_row == doc_column), 1.0, 0.0))
    allowed = jnp.concatenate(masks, axis=1) > 0.5
    scale_factor = 1.0 / math.sqrt(HD)
    for h in range(queries_ref.shape[1] // HD):
        columns = slice(h * HD, (h + 1) * HD)
        scores = dot(queries_ref[:, columns], keys, ((1,), (1,))) * scale_factor
        scores = jnp.where(allowed, scores, -1e30)
        top = jnp.max(scores, axis=1, keepdims=True)
        probs = jnp.where(allowed, jnp.exp(scores - top), 0.0)
        total = jnp.sum(probs, axis=1, keepdims=True)
        out_ref[:, columns] = (dot(probs.astype(BF), values) / total).astype(BF)


def attention_rows(queries, parcels, pieces):
    tokens, width = queries.shape
    return call(
        attention_kernel,
        jax.ShapeDtypeStruct((tokens, width), BF),
        (queries, *parcels, *pieces),
        0,
        4 * tokens * width,
    )


def pick_entry(refs, at):
    d, c, b, a = (ref[...] for ref in refs)
    odd = at % 2 == 1
    return jnp.where(at >= 2, jnp.where(odd, d, c), jnp.where(odd, b, a))


def away_kernel(peer, *refs):
    *entries, proj_ref, out_ref = refs
    me, mine = indices()
    block = pick_entry(entries, me ^ mine ^ peer)
    out_ref[...] = dot(block, proj_ref[...]).astype(BF)


def kept_kernel(*refs):
    *entries, proj_ref, own_ref, normed_ref = refs
    me, mine = indices()
    rows = entries[0].shape[0]
    for k, spot in enumerate((0, 2, 1, 3)):
        normed_ref[spot * rows : (spot + 1) * rows, :] = pick_entry(entries, me ^ mine ^ k)
    own_ref[...] = dot(normed_ref[:rows, :], proj_ref[...])


def away_partial(peer, entries, proj):
    rows, depth = entries[0].shape
    out = jax.ShapeDtypeStruct((rows, proj.shape[1]), BF)
    return call(functools.partial(away_kernel, peer), out, (*entries, proj), 0, 0)


def kept_partial(entries, proj):
    rows, depth = entries[0].shape
    out = jax.ShapeDtypeStruct((rows, proj.shape[1]), F32)
    shapes = [out, jax.ShapeDtypeStruct((4 * rows, depth), BF)]
    return call(kept_kernel, shapes, (*entries, proj), 0, 0)


def product_kernel(delta_ref, proj_ref, out_ref):
    out_ref[...] = dot(delta_ref[...], proj_ref[...], ((1,), (1,))).astype(BF)


def product(delta, proj):
    out = jax.ShapeDtypeStruct((delta.shape[0], proj.shape[0]), BF)
    return call(product_kernel, out, (delta, proj), 0, 0)


def route_kernel(first_ref, second_ref, third_ref, delta_ref, proj_ref, sent_ref, kept_ref, held):
    me, mine = indices()
    last = dot(delta_ref[...], proj_ref[...], ((1,), (1,))).astype(BF)
    for k, block in enumerate((first_ref[...], second_ref[...], third_ref[...], last)):
        held[k] = block
    off = me ^ mine
    kept_ref[0] = held[off]
    sent_ref[0] = held[off ^ 1]
    kept_ref[1] = held[off ^ 2]
    sent_ref[1] = held[off ^ 3]


def route_products(products, delta, proj):
    tokens, depth = products[0].shape
    pair = jax.ShapeDtypeStruct((2, tokens, depth), BF)
    return call(
        route_kernel,
        [pair, pair],
        (*products, delta, proj),
        0,
        0,
        scratch_shapes=[pltpu.VMEM((4, tokens, depth), BF)],
    )


def leave_kernel(peers, drop_ref, kept_ref, got_ref, crossed_ref, *outs):
    near = kept_ref[0].astype(F32) + got_ref[0].astype(F32)
    rows = (near + crossed_ref[...].astype(F32)).astype(BF)
    slots = outs[0].shape[0]
    for k, out in zip(peers, outs):
        out[...] = dot(drop_ref[k * slots : (k + 1) * slots, :], rows).astype(BF)


def leaving_rows(peers, drop, kept, got, crossed):
    out = jax.ShapeDtypeStruct((drop.shape[0] // 4, crossed.shape[1]), BF)
    kernel = functools.partial(leave_kernel, peers)
    return call(kernel, [out] * len(peers), (drop, kept, got, crossed), 0, 0)


def rows_kernel(hidden_ref, small_ref, *refs):
    *pieces, out_ref = refs
    me, _ = indices()
    blocks, rows, width = hidden_ref.shape
    n = len(pieces) // blocks
    tiles = width // n // LANES
    for i in range(blocks):
        inverse = inverse_rms(hidden_ref[i].astype(F32))
        spots = [
            (piece, tile, (me ^ k) * tiles + tile)
            for k, piece in enumerate(pieces[i * n : (i + 1) * n])
            for tile in range(tiles)
        ]
        total = jnp.zeros((rows, LANES), F32)
        for piece, tile, at in spots:
            columns = pl.ds(pl.multiple_of(at * LANES, LANES), LANES)
            block = hidden_ref[i, :, columns].astype(F32)
            grad = piece[:, tile * LANES : (tile + 1) * LANES].astype(F32)
            total = total + grad * small_ref[pl.ds(at, 1), :] * block
        mean = jnp.sum(total, axis=1, keepdims=True) / width
        lean = inverse * inverse * inverse * mean
        for piece, tile, at in spots:
            columns = pl.ds(pl.multiple_of(at * LANES, LANES), LANES)
            block = hidden_ref[i, :, columns].astype(F32)
            grad = piece[:, tile * LANES : (tile + 1) * LANES].astype(F32)
            grad = inverse * (grad * small_ref[pl.ds(at, 1), :]) - lean * block
            out_ref[i, :, columns] = grad.astype(BF)


def grad_rows(hidden, small, pieces):
    return call(
        rows_kernel,
        jax.ShapeDtypeStruct(hidden.shape, BF),
        (hidden, small, *pieces),
        14 * hidden.size,
        6 * hidden.size,
    )


def write_kernel(first, pair_ref, out_ref, done):
    _, mine = indices()
    copies = [
        pltpu.make_async_copy(pair_ref.at[i], out_ref.at[mine ^ first ^ (2 * i)], done.at[i])
        for i in range(2)
    ]
    for copy in copies:
        copy.start()
    for copy in copies:
        copy.wait()


def write_rows(pair, first, target=None):
    _, rows, width = pair.shape
    hbm, vmem = pl.BlockSpec(memory_space=pltpu.HBM), pl.BlockSpec(memory_space=pltpu.VMEM)
    kernel = functools.partial(write_kernel, first)
    args, specs, aliases = (pair,), [vmem], {}
    if target is not None:
        kernel = lambda t, *refs: write_kernel(first, *refs)
        args, specs, aliases = (target, pair), [hbm, vmem], {0: 0}
    return call(
        kernel,
        jax.ShapeDtypeStruct((4, rows, width), BF),
        args,
        0,
        4 * pair.size,
        in_specs=specs,
        out_specs=hbm,
        input_output_aliases=aliases,
        scratch_shapes=[pltpu.SemaphoreType.DMA((2,))],
    )


def swap(x, axis, k=1):
    return lax.ppermute(x, axis, [(i, i ^ k) for i in range(lax.axis_size(axis))])


def onward(x):
    return lax.ppermute(x, "seq", [(i, i + 1) for i in range(lax.axis_size("seq") - 1)])


def exchange(blocks):
    got = {k: swap(blocks[k], "seq", k) for k in reversed(range(1, len(blocks)))}
    return [got[k] for k in range(1, len(blocks))]


def after(x, *others):
    return lax.optimization_barrier((x, *others))[0]


def pairwise(
    teacher_queries, teacher_keys, teacher_values, doc_ids, owner, student_hidden, norm_gain, proj
):
    n = 4
    me, mine = indices()
    side = lax.axis_index("side")
    rows = teacher_queries.shape[0]
    heads = teacher_queries.shape[1] // HD
    kv_local = teacher_keys.shape[1] // HD
    group = heads * 2 // kv_local
    capacity, width = student_hidden.shape
    slots = capacity // n
    student = student_hidden.reshape(n, slots, width)
    tiles = width // LANES
    line = lax.broadcasted_iota(I32, (tiles + 2, LANES), 0)
    ids = jnp.where(line == tiles, owner[:, 0][None, :], doc_ids[None, :]).astype(F32)
    gain = jnp.pad(norm_gain.reshape(tiles, LANES), ((0, 2), (0, 0)))
    small = jnp.where(line < tiles, gain, ids)

    *made, hidden = norm_pieces(student, small)
    pieces = [made[0]] + exchange(made)

    head = side * heads // group
    parcel = jnp.concatenate(
        [
            lax.dynamic_slice_in_dim(teacher_keys, head * HD, HD, 1),
            lax.dynamic_slice_in_dim(teacher_values, head * HD, HD, 1),
        ]
    )
    parcels = [after(lax.optimization_barrier(parcel), made[0])]
    parcels.append(onward(parcels[0]))
    normed_own, drop = pick_rows([after(piece, parcels[1]) for piece in pieces], rows)

    far = swap(normed_own, "mp")
    mate = swap(normed_own, "side")
    parcels.append(onward(after(parcels[1], normed_own)))
    far_mate = swap(after(far, mate, parcels[2]), "side")
    entries = [far_mate, far, mate, normed_own]

    got, last = [], []
    for k in (3, 2, 1):
        partial = away_partial(k, [after(e, *last) for e in entries], proj)
        last = [partial]
        got.append(swap(partial, "seq", k).astype(F32))
    own, normed = kept_partial([after(e, *last) for e in entries], proj)
    parcels.append(onward(after(parcels[2], own)))
    teacher_rows = attention_rows(after(teacher_queries, own), parcels, pieces)
    predicted = lax.optimization_barrier(own + got[0])
    predicted = lax.optimization_barrier(predicted + got[1]) + got[2]
    delta = (predicted - teacher_rows.astype(F32)).astype(BF)

    delta_far = swap(delta, "seq", 2)
    own_product = product(delta, proj)
    delta_beside = swap(after(delta, own_product), "seq", 1)
    delta_last = swap(delta_far, "seq", 1)
    deltas = [delta, delta_beside, delta_far, delta_last]
    products = [own_product, product(delta_beside, proj), product(delta_far, proj)]

    sent, kept = route_products(products, delta_last, proj)
    got = swap(sent, "side")
    cross = lax.optimization_barrier((kept[1].astype(F32) + got[1].astype(F32)).astype(BF))
    crossed = swap(cross, "mp")

    factor = 1.0 / math.sqrt(rows * n)
    deltas = after(jnp.concatenate([deltas[k] for k in (0, 2, 1, 3)]), cross)
    grad_proj = lax.optimization_barrier(dot(normed, deltas, ((0,), (0,))) * factor)
    crossed = after(crossed, grad_proj)
    leaving = leaving_rows(range(n), drop, kept, got, crossed)

    arrived = [leaving[0]] + exchange(leaving)
    across = [swap(block, "mp") for block in arrived]
    grad_pair = grad_rows(hidden, small, arrived + across)
    grad_mates = swap(grad_pair, "side")
    grad_hidden = write_rows(grad_mates, 1, write_rows(grad_pair, 0)).reshape(capacity, width)
    return (grad_hidden, grad_proj)


def general(
    teacher_queries, teacher_keys, teacher_values, doc_ids, owner, student_hidden, norm_gain, proj
):
    n = lax.axis_size("seq")
    me = lax.axis_index("seq")
    side = lax.axis_index("side")
    plane = lax.axis_size("mp") * lax.axis_size("side")
    mine = lax.axis_index("mp") * lax.axis_size("side") + side
    rows = teacher_queries.shape[0]
    heads = teacher_queries.shape[1] // HD
    kv_local = teacher_keys.shape[1] // HD
    group = heads * lax.axis_size("side") // kv_local
    width = student_hidden.shape[1]
    depth = proj.shape[0]
    capacity = student_hidden.shape[0]
    slots = capacity // n
    shared = n // plane
    held = shared * slots

    hidden = lax.dynamic_slice_in_dim(student_hidden, mine * held, held, 0).astype(F32)
    inverse_rms = lax.rsqrt(jnp.mean(hidden * hidden, axis=1, keepdims=True) + 1e-06)
    normed = (hidden * inverse_rms * norm_gain).astype(BF)
    normed_slots = lax.all_to_all(
        normed.reshape(held, n, depth).transpose(1, 0, 2), "seq", 0, 0, tiled=True
    )

    head = side * heads // group
    key_head = lax.dynamic_slice_in_dim(teacher_keys, head * HD, HD, 1)
    value_head = lax.dynamic_slice_in_dim(teacher_values, head * HD, HD, 1)
    small = jnp.stack([doc_ids, owner[:, 0]]).astype(BF)
    parcel = jnp.concatenate([key_head, value_head, jnp.pad(small, ((0, 14), (0, 0)))])
    parcel = lax.all_gather(parcel, "seq", axis=0, tiled=False)
    keys, values = parcel[:, :rows], parcel[:, rows : 2 * rows]
    docs = parcel[:, 2 * rows].astype(I32)
    owners = parcel[:, 2 * rows + 1].astype(I32)

    query_pos = me * rows + jnp.arange(rows, dtype=I32)
    key_pos = jnp.arange(n * rows, dtype=I32)
    allowed = (docs.reshape(-1)[None, :] == doc_ids[:, None]) & (
        key_pos[None, :] <= query_pos[:, None]
    )
    stacked = teacher_queries.reshape(rows, heads, HD).transpose(1, 0, 2)
    scores = jnp.einsum("hqd,kd->hqk", stacked, keys.reshape(-1, HD), preferred_element_type=F32)
    scores = jnp.where(allowed[None], scores * (1.0 / math.sqrt(HD)), -1e30)
    top = jnp.max(scores, axis=2, keepdims=True)
    probs = jnp.where(allowed[None], jnp.exp(scores - top), 0.0)
    totals = jnp.sum(probs, axis=2, keepdims=True)
    weighted = jnp.einsum(
        "hqk,kd->hqd", probs.astype(BF), values.reshape(-1, HD), preferred_element_type=F32
    )
    teacher_rows = (weighted / totals).astype(BF).transpose(1, 0, 2).reshape(rows, heads * HD)

    own_blocks = lax.dynamic_slice_in_dim(owners, mine * shared, shared, 0)
    order = jnp.arange(rows, dtype=I32)
    same = (own_blocks[:, :, None] == own_blocks[:, None, :]) & (order[:, None] > order[None, :])
    rank = jnp.sum(same.astype(I32), axis=2)
    spot = own_blocks * held + jnp.arange(shared, dtype=I32)[:, None] * slots + rank
    pick = (spot.reshape(-1)[:, None] == jnp.arange(n * held, dtype=I32)[None, :]).astype(BF)

    normed_own = dot(pick, normed_slots.reshape(n * held, depth)).astype(BF)
    normed_rows = lax.all_gather(normed_own, ("mp", "side"), axis=0, tiled=True)
    partial = dot(normed_rows, proj).astype(BF)
    predicted = lax.psum_scatter(partial, "seq", scatter_dimension=0, tiled=True).astype(F32)
    delta = (predicted - teacher_rows.astype(F32)).astype(BF)
    deltas = lax.all_gather(delta, "seq", axis=0, tiled=True)

    products = dot(deltas, proj, ((1,), (1,))).astype(BF)
    feature_rows = lax.psum_scatter(products, ("mp", "side"), scatter_dimension=0, tiled=True)
    feature_slots = dot(pick, feature_rows, ((0,), (0,))).astype(BF).reshape(n, held, depth)
    received = lax.all_to_all(feature_slots, "seq", 0, 0, tiled=True)
    feature_grad = received.transpose(1, 0, 2).reshape(held, width)

    gain_grad = feature_grad.astype(F32) * norm_gain
    mean_term = jnp.mean(gain_grad * hidden, axis=1, keepdims=True)
    grad_own = (inverse_rms * gain_grad - inverse_rms**3 * hidden * mean_term).astype(BF)
    grad_hidden = lax.all_gather(grad_own, ("mp", "side"), axis=0, tiled=True)

    grad_proj = dot(normed_rows, deltas, ((0,), (0,))) * (1.0 / math.sqrt(rows * n))
    return (grad_hidden, grad_proj)


def solution(mesh):
    sizes = mesh.shape
    paired = PAIRWISE and (sizes["seq"], sizes["mp"], sizes["side"]) == (4, 2, 2)
    return jax.shard_map(
        pairwise if paired else general,
        mesh=mesh,
        in_specs=(
            P(("groups", "seq"), ("mp", "side")),
            P(("groups", "seq"), "mp"),
            P(("groups", "seq"), "mp"),
            P(("groups", "seq")),
            P(("groups", "seq"), None),
            P(("groups", "seq"), None),
            P(),
            P("seq", ("mp", "side")),
        ),
        out_specs=(P(("groups", "seq"), None), P(("groups", "seq"), ("mp", "side"))),
        check_vma=False,
    )
```

```python
import functools
import math

import jax
import jax.numpy as jnp
from jax import lax
from jax.experimental import pallas as pl
from jax.experimental.pallas import tpu as pltpu
from jax.sharding import PartitionSpec as P

HD = 128
LANES = 128
BF = jnp.bfloat16
F32 = jnp.float32
I32 = jnp.int32
PARAMS = pltpu.CompilerParams(vmem_limit_bytes=16 * 1024 * 1024)
NORM_MB = 52
PAIRWISE = True


def dot(a, b, dims=((1,), (0,))):
    return lax.dot_general(a, b, (dims, ((), ())), preferred_element_type=F32)


def eye(size):
    return lax.broadcasted_iota(I32, (size, size), 0) == lax.broadcasted_iota(I32, (size, size), 1)


def to_row(column):
    return jnp.sum(jnp.where(eye(column.shape[0]), column, 0.0), axis=0, keepdims=True)


def to_column(row):
    return jnp.sum(jnp.where(eye(row.shape[1]), row, 0.0), axis=1, keepdims=True)


def indices():
    return lax.axis_index("seq"), lax.axis_index("mp") * 2 + lax.axis_index("side")


def call(kernel, shapes, args, flops, moved, transcendentals=0, **more):
    vmem = pl.BlockSpec(memory_space=pltpu.VMEM)
    options = dict(
        in_specs=[vmem] * len(args),
        out_specs=jax.tree.map(lambda s: vmem, shapes),
        compiler_params=PARAMS,
    )
    options.update(more)
    return pl.pallas_call(
        kernel,
        out_shape=shapes,
        cost_estimate=pl.CostEstimate(
            flops=flops, bytes_accessed=moved, transcendentals=transcendentals
        ),
        **options,
    )(*args)


def inverse_rms(hidden):
    width = hidden.shape[1]
    return lax.rsqrt(jnp.sum(hidden * hidden, axis=1, keepdims=True) / width + 1e-06)


def norm_kernel(student_any, small_ref, *refs):
    *pieces, hidden_ref, arrived = refs
    me, mine = indices()
    copies = [
        pltpu.make_async_copy(student_any.at[mine ^ (2 * i)], hidden_ref.at[i], arrived.at[i])
        for i in range(2)
    ]
    for copy in copies:
        copy.start()
    _, rows, width = hidden_ref.shape
    tiles = width // len(pieces) // LANES
    line = lax.broadcasted_iota(I32, (rows, LANES), 0)
    last = width // LANES
    owner_row, docs_row = small_ref[last : last + 1, :], small_ref[last + 1 : last + 2, :]
    extra = jnp.where(line == 0, owner_row, jnp.where(line == 1, docs_row, 0.0)).astype(BF)
    for piece in pieces:
        piece[:, tiles * LANES :] = extra
    copies[0].wait()
    inverse = inverse_rms(hidden_ref[0].astype(F32))
    for k, piece in enumerate(pieces):
        for tile in range(tiles):
            at = (me ^ k) * tiles + tile
            columns = pl.ds(pl.multiple_of(at * LANES, LANES), LANES)
            block = hidden_ref[0, :, columns].astype(F32)
            normed = block * inverse * small_ref[pl.ds(at, 1), :]
            piece[:, tile * LANES : (tile + 1) * LANES] = normed.astype(BF)
    copies[1].wait()


def norm_pieces(student, small):
    n, rows, width = student.shape
    piece = jax.ShapeDtypeStruct((rows, width // n + LANES), BF)
    return call(
        norm_kernel,
        [piece] * n + [jax.ShapeDtypeStruct((2, rows, width), BF)],
        (student, small),
        6 * rows * width,
        8 * rows * width,
        in_specs=[pl.BlockSpec(memory_space=pl.ANY), pl.BlockSpec(memory_space=pltpu.VMEM)],
        scratch_shapes=[pltpu.SemaphoreType.DMA((2,))],
        compiler_params=pltpu.CompilerParams(vmem_limit_bytes=NORM_MB * 1024 * 1024),
    )


def pick_kernel(*refs):
    *pieces, out_ref, drop_ref = refs
    pieces = pieces[::-1]
    me, mine = indices()
    tokens, depth = out_ref.shape
    slots = pieces[0].shape[0]
    spots = slots * len(pieces)
    owner_row = jnp.zeros((1, tokens), F32)
    for k, piece in enumerate(pieces):
        tile = piece[0:16, depth:].astype(F32)[0:1]
        owner_row = owner_row + jnp.where((me ^ mine) == k, tile, 0.0)
    owner = to_column(owner_row)
    earlier = lax.broadcasted_iota(I32, (tokens, tokens), 1) < lax.broadcasted_iota(
        I32, (tokens, tokens), 0
    )
    same = jnp.where(earlier & (owner == owner_row), 1.0, 0.0)
    rank = jnp.sum(same, axis=1, keepdims=True)
    peer = owner.astype(I32) ^ me
    spot = (peer * slots).astype(F32) + rank
    take = (lax.broadcasted_iota(I32, (tokens, spots), 1) == spot.astype(I32)).astype(F32)
    stacked = jnp.concatenate([piece[:, :depth] for piece in pieces], axis=0)
    out_ref[...] = dot(take.astype(BF), stacked).astype(BF)
    spot_row = to_row(spot).astype(I32)
    drop = (lax.broadcasted_iota(I32, (spots, tokens), 0) == spot_row).astype(F32)
    drop_ref[...] = drop.astype(BF)


def pick_rows(pieces, tokens):
    slots, wide = pieces[0].shape
    depth, spots = wide - LANES, slots * len(pieces)
    return call(
        pick_kernel,
        [jax.ShapeDtypeStruct((tokens, depth), BF), jax.ShapeDtypeStruct((spots, tokens), BF)],
        pieces[::-1],
        2 * tokens * spots * depth,
        4 * spots * depth,
    )


def attention_kernel(queries_ref, *refs):
    out_ref = refs[-1]
    n = (len(refs) - 1) // 2
    parcels, pieces = refs[:n], refs[n : 2 * n]
    tokens = queries_ref.shape[0]
    depth = pieces[0].shape[1] - LANES
    me, _ = indices()
    keys = jnp.concatenate([parcel[:tokens, :] for parcel in parcels], axis=0)
    values = jnp.concatenate([parcel[tokens:, :] for parcel in parcels], axis=0)
    docs = [piece[0:16, depth:].astype(F32)[1:2] for piece in pieces]
    doc_column = to_column(docs[0])
    query_pos = me * tokens + lax.broadcasted_iota(I32, (tokens, tokens), 0)
    within = lax.broadcasted_iota(I32, (tokens, tokens), 1)
    masks = []
    for k in range(n):
        block = (me - k + n) % n
        doc_row = sum(jnp.where((me ^ block) == i, docs[i], 0.0) for i in range(n))
        near = block * tokens + within <= query_pos
        masks.append(jnp.where(near & (doc_row == doc_column), 1.0, 0.0))
    allowed = jnp.concatenate(masks, axis=1) > 0.5
    scale_factor = 1.0 / math.sqrt(HD)
    for h in range(queries_ref.shape[1] // HD):
        columns = slice(h * HD, (h + 1) * HD)
        scores = dot(queries_ref[:, columns], keys, ((1,), (1,))) * scale_factor
        scores = jnp.where(allowed, scores, -1e30)
        top = jnp.max(scores, axis=1, keepdims=True)
        probs = jnp.where(allowed, jnp.exp(scores - top), 0.0)
        total = jnp.sum(probs, axis=1, keepdims=True)
        out_ref[:, columns] = (dot(probs.astype(BF), values) / total).astype(BF)


def attention_rows(queries, parcels, pieces):
    tokens, width = queries.shape
    return call(
        attention_kernel,
        jax.ShapeDtypeStruct((tokens, width), BF),
        (queries, *parcels, *pieces),
        0,
        4 * tokens * width,
    )


def pick_entry(refs, at):
    d, c, b, a = (ref[...] for ref in refs)
    odd = at % 2 == 1
    return jnp.where(at >= 2, jnp.where(odd, d, c), jnp.where(odd, b, a))


def away_kernel(*refs):
    *entries, proj_ref, out_ref = refs
    me, mine = indices()
    block = pick_entry(entries, me ^ mine ^ 3)
    out_ref[...] = dot(block, proj_ref[...]).astype(BF)


def kept_kernel(*refs):
    *entries, proj_ref, own_ref, over_ref, normed_ref = refs
    me, mine = indices()
    rows = entries[0].shape[0]
    for k, spot in enumerate((0, 2, 1, 3)):
        normed_ref[spot * rows : (spot + 1) * rows, :] = pick_entry(entries, me ^ mine ^ k)
    columns = 256
    for first in range(0, proj_ref.shape[1], columns):
        part = slice(first, first + columns)
        product = dot(normed_ref[: 2 * rows, :], proj_ref[:, part])
        own_ref[:, part] = product[:rows]
        over_ref[:, part] = product[rows:]


def beside_kernel(normed_ref, proj_ref, out_ref):
    rows = out_ref.shape[0]
    out_ref[...] = dot(normed_ref[2 * rows : 3 * rows, :], proj_ref[...]).astype(BF)


def away_partial(entries, proj):
    rows, depth = entries[0].shape
    out = jax.ShapeDtypeStruct((rows, proj.shape[1]), BF)
    return call(away_kernel, out, (*entries, proj), 0, 0)


def kept_partials(entries, proj):
    rows, depth = entries[0].shape
    out = jax.ShapeDtypeStruct((rows, proj.shape[1]), F32)
    shapes = [out, out, jax.ShapeDtypeStruct((4 * rows, depth), BF)]
    return call(kept_kernel, shapes, (*entries, proj), 0, 0)


def beside_partial(normed, proj):
    out = jax.ShapeDtypeStruct((normed.shape[0] // 4, proj.shape[1]), BF)
    return call(beside_kernel, out, (normed, proj), 0, 0)


def product_kernel(delta_ref, proj_ref, out_ref):
    out_ref[...] = dot(delta_ref[...], proj_ref[...], ((1,), (1,))).astype(BF)


def product(delta, proj):
    out = jax.ShapeDtypeStruct((delta.shape[0], proj.shape[0]), BF)
    return call(product_kernel, out, (delta, proj), 0, 0)


def route_kernel(first_ref, second_ref, third_ref, delta_ref, proj_ref, sent_ref, kept_ref, held):
    me, mine = indices()
    last = dot(delta_ref[...], proj_ref[...], ((1,), (1,))).astype(BF)
    for k, block in enumerate((first_ref[...], second_ref[...], third_ref[...], last)):
        held[k] = block
    off = me ^ mine
    kept_ref[0] = held[off]
    sent_ref[0] = held[off ^ 1]
    kept_ref[1] = held[off ^ 2]
    sent_ref[1] = held[off ^ 3]


def route_products(products, delta, proj):
    tokens, depth = products[0].shape
    pair = jax.ShapeDtypeStruct((2, tokens, depth), BF)
    return call(
        route_kernel,
        [pair, pair],
        (*products, delta, proj),
        0,
        0,
        scratch_shapes=[pltpu.VMEM((4, tokens, depth), BF)],
    )


def leave_kernel(peers, drop_ref, kept_ref, got_ref, crossed_ref, *outs):
    near = kept_ref[0].astype(F32) + got_ref[0].astype(F32)
    rows = (near + crossed_ref[...].astype(F32)).astype(BF)
    slots = outs[0].shape[0]
    for k, out in zip(peers, outs):
        out[...] = dot(drop_ref[k * slots : (k + 1) * slots, :], rows).astype(BF)


def leaving_rows(peers, drop, kept, got, crossed):
    out = jax.ShapeDtypeStruct((drop.shape[0] // 4, crossed.shape[1]), BF)
    kernel = functools.partial(leave_kernel, peers)
    return call(kernel, [out] * len(peers), (drop, kept, got, crossed), 0, 0)


def rows_kernel(which, hidden_ref, small_ref, *refs):
    *pieces, out_ref = refs
    me, _ = indices()
    _, rows, width = hidden_ref.shape
    tiles = width // len(pieces) // LANES
    inverse = inverse_rms(hidden_ref[which].astype(F32))
    spots = [
        (piece, tile, (me ^ k) * tiles + tile)
        for k, piece in enumerate(pieces)
        for tile in range(tiles)
    ]
    total = jnp.zeros((rows, LANES), F32)
    for piece, tile, at in spots:
        columns = pl.ds(pl.multiple_of(at * LANES, LANES), LANES)
        block = hidden_ref[which, :, columns].astype(F32)
        grad = piece[:, tile * LANES : (tile + 1) * LANES].astype(F32)
        total = total + grad * small_ref[pl.ds(at, 1), :] * block
    mean = jnp.sum(total, axis=1, keepdims=True) / width
    lean = inverse * inverse * inverse * mean
    for piece, tile, at in spots:
        columns = pl.ds(pl.multiple_of(at * LANES, LANES), LANES)
        block = hidden_ref[which, :, columns].astype(F32)
        grad = piece[:, tile * LANES : (tile + 1) * LANES].astype(F32)
        grad = inverse * (grad * small_ref[pl.ds(at, 1), :]) - lean * block
        out_ref[:, columns] = grad.astype(BF)


def grad_rows(which, hidden, small, pieces):
    out = jax.ShapeDtypeStruct(hidden.shape[1:], BF)
    return call(functools.partial(rows_kernel, which), out, (hidden, small, *pieces), 0, 0)


def write_kernel(places, *refs):
    *blocks, out_ref, done = refs
    _, mine = indices()
    copies = [
        pltpu.make_async_copy(block, out_ref.at[mine ^ place], done.at[i])
        for i, (block, place) in enumerate(zip(blocks, places))
    ]
    for copy in copies:
        copy.start()
    for copy in copies:
        copy.wait()


def write_rows(blocks, places, target=None):
    rows, width = blocks[0].shape
    hbm, vmem = pl.BlockSpec(memory_space=pltpu.HBM), pl.BlockSpec(memory_space=pltpu.VMEM)
    kernel = functools.partial(write_kernel, places)
    args, specs, aliases = tuple(blocks), [vmem] * len(blocks), {}
    if target is not None:
        kernel = lambda t, *refs: write_kernel(places, *refs)
        args, specs, aliases = (target, *args), [hbm] + specs, {0: 0}
    return call(
        kernel,
        jax.ShapeDtypeStruct((4, rows, width), BF),
        args,
        0,
        4 * len(blocks) * rows * width,
        in_specs=specs,
        out_specs=hbm,
        input_output_aliases=aliases,
        scratch_shapes=[pltpu.SemaphoreType.DMA((len(blocks),))],
    )


def swap(x, axis, k=1):
    return lax.ppermute(x, axis, [(i, i ^ k) for i in range(lax.axis_size(axis))])


def onward(x):
    return lax.ppermute(x, "seq", [(i, i + 1) for i in range(lax.axis_size("seq") - 1)])


def exchange(blocks):
    got = {k: swap(blocks[k], "seq", k) for k in reversed(range(1, len(blocks)))}
    return [got[k] for k in range(1, len(blocks))]


def after(x, *others):
    return lax.optimization_barrier((x, *others))[0]


def pairwise(
    teacher_queries, teacher_keys, teacher_values, doc_ids, owner, student_hidden, norm_gain, proj
):
    n = 4
    me, mine = indices()
    side = lax.axis_index("side")
    rows = teacher_queries.shape[0]
    heads = teacher_queries.shape[1] // HD
    kv_local = teacher_keys.shape[1] // HD
    group = heads * 2 // kv_local
    capacity, width = student_hidden.shape
    slots = capacity // n
    student = student_hidden.reshape(n, slots, width)
    tiles = width // LANES
    line = lax.broadcasted_iota(I32, (tiles + 2, LANES), 0)
    ids = jnp.where(line == tiles, owner[:, 0][None, :], doc_ids[None, :]).astype(F32)
    gain = jnp.pad(norm_gain.reshape(tiles, LANES), ((0, 2), (0, 0)))
    small = jnp.where(line < tiles, gain, ids)

    *made, hidden = norm_pieces(student, small)
    pieces = [made[0]] + exchange(made)

    head = side * heads // group
    parcel = jnp.concatenate(
        [
            lax.dynamic_slice_in_dim(teacher_keys, head * HD, HD, 1),
            lax.dynamic_slice_in_dim(teacher_values, head * HD, HD, 1),
        ]
    )
    parcels = [after(lax.optimization_barrier(parcel), made[0])]
    parcels.append(onward(parcels[0]))
    normed_own, drop = pick_rows([after(piece, parcels[1]) for piece in pieces], rows)

    far = swap(normed_own, "mp")
    mate = swap(normed_own, "side")
    parcels.append(onward(after(parcels[1], normed_own)))
    far_mate = swap(after(far, mate, parcels[2]), "side")
    entries = [far_mate, far, mate, normed_own]

    away = away_partial(entries, proj)
    own, over_own, normed = kept_partials([after(e, away) for e in entries], proj)
    parcels.append(onward(after(parcels[2], away)))
    got_over = after(swap(away, "seq", 1), over_own, parcels[3])
    over = lax.optimization_barrier((over_own + got_over.astype(F32)).astype(BF))
    got_far = swap(over, "seq", 2)
    got_beside = swap(beside_partial(after(normed, over), proj), "seq", 1)
    teacher_rows = attention_rows(after(teacher_queries, over), parcels, pieces)
    predicted = lax.optimization_barrier(own + got_far.astype(F32)) + got_beside.astype(F32)
    delta = (predicted - teacher_rows.astype(F32)).astype(BF)

    delta_far = swap(delta, "seq", 2)
    own_product = product(delta, proj)
    delta_beside = swap(after(delta, own_product), "seq", 1)
    delta_last = swap(delta_far, "seq", 1)
    deltas = [delta, delta_beside, delta_far, delta_last]
    products = [own_product, product(delta_beside, proj), product(delta_far, proj)]

    sent, kept = route_products(products, delta_last, proj)
    got = swap(sent, "side")
    cross = lax.optimization_barrier((kept[1].astype(F32) + got[1].astype(F32)).astype(BF))
    crossed = swap(cross, "mp")

    factor = 1.0 / math.sqrt(rows * n)
    deltas = after(jnp.concatenate([deltas[k] for k in (0, 2, 1, 3)]), cross)
    grad_proj = lax.optimization_barrier(dot(normed, deltas, ((0,), (0,))) * factor)
    crossed = after(crossed, grad_proj)
    leaving = leaving_rows(range(n), drop, kept, got, crossed)

    arrived = [leaving[0]] + exchange(leaving)
    across = [swap(block, "mp") for block in arrived]
    own_ready = [after(block, leaving[0]) for block in arrived]
    grad_own = grad_rows(0, hidden, small, own_ready)
    grad_mate = swap(grad_own, "side")
    grad_far = grad_rows(1, hidden, small, across)
    grad_last = swap(grad_far, "side")
    grad_hidden = write_rows([grad_own, grad_mate, grad_far], (0, 1, 2))
    grad_hidden = write_rows([grad_last], (3,), grad_hidden).reshape(capacity, width)
    return (grad_hidden, grad_proj)


def general(
    teacher_queries, teacher_keys, teacher_values, doc_ids, owner, student_hidden, norm_gain, proj
):
    n = lax.axis_size("seq")
    me = lax.axis_index("seq")
    side = lax.axis_index("side")
    plane = lax.axis_size("mp") * lax.axis_size("side")
    mine = lax.axis_index("mp") * lax.axis_size("side") + side
    rows = teacher_queries.shape[0]
    heads = teacher_queries.shape[1] // HD
    kv_local = teacher_keys.shape[1] // HD
    group = heads * lax.axis_size("side") // kv_local
    width = student_hidden.shape[1]
    depth = proj.shape[0]
    capacity = student_hidden.shape[0]
    slots = capacity // n
    shared = n // plane
    held = shared * slots

    hidden = lax.dynamic_slice_in_dim(student_hidden, mine * held, held, 0).astype(F32)
    inverse_rms = lax.rsqrt(jnp.mean(hidden * hidden, axis=1, keepdims=True) + 1e-06)
    normed = (hidden * inverse_rms * norm_gain).astype(BF)
    normed_slots = lax.all_to_all(
        normed.reshape(held, n, depth).transpose(1, 0, 2), "seq", 0, 0, tiled=True
    )

    head = side * heads // group
    key_head = lax.dynamic_slice_in_dim(teacher_keys, head * HD, HD, 1)
    value_head = lax.dynamic_slice_in_dim(teacher_values, head * HD, HD, 1)
    small = jnp.stack([doc_ids, owner[:, 0]]).astype(BF)
    parcel = jnp.concatenate([key_head, value_head, jnp.pad(small, ((0, 14), (0, 0)))])
    parcel = lax.all_gather(parcel, "seq", axis=0, tiled=False)
    keys, values = parcel[:, :rows], parcel[:, rows : 2 * rows]
    docs = parcel[:, 2 * rows].astype(I32)
    owners = parcel[:, 2 * rows + 1].astype(I32)

    query_pos = me * rows + jnp.arange(rows, dtype=I32)
    key_pos = jnp.arange(n * rows, dtype=I32)
    allowed = (docs.reshape(-1)[None, :] == doc_ids[:, None]) & (
        key_pos[None, :] <= query_pos[:, None]
    )
    stacked = teacher_queries.reshape(rows, heads, HD).transpose(1, 0, 2)
    scores = jnp.einsum("hqd,kd->hqk", stacked, keys.reshape(-1, HD), preferred_element_type=F32)
    scores = jnp.where(allowed[None], scores * (1.0 / math.sqrt(HD)), -1e30)
    top = jnp.max(scores, axis=2, keepdims=True)
    probs = jnp.where(allowed[None], jnp.exp(scores - top), 0.0)
    totals = jnp.sum(probs, axis=2, keepdims=True)
    weighted = jnp.einsum(
        "hqk,kd->hqd", probs.astype(BF), values.reshape(-1, HD), preferred_element_type=F32
    )
    teacher_rows = (weighted / totals).astype(BF).transpose(1, 0, 2).reshape(rows, heads * HD)

    own_blocks = lax.dynamic_slice_in_dim(owners, mine * shared, shared, 0)
    order = jnp.arange(rows, dtype=I32)
    same = (own_blocks[:, :, None] == own_blocks[:, None, :]) & (order[:, None] > order[None, :])
    rank = jnp.sum(same.astype(I32), axis=2)
    spot = own_blocks * held + jnp.arange(shared, dtype=I32)[:, None] * slots + rank
    pick = (spot.reshape(-1)[:, None] == jnp.arange(n * held, dtype=I32)[None, :]).astype(BF)

    normed_own = dot(pick, normed_slots.reshape(n * held, depth)).astype(BF)
    normed_rows = lax.all_gather(normed_own, ("mp", "side"), axis=0, tiled=True)
    partial = dot(normed_rows, proj).astype(BF)
    predicted = lax.psum_scatter(partial, "seq", scatter_dimension=0, tiled=True).astype(F32)
    delta = (predicted - teacher_rows.astype(F32)).astype(BF)
    deltas = lax.all_gather(delta, "seq", axis=0, tiled=True)

    products = dot(deltas, proj, ((1,), (1,))).astype(BF)
    feature_rows = lax.psum_scatter(products, ("mp", "side"), scatter_dimension=0, tiled=True)
    feature_slots = dot(pick, feature_rows, ((0,), (0,))).astype(BF).reshape(n, held, depth)
    received = lax.all_to_all(feature_slots, "seq", 0, 0, tiled=True)
    feature_grad = received.transpose(1, 0, 2).reshape(held, width)

    gain_grad = feature_grad.astype(F32) * norm_gain
    mean_term = jnp.mean(gain_grad * hidden, axis=1, keepdims=True)
    grad_own = (inverse_rms * gain_grad - inverse_rms**3 * hidden * mean_term).astype(BF)
    grad_hidden = lax.all_gather(grad_own, ("mp", "side"), axis=0, tiled=True)

    grad_proj = dot(normed_rows, deltas, ((0,), (0,))) * (1.0 / math.sqrt(rows * n))
    return (grad_hidden, grad_proj)


def solution(mesh):
    sizes = mesh.shape
    paired = PAIRWISE and (sizes["seq"], sizes["mp"], sizes["side"]) == (4, 2, 2)
    return jax.shard_map(
        pairwise if paired else general,
        mesh=mesh,
        in_specs=(
            P(("groups", "seq"), ("mp", "side")),
            P(("groups", "seq"), "mp"),
            P(("groups", "seq"), "mp"),
            P(("groups", "seq")),
            P(("groups", "seq"), None),
            P(("groups", "seq"), None),
            P(),
            P("seq", ("mp", "side")),
        ),
        out_specs=(P(("groups", "seq"), None), P(("groups", "seq"), ("mp", "side"))),
        check_vma=False,
    )
```

```python
import functools
import math

import jax
import jax.numpy as jnp
from jax import lax
from jax.experimental import pallas as pl
from jax.experimental.pallas import tpu as pltpu
from jax.sharding import PartitionSpec as P

HD = 128
LANES = 128
BF = jnp.bfloat16
F32 = jnp.float32
I32 = jnp.int32
PARAMS = pltpu.CompilerParams(vmem_limit_bytes=16 * 1024 * 1024)
NORM_MB = 52
PAIRWISE = True


def dot(a, b, dims=((1,), (0,))):
    return lax.dot_general(a, b, (dims, ((), ())), preferred_element_type=F32)


def eye(size):
    return lax.broadcasted_iota(I32, (size, size), 0) == lax.broadcasted_iota(I32, (size, size), 1)


def to_row(column):
    return jnp.sum(jnp.where(eye(column.shape[0]), column, 0.0), axis=0, keepdims=True)


def to_column(row):
    return jnp.sum(jnp.where(eye(row.shape[1]), row, 0.0), axis=1, keepdims=True)


def indices():
    return lax.axis_index("seq"), lax.axis_index("mp") * 2 + lax.axis_index("side")


def call(kernel, shapes, args, flops, moved, transcendentals=0, **more):
    vmem = pl.BlockSpec(memory_space=pltpu.VMEM)
    options = dict(
        in_specs=[vmem] * len(args),
        out_specs=jax.tree.map(lambda s: vmem, shapes),
        compiler_params=PARAMS,
    )
    options.update(more)
    return pl.pallas_call(
        kernel,
        out_shape=shapes,
        cost_estimate=pl.CostEstimate(
            flops=flops, bytes_accessed=moved, transcendentals=transcendentals
        ),
        **options,
    )(*args)


def inverse_rms(hidden):
    width = hidden.shape[1]
    return lax.rsqrt(jnp.sum(hidden * hidden, axis=1, keepdims=True) / width + 1e-06)


def norm_kernel(student_any, small_ref, *refs):
    *pieces, hidden_ref, arrived = refs
    me, mine = indices()
    copies = [
        pltpu.make_async_copy(student_any.at[mine ^ (2 * i)], hidden_ref.at[i], arrived.at[i])
        for i in range(2)
    ]
    for copy in copies:
        copy.start()
    _, rows, width = hidden_ref.shape
    tiles = width // len(pieces) // LANES
    line = lax.broadcasted_iota(I32, (rows, LANES), 0)
    last = width // LANES
    owner_row, docs_row = small_ref[last : last + 1, :], small_ref[last + 1 : last + 2, :]
    extra = jnp.where(line == 0, owner_row, jnp.where(line == 1, docs_row, 0.0)).astype(BF)
    for piece in pieces:
        piece[:, tiles * LANES :] = extra
    copies[0].wait()
    inverse = inverse_rms(hidden_ref[0].astype(F32))
    for k, piece in enumerate(pieces):
        for tile in range(tiles):
            at = (me ^ k) * tiles + tile
            columns = pl.ds(pl.multiple_of(at * LANES, LANES), LANES)
            block = hidden_ref[0, :, columns].astype(F32)
            normed = block * inverse * small_ref[pl.ds(at, 1), :]
            piece[:, tile * LANES : (tile + 1) * LANES] = normed.astype(BF)
    copies[1].wait()


def norm_pieces(student, small):
    n, rows, width = student.shape
    piece = jax.ShapeDtypeStruct((rows, width // n + LANES), BF)
    return call(
        norm_kernel,
        [piece] * n + [jax.ShapeDtypeStruct((2, rows, width), BF)],
        (student, small),
        6 * rows * width,
        8 * rows * width,
        in_specs=[pl.BlockSpec(memory_space=pl.ANY), pl.BlockSpec(memory_space=pltpu.VMEM)],
        scratch_shapes=[pltpu.SemaphoreType.DMA((2,))],
        compiler_params=pltpu.CompilerParams(vmem_limit_bytes=NORM_MB * 1024 * 1024),
    )


def pick_kernel(*refs):
    *pieces, out_ref, drop_ref = refs
    pieces = pieces[::-1]
    me, mine = indices()
    tokens, depth = out_ref.shape
    slots = pieces[0].shape[0]
    spots = slots * len(pieces)
    owner_row = jnp.zeros((1, tokens), F32)
    for k, piece in enumerate(pieces):
        tile = piece[0:16, depth:].astype(F32)[0:1]
        owner_row = owner_row + jnp.where((me ^ mine) == k, tile, 0.0)
    owner = to_column(owner_row)
    earlier = lax.broadcasted_iota(I32, (tokens, tokens), 1) < lax.broadcasted_iota(
        I32, (tokens, tokens), 0
    )
    same = jnp.where(earlier & (owner == owner_row), 1.0, 0.0)
    rank = jnp.sum(same, axis=1, keepdims=True)
    peer = owner.astype(I32) ^ me
    spot = (peer * slots).astype(F32) + rank
    take = (lax.broadcasted_iota(I32, (tokens, spots), 1) == spot.astype(I32)).astype(F32)
    stacked = jnp.concatenate([piece[:, :depth] for piece in pieces], axis=0)
    out_ref[...] = dot(take.astype(BF), stacked).astype(BF)
    spot_row = to_row(spot).astype(I32)
    drop = (lax.broadcasted_iota(I32, (spots, tokens), 0) == spot_row).astype(F32)
    drop_ref[...] = drop.astype(BF)


def pick_rows(pieces, tokens):
    slots, wide = pieces[0].shape
    depth, spots = wide - LANES, slots * len(pieces)
    return call(
        pick_kernel,
        [jax.ShapeDtypeStruct((tokens, depth), BF), jax.ShapeDtypeStruct((spots, tokens), BF)],
        pieces[::-1],
        2 * tokens * spots * depth,
        4 * spots * depth,
    )


def attention_kernel(queries_ref, *refs):
    out_ref = refs[-1]
    n = (len(refs) - 1) // 2
    parcels, pieces = refs[:n], refs[n : 2 * n]
    tokens = queries_ref.shape[0]
    depth = pieces[0].shape[1] - LANES
    me, _ = indices()
    keys = jnp.concatenate([parcel[:tokens, :] for parcel in parcels], axis=0)
    values = jnp.concatenate([parcel[tokens:, :] for parcel in parcels], axis=0)
    docs = [piece[0:16, depth:].astype(F32)[1:2] for piece in pieces]
    doc_column = to_column(docs[0])
    query_pos = me * tokens + lax.broadcasted_iota(I32, (tokens, tokens), 0)
    within = lax.broadcasted_iota(I32, (tokens, tokens), 1)
    masks = []
    for k in range(n):
        block = (me - k + n) % n
        doc_row = sum(jnp.where((me ^ block) == i, docs[i], 0.0) for i in range(n))
        near = block * tokens + within <= query_pos
        masks.append(jnp.where(near & (doc_row == doc_column), 1.0, 0.0))
    allowed = jnp.concatenate(masks, axis=1) > 0.5
    scale_factor = 1.0 / math.sqrt(HD)
    for h in range(queries_ref.shape[1] // HD):
        columns = slice(h * HD, (h + 1) * HD)
        scores = dot(queries_ref[:, columns], keys, ((1,), (1,))) * scale_factor
        scores = jnp.where(allowed, scores, -1e30)
        top = jnp.max(scores, axis=1, keepdims=True)
        probs = jnp.where(allowed, jnp.exp(scores - top), 0.0)
        total = jnp.sum(probs, axis=1, keepdims=True)
        out_ref[:, columns] = (dot(probs.astype(BF), values) / total).astype(BF)


def attention_rows(queries, parcels, pieces):
    tokens, width = queries.shape
    return call(
        attention_kernel,
        jax.ShapeDtypeStruct((tokens, width), BF),
        (queries, *parcels, *pieces),
        0,
        4 * tokens * width,
    )


def pick_entry(refs, at):
    d, c, b, a = (ref[...] for ref in refs)
    odd = at % 2 == 1
    return jnp.where(at >= 2, jnp.where(odd, d, c), jnp.where(odd, b, a))


def away_kernel(*refs):
    *entries, proj_ref, out_ref = refs
    me, mine = indices()
    block = pick_entry(entries, me ^ mine ^ 3)
    out_ref[...] = dot(block, proj_ref[...]).astype(BF)


def kept_kernel(*refs):
    *entries, proj_ref, own_ref, over_ref, normed_ref = refs
    me, mine = indices()
    rows = entries[0].shape[0]
    for k, spot in enumerate((0, 2, 1, 3)):
        normed_ref[spot * rows : (spot + 1) * rows, :] = pick_entry(entries, me ^ mine ^ k)
    columns = 256
    for first in range(0, proj_ref.shape[1], columns):
        part = slice(first, first + columns)
        product = dot(normed_ref[: 2 * rows, :], proj_ref[:, part])
        own_ref[:, part] = product[:rows]
        over_ref[:, part] = product[rows:]


def beside_kernel(normed_ref, proj_ref, out_ref):
    rows = out_ref.shape[0]
    out_ref[...] = dot(normed_ref[2 * rows : 3 * rows, :], proj_ref[...]).astype(BF)


def away_partial(entries, proj):
    rows, depth = entries[0].shape
    out = jax.ShapeDtypeStruct((rows, proj.shape[1]), BF)
    return call(away_kernel, out, (*entries, proj), 0, 0)


def kept_partials(entries, proj):
    rows, depth = entries[0].shape
    out = jax.ShapeDtypeStruct((rows, proj.shape[1]), F32)
    shapes = [out, out, jax.ShapeDtypeStruct((4 * rows, depth), BF)]
    return call(kept_kernel, shapes, (*entries, proj), 0, 0)


def beside_partial(normed, proj):
    out = jax.ShapeDtypeStruct((normed.shape[0] // 4, proj.shape[1]), BF)
    return call(beside_kernel, out, (normed, proj), 0, 0)


def product_kernel(delta_ref, proj_ref, out_ref):
    out_ref[...] = dot(delta_ref[...], proj_ref[...], ((1,), (1,))).astype(BF)


def product(delta, proj):
    out = jax.ShapeDtypeStruct((delta.shape[0], proj.shape[0]), BF)
    return call(product_kernel, out, (delta, proj), 0, 0)


def route_kernel(first_ref, second_ref, third_ref, delta_ref, proj_ref, *refs):
    *outs, held = refs
    me, mine = indices()
    last = dot(delta_ref[...], proj_ref[...], ((1,), (1,))).astype(BF)
    for k, block in enumerate((first_ref[...], second_ref[...], third_ref[...], last)):
        held[k] = block
    for k, out in enumerate(outs):
        out[...] = held[me ^ mine ^ k]


def route_products(products, delta, proj):
    tokens, depth = products[0].shape
    out = jax.ShapeDtypeStruct((tokens, depth), BF)
    return call(
        route_kernel,
        [out] * 4,
        (*products, delta, proj),
        0,
        0,
        scratch_shapes=[pltpu.VMEM((4, tokens, depth), BF)],
    )


def leave_kernel(peers, drop_ref, kept_ref, got_ref, crossed_ref, *outs):
    near = kept_ref[...].astype(F32) + got_ref[...].astype(F32)
    rows = (near + crossed_ref[...].astype(F32)).astype(BF)
    slots = outs[0].shape[0]
    for k, out in zip(peers, outs):
        out[...] = dot(drop_ref[k * slots : (k + 1) * slots, :], rows).astype(BF)


def leaving_rows(peers, drop, kept, got, crossed):
    out = jax.ShapeDtypeStruct((drop.shape[0] // 4, crossed.shape[1]), BF)
    kernel = functools.partial(leave_kernel, peers)
    return call(kernel, [out] * len(peers), (drop, kept, got, crossed), 0, 0)


def rows_kernel(which, hidden_ref, small_ref, *refs):
    *pieces, out_ref = refs
    me, _ = indices()
    _, rows, width = hidden_ref.shape
    tiles = width // len(pieces) // LANES
    inverse = inverse_rms(hidden_ref[which].astype(F32))
    spots = [
        (piece, tile, (me ^ k) * tiles + tile)
        for k, piece in enumerate(pieces)
        for tile in range(tiles)
    ]
    total = jnp.zeros((rows, LANES), F32)
    for piece, tile, at in spots:
        columns = pl.ds(pl.multiple_of(at * LANES, LANES), LANES)
        block = hidden_ref[which, :, columns].astype(F32)
        grad = piece[:, tile * LANES : (tile + 1) * LANES].astype(F32)
        total = total + grad * small_ref[pl.ds(at, 1), :] * block
    mean = jnp.sum(total, axis=1, keepdims=True) / width
    lean = inverse * inverse * inverse * mean
    for piece, tile, at in spots:
        columns = pl.ds(pl.multiple_of(at * LANES, LANES), LANES)
        block = hidden_ref[which, :, columns].astype(F32)
        grad = piece[:, tile * LANES : (tile + 1) * LANES].astype(F32)
        grad = inverse * (grad * small_ref[pl.ds(at, 1), :]) - lean * block
        out_ref[:, columns] = grad.astype(BF)


def grad_rows(which, hidden, small, pieces):
    out = jax.ShapeDtypeStruct(hidden.shape[1:], BF)
    return call(functools.partial(rows_kernel, which), out, (hidden, small, *pieces), 0, 0)


def write_kernel(places, *refs):
    *blocks, out_ref, done = refs
    _, mine = indices()
    copies = [
        pltpu.make_async_copy(block, out_ref.at[mine ^ place], done.at[i])
        for i, (block, place) in enumerate(zip(blocks, places))
    ]
    for copy in copies:
        copy.start()
    for copy in copies:
        copy.wait()


def write_rows(blocks, places, target=None):
    rows, width = blocks[0].shape
    hbm, vmem = pl.BlockSpec(memory_space=pltpu.HBM), pl.BlockSpec(memory_space=pltpu.VMEM)
    kernel = functools.partial(write_kernel, places)
    args, specs, aliases = tuple(blocks), [vmem] * len(blocks), {}
    if target is not None:
        kernel = lambda t, *refs: write_kernel(places, *refs)
        args, specs, aliases = (target, *args), [hbm] + specs, {0: 0}
    return call(
        kernel,
        jax.ShapeDtypeStruct((4, rows, width), BF),
        args,
        0,
        4 * len(blocks) * rows * width,
        in_specs=specs,
        out_specs=hbm,
        input_output_aliases=aliases,
        scratch_shapes=[pltpu.SemaphoreType.DMA((len(blocks),))],
    )


def swap(x, axis, k=1):
    return lax.ppermute(x, axis, [(i, i ^ k) for i in range(lax.axis_size(axis))])


def onward(x):
    return lax.ppermute(x, "seq", [(i, i + 1) for i in range(lax.axis_size("seq") - 1)])


def exchange(blocks):
    got = {k: swap(blocks[k], "seq", k) for k in reversed(range(1, len(blocks)))}
    return [got[k] for k in range(1, len(blocks))]


def after(x, *others):
    return lax.optimization_barrier((x, *others))[0]


def pairwise(
    teacher_queries, teacher_keys, teacher_values, doc_ids, owner, student_hidden, norm_gain, proj
):
    n = 4
    me, mine = indices()
    side = lax.axis_index("side")
    rows = teacher_queries.shape[0]
    heads = teacher_queries.shape[1] // HD
    kv_local = teacher_keys.shape[1] // HD
    group = heads * 2 // kv_local
    capacity, width = student_hidden.shape
    slots = capacity // n
    student = student_hidden.reshape(n, slots, width)
    tiles = width // LANES
    line = lax.broadcasted_iota(I32, (tiles + 2, LANES), 0)
    ids = jnp.where(line == tiles, owner[:, 0][None, :], doc_ids[None, :]).astype(F32)
    gain = jnp.pad(norm_gain.reshape(tiles, LANES), ((0, 2), (0, 0)))
    small = jnp.where(line < tiles, gain, ids)

    *made, hidden = norm_pieces(student, small)
    pieces = [made[0]] + exchange(made)

    head = side * heads // group
    parcel = jnp.concatenate(
        [
            lax.dynamic_slice_in_dim(teacher_keys, head * HD, HD, 1),
            lax.dynamic_slice_in_dim(teacher_values, head * HD, HD, 1),
        ]
    )
    parcels = [after(lax.optimization_barrier(parcel), made[0])]
    parcels.append(onward(parcels[0]))
    normed_own, drop = pick_rows([after(piece, parcels[1]) for piece in pieces], rows)

    far = swap(normed_own, "mp")
    mate = swap(normed_own, "side")
    parcels.append(onward(after(parcels[1], normed_own)))
    far_mate = swap(after(far, mate, parcels[2]), "side")
    entries = [far_mate, far, mate, normed_own]

    away = away_partial(entries, proj)
    own, over_own, normed = kept_partials([after(e, away) for e in entries], proj)
    parcels.append(onward(after(parcels[2], away)))
    got_over = after(swap(away, "seq", 1), over_own, parcels[3])
    over = lax.optimization_barrier((over_own + got_over.astype(F32)).astype(BF))
    got_far = swap(over, "seq", 2)
    got_beside = swap(beside_partial(after(normed, over), proj), "seq", 1)
    teacher_rows = attention_rows(after(teacher_queries, over), parcels, pieces)
    predicted = lax.optimization_barrier(own + got_far.astype(F32)) + got_beside.astype(F32)
    delta = (predicted - teacher_rows.astype(F32)).astype(BF)

    delta_far = swap(delta, "seq", 2)
    own_product = product(delta, proj)
    delta_beside = swap(after(delta, own_product), "seq", 1)
    delta_last = swap(delta_far, "seq", 1)
    deltas = [delta, delta_beside, delta_far, delta_last]
    products = [own_product, product(delta_beside, proj), product(delta_far, proj)]

    near, mates_near, over, mates_over = route_products(products, delta_last, proj)
    got_cross = swap(mates_over, "side")
    cross = lax.optimization_barrier((over.astype(F32) + got_cross.astype(F32)).astype(BF))
    got_near = swap(after(mates_near, cross), "side")
    crossed = swap(cross, "mp")

    factor = 1.0 / math.sqrt(rows * n)
    deltas = after(jnp.concatenate([deltas[k] for k in (0, 2, 1, 3)]), cross)
    grad_proj = lax.optimization_barrier(dot(normed, deltas, ((0,), (0,))) * factor)
    crossed = after(crossed, grad_proj)
    leaving = leaving_rows(range(n), drop, near, got_near, crossed)

    arrived = [leaving[0]] + exchange(leaving)
    across = [swap(block, "mp") for block in arrived]
    own_ready = [after(block, leaving[0]) for block in arrived]
    grad_own = grad_rows(0, hidden, small, own_ready)
    grad_mate = swap(grad_own, "side")
    grad_far = grad_rows(1, hidden, small, across)
    grad_last = swap(grad_far, "side")
    grad_hidden = write_rows([grad_own, grad_mate, grad_far], (0, 1, 2))
    grad_hidden = write_rows([grad_last], (3,), grad_hidden).reshape(capacity, width)
    return (grad_hidden, grad_proj)


def general(
    teacher_queries, teacher_keys, teacher_values, doc_ids, owner, student_hidden, norm_gain, proj
):
    n = lax.axis_size("seq")
    me = lax.axis_index("seq")
    side = lax.axis_index("side")
    plane = lax.axis_size("mp") * lax.axis_size("side")
    mine = lax.axis_index("mp") * lax.axis_size("side") + side
    rows = teacher_queries.shape[0]
    heads = teacher_queries.shape[1] // HD
    kv_local = teacher_keys.shape[1] // HD
    group = heads * lax.axis_size("side") // kv_local
    width = student_hidden.shape[1]
    depth = proj.shape[0]
    capacity = student_hidden.shape[0]
    slots = capacity // n
    shared = n // plane
    held = shared * slots

    hidden = lax.dynamic_slice_in_dim(student_hidden, mine * held, held, 0).astype(F32)
    inverse_rms = lax.rsqrt(jnp.mean(hidden * hidden, axis=1, keepdims=True) + 1e-06)
    normed = (hidden * inverse_rms * norm_gain).astype(BF)
    normed_slots = lax.all_to_all(
        normed.reshape(held, n, depth).transpose(1, 0, 2), "seq", 0, 0, tiled=True
    )

    head = side * heads // group
    key_head = lax.dynamic_slice_in_dim(teacher_keys, head * HD, HD, 1)
    value_head = lax.dynamic_slice_in_dim(teacher_values, head * HD, HD, 1)
    small = jnp.stack([doc_ids, owner[:, 0]]).astype(BF)
    parcel = jnp.concatenate([key_head, value_head, jnp.pad(small, ((0, 14), (0, 0)))])
    parcel = lax.all_gather(parcel, "seq", axis=0, tiled=False)
    keys, values = parcel[:, :rows], parcel[:, rows : 2 * rows]
    docs = parcel[:, 2 * rows].astype(I32)
    owners = parcel[:, 2 * rows + 1].astype(I32)

    query_pos = me * rows + jnp.arange(rows, dtype=I32)
    key_pos = jnp.arange(n * rows, dtype=I32)
    allowed = (docs.reshape(-1)[None, :] == doc_ids[:, None]) & (
        key_pos[None, :] <= query_pos[:, None]
    )
    stacked = teacher_queries.reshape(rows, heads, HD).transpose(1, 0, 2)
    scores = jnp.einsum("hqd,kd->hqk", stacked, keys.reshape(-1, HD), preferred_element_type=F32)
    scores = jnp.where(allowed[None], scores * (1.0 / math.sqrt(HD)), -1e30)
    top = jnp.max(scores, axis=2, keepdims=True)
    probs = jnp.where(allowed[None], jnp.exp(scores - top), 0.0)
    totals = jnp.sum(probs, axis=2, keepdims=True)
    weighted = jnp.einsum(
        "hqk,kd->hqd", probs.astype(BF), values.reshape(-1, HD), preferred_element_type=F32
    )
    teacher_rows = (weighted / totals).astype(BF).transpose(1, 0, 2).reshape(rows, heads * HD)

    own_blocks = lax.dynamic_slice_in_dim(owners, mine * shared, shared, 0)
    order = jnp.arange(rows, dtype=I32)
    same = (own_blocks[:, :, None] == own_blocks[:, None, :]) & (order[:, None] > order[None, :])
    rank = jnp.sum(same.astype(I32), axis=2)
    spot = own_blocks * held + jnp.arange(shared, dtype=I32)[:, None] * slots + rank
    pick = (spot.reshape(-1)[:, None] == jnp.arange(n * held, dtype=I32)[None, :]).astype(BF)

    normed_own = dot(pick, normed_slots.reshape(n * held, depth)).astype(BF)
    normed_rows = lax.all_gather(normed_own, ("mp", "side"), axis=0, tiled=True)
    partial = dot(normed_rows, proj).astype(BF)
    predicted = lax.psum_scatter(partial, "seq", scatter_dimension=0, tiled=True).astype(F32)
    delta = (predicted - teacher_rows.astype(F32)).astype(BF)
    deltas = lax.all_gather(delta, "seq", axis=0, tiled=True)

    products = dot(deltas, proj, ((1,), (1,))).astype(BF)
    feature_rows = lax.psum_scatter(products, ("mp", "side"), scatter_dimension=0, tiled=True)
    feature_slots = dot(pick, feature_rows, ((0,), (0,))).astype(BF).reshape(n, held, depth)
    received = lax.all_to_all(feature_slots, "seq", 0, 0, tiled=True)
    feature_grad = received.transpose(1, 0, 2).reshape(held, width)

    gain_grad = feature_grad.astype(F32) * norm_gain
    mean_term = jnp.mean(gain_grad * hidden, axis=1, keepdims=True)
    grad_own = (inverse_rms * gain_grad - inverse_rms**3 * hidden * mean_term).astype(BF)
    grad_hidden = lax.all_gather(grad_own, ("mp", "side"), axis=0, tiled=True)

    grad_proj = dot(normed_rows, deltas, ((0,), (0,))) * (1.0 / math.sqrt(rows * n))
    return (grad_hidden, grad_proj)


def solution(mesh):
    sizes = mesh.shape
    paired = PAIRWISE and (sizes["seq"], sizes["mp"], sizes["side"]) == (4, 2, 2)
    return jax.shard_map(
        pairwise if paired else general,
        mesh=mesh,
        in_specs=(
            P(("groups", "seq"), ("mp", "side")),
            P(("groups", "seq"), "mp"),
            P(("groups", "seq"), "mp"),
            P(("groups", "seq")),
            P(("groups", "seq"), None),
            P(("groups", "seq"), None),
            P(),
            P("seq", ("mp", "side")),
        ),
        out_specs=(P(("groups", "seq"), None), P(("groups", "seq"), ("mp", "side"))),
        check_vma=False,
    )
```

```python
import functools
import math

import jax
import jax.numpy as jnp
from jax import lax
from jax.experimental import pallas as pl
from jax.experimental.pallas import tpu as pltpu
from jax.sharding import PartitionSpec as P

HD = 128
LANES = 128
BF = jnp.bfloat16
F32 = jnp.float32
I32 = jnp.int32
PARAMS = pltpu.CompilerParams(vmem_limit_bytes=16 * 1024 * 1024)
NORM_MB = 52
PAIRWISE = True


def dot(a, b, dims=((1,), (0,))):
    return lax.dot_general(a, b, (dims, ((), ())), preferred_element_type=F32)


def eye(size):
    return lax.broadcasted_iota(I32, (size, size), 0) == lax.broadcasted_iota(I32, (size, size), 1)


def to_row(column):
    return jnp.sum(jnp.where(eye(column.shape[0]), column, 0.0), axis=0, keepdims=True)


def to_column(row):
    return jnp.sum(jnp.where(eye(row.shape[1]), row, 0.0), axis=1, keepdims=True)


def indices():
    return lax.axis_index("seq"), lax.axis_index("mp") * 2 + lax.axis_index("side")


def call(kernel, shapes, args, flops, moved, transcendentals=0, **more):
    vmem = pl.BlockSpec(memory_space=pltpu.VMEM)
    options = dict(
        in_specs=[vmem] * len(args),
        out_specs=jax.tree.map(lambda s: vmem, shapes),
        compiler_params=PARAMS,
    )
    options.update(more)
    return pl.pallas_call(
        kernel,
        out_shape=shapes,
        cost_estimate=pl.CostEstimate(
            flops=flops, bytes_accessed=moved, transcendentals=transcendentals
        ),
        **options,
    )(*args)


def inverse_rms(hidden):
    width = hidden.shape[1]
    return lax.rsqrt(jnp.sum(hidden * hidden, axis=1, keepdims=True) / width + 1e-06)


def norm_kernel(student_any, small_ref, *refs):
    *pieces, hidden_ref, arrived = refs
    me, mine = indices()
    copies = [
        pltpu.make_async_copy(student_any.at[mine ^ (2 * i)], hidden_ref.at[i], arrived.at[i])
        for i in range(2)
    ]
    for copy in copies:
        copy.start()
    _, rows, width = hidden_ref.shape
    tiles = width // len(pieces) // LANES
    line = lax.broadcasted_iota(I32, (rows, LANES), 0)
    last = width // LANES
    owner_row, docs_row = small_ref[last : last + 1, :], small_ref[last + 1 : last + 2, :]
    extra = jnp.where(line == 0, owner_row, jnp.where(line == 1, docs_row, 0.0)).astype(BF)
    for piece in pieces:
        piece[:, tiles * LANES :] = extra
    copies[0].wait()
    inverse = inverse_rms(hidden_ref[0].astype(F32))
    for k, piece in enumerate(pieces):
        for tile in range(tiles):
            at = (me ^ k) * tiles + tile
            columns = pl.ds(pl.multiple_of(at * LANES, LANES), LANES)
            block = hidden_ref[0, :, columns].astype(F32)
            normed = block * inverse * small_ref[pl.ds(at, 1), :]
            piece[:, tile * LANES : (tile + 1) * LANES] = normed.astype(BF)
    copies[1].wait()


def norm_pieces(student, small):
    n, rows, width = student.shape
    piece = jax.ShapeDtypeStruct((rows, width // n + LANES), BF)
    return call(
        norm_kernel,
        [piece] * n + [jax.ShapeDtypeStruct((2, rows, width), BF)],
        (student, small),
        6 * rows * width,
        8 * rows * width,
        in_specs=[pl.BlockSpec(memory_space=pl.ANY), pl.BlockSpec(memory_space=pltpu.VMEM)],
        scratch_shapes=[pltpu.SemaphoreType.DMA((2,))],
        compiler_params=pltpu.CompilerParams(vmem_limit_bytes=NORM_MB * 1024 * 1024),
    )


def pick_kernel(*refs):
    *pieces, out_ref, drop_ref = refs
    pieces = pieces[::-1]
    me, mine = indices()
    tokens, depth = out_ref.shape
    slots = pieces[0].shape[0]
    spots = slots * len(pieces)
    owner_row = jnp.zeros((1, tokens), F32)
    for k, piece in enumerate(pieces):
        tile = piece[0:16, depth:].astype(F32)[0:1]
        owner_row = owner_row + jnp.where((me ^ mine) == k, tile, 0.0)
    owner = to_column(owner_row)
    earlier = lax.broadcasted_iota(I32, (tokens, tokens), 1) < lax.broadcasted_iota(
        I32, (tokens, tokens), 0
    )
    same = jnp.where(earlier & (owner == owner_row), 1.0, 0.0)
    rank = jnp.sum(same, axis=1, keepdims=True)
    peer = owner.astype(I32) ^ me
    spot = (peer * slots).astype(F32) + rank
    take = (lax.broadcasted_iota(I32, (tokens, spots), 1) == spot.astype(I32)).astype(F32)
    stacked = jnp.concatenate([piece[:, :depth] for piece in pieces], axis=0)
    out_ref[...] = dot(take.astype(BF), stacked).astype(BF)
    spot_row = to_row(spot).astype(I32)
    drop = (lax.broadcasted_iota(I32, (spots, tokens), 0) == spot_row).astype(F32)
    drop_ref[...] = drop.astype(BF)


def pick_rows(pieces, tokens):
    slots, wide = pieces[0].shape
    depth, spots = wide - LANES, slots * len(pieces)
    return call(
        pick_kernel,
        [jax.ShapeDtypeStruct((tokens, depth), BF), jax.ShapeDtypeStruct((spots, tokens), BF)],
        pieces[::-1],
        2 * tokens * spots * depth,
        4 * spots * depth,
    )


def attention_kernel(queries_ref, *refs):
    out_ref = refs[-1]
    n = (len(refs) - 1) // 2
    parcels, pieces = refs[:n], refs[n : 2 * n]
    tokens = queries_ref.shape[0]
    depth = pieces[0].shape[1] - LANES
    me, _ = indices()
    keys = jnp.concatenate([parcel[:tokens, :] for parcel in parcels], axis=0)
    values = jnp.concatenate([parcel[tokens:, :] for parcel in parcels], axis=0)
    docs = [piece[0:16, depth:].astype(F32)[1:2] for piece in pieces]
    doc_column = to_column(docs[0])
    query_pos = me * tokens + lax.broadcasted_iota(I32, (tokens, tokens), 0)
    within = lax.broadcasted_iota(I32, (tokens, tokens), 1)
    masks = []
    for k in range(n):
        block = (me - k + n) % n
        doc_row = sum(jnp.where((me ^ block) == i, docs[i], 0.0) for i in range(n))
        near = block * tokens + within <= query_pos
        masks.append(jnp.where(near & (doc_row == doc_column), 1.0, 0.0))
    allowed = jnp.concatenate(masks, axis=1) > 0.5
    scale_factor = 1.0 / math.sqrt(HD)
    for h in range(queries_ref.shape[1] // HD):
        columns = slice(h * HD, (h + 1) * HD)
        scores = dot(queries_ref[:, columns], keys, ((1,), (1,))) * scale_factor
        scores = jnp.where(allowed, scores, -1e30)
        top = jnp.max(scores, axis=1, keepdims=True)
        probs = jnp.where(allowed, jnp.exp(scores - top), 0.0)
        total = jnp.sum(probs, axis=1, keepdims=True)
        out_ref[:, columns] = (dot(probs.astype(BF), values) / total).astype(BF)


def attention_rows(queries, parcels, pieces):
    tokens, width = queries.shape
    return call(
        attention_kernel,
        jax.ShapeDtypeStruct((tokens, width), BF),
        (queries, *parcels, *pieces),
        0,
        4 * tokens * width,
    )


def pick_entry(refs, at):
    d, c, b, a = (ref[...] for ref in refs)
    odd = at % 2 == 1
    return jnp.where(at >= 2, jnp.where(odd, d, c), jnp.where(odd, b, a))


def away_kernel(*refs):
    *entries, proj_ref, out_ref = refs
    me, mine = indices()
    block = pick_entry(entries, me ^ mine ^ 3)
    out_ref[...] = dot(block, proj_ref[...]).astype(BF)


def kept_kernel(*refs):
    *entries, proj_ref, own_ref, over_ref, normed_ref = refs
    me, mine = indices()
    rows = entries[0].shape[0]
    for k, spot in enumerate((0, 2, 1, 3)):
        normed_ref[spot * rows : (spot + 1) * rows, :] = pick_entry(entries, me ^ mine ^ k)
    columns = 256
    for first in range(0, proj_ref.shape[1], columns):
        part = slice(first, first + columns)
        product = dot(normed_ref[: 2 * rows, :], proj_ref[:, part])
        own_ref[:, part] = product[:rows]
        over_ref[:, part] = product[rows:]


def beside_kernel(normed_ref, proj_ref, out_ref):
    rows = out_ref.shape[0]
    out_ref[...] = dot(normed_ref[2 * rows : 3 * rows, :], proj_ref[...]).astype(BF)


def away_partial(entries, proj):
    rows, depth = entries[0].shape
    out = jax.ShapeDtypeStruct((rows, proj.shape[1]), BF)
    return call(away_kernel, out, (*entries, proj), 0, 0)


def kept_partials(entries, proj):
    rows, depth = entries[0].shape
    out = jax.ShapeDtypeStruct((rows, proj.shape[1]), F32)
    shapes = [out, out, jax.ShapeDtypeStruct((4 * rows, depth), BF)]
    return call(kept_kernel, shapes, (*entries, proj), 0, 0)


def beside_partial(normed, proj):
    out = jax.ShapeDtypeStruct((normed.shape[0] // 4, proj.shape[1]), BF)
    return call(beside_kernel, out, (normed, proj), 0, 0)


def product_kernel(delta_ref, proj_ref, out_ref):
    out_ref[...] = dot(delta_ref[...], proj_ref[...], ((1,), (1,))).astype(BF)


def product(delta, proj):
    out = jax.ShapeDtypeStruct((delta.shape[0], proj.shape[0]), BF)
    return call(product_kernel, out, (delta, proj), 0, 0)


def route_kernel(first_ref, second_ref, third_ref, delta_ref, proj_ref, *refs):
    *outs, held = refs
    me, mine = indices()
    last = dot(delta_ref[...], proj_ref[...], ((1,), (1,))).astype(BF)
    for k, block in enumerate((first_ref[...], second_ref[...], third_ref[...], last)):
        held[k] = block
    for k, out in enumerate(outs):
        out[...] = held[me ^ mine ^ k]


def route_products(products, delta, proj):
    tokens, depth = products[0].shape
    out = jax.ShapeDtypeStruct((tokens, depth), BF)
    return call(
        route_kernel,
        [out] * 4,
        (*products, delta, proj),
        0,
        0,
        scratch_shapes=[pltpu.VMEM((4, tokens, depth), BF)],
    )


def leave_kernel(peers, drop_ref, kept_ref, got_ref, crossed_ref, *outs):
    near = kept_ref[...].astype(F32) + got_ref[...].astype(F32)
    rows = (near + crossed_ref[...].astype(F32)).astype(BF)
    slots = outs[0].shape[0]
    for k, out in zip(peers, outs):
        out[...] = dot(drop_ref[k * slots : (k + 1) * slots, :], rows).astype(BF)


def leaving_rows(peers, drop, kept, got, crossed):
    out = jax.ShapeDtypeStruct((drop.shape[0] // 4, crossed.shape[1]), BF)
    kernel = functools.partial(leave_kernel, peers)
    return call(kernel, [out] * len(peers), (drop, kept, got, crossed), 0, 0)


def rows_kernel(which, hidden_ref, small_ref, *refs):
    *pieces, out_ref = refs
    me, _ = indices()
    _, rows, width = hidden_ref.shape
    tiles = width // len(pieces) // LANES
    inverse = inverse_rms(hidden_ref[which].astype(F32))
    spots = [
        (piece, tile, (me ^ k) * tiles + tile)
        for k, piece in enumerate(pieces)
        for tile in range(tiles)
    ]
    total = jnp.zeros((rows, LANES), F32)
    for piece, tile, at in spots:
        columns = pl.ds(pl.multiple_of(at * LANES, LANES), LANES)
        block = hidden_ref[which, :, columns].astype(F32)
        grad = piece[:, tile * LANES : (tile + 1) * LANES].astype(F32)
        total = total + grad * small_ref[pl.ds(at, 1), :] * block
    mean = jnp.sum(total, axis=1, keepdims=True) / width
    lean = inverse * inverse * inverse * mean
    for piece, tile, at in spots:
        columns = pl.ds(pl.multiple_of(at * LANES, LANES), LANES)
        block = hidden_ref[which, :, columns].astype(F32)
        grad = piece[:, tile * LANES : (tile + 1) * LANES].astype(F32)
        grad = inverse * (grad * small_ref[pl.ds(at, 1), :]) - lean * block
        out_ref[:, columns] = grad.astype(BF)


def grad_rows(which, hidden, small, pieces):
    out = jax.ShapeDtypeStruct(hidden.shape[1:], BF)
    return call(functools.partial(rows_kernel, which), out, (hidden, small, *pieces), 0, 0)


def write_kernel(places, *refs):
    *blocks, out_ref, done = refs
    _, mine = indices()
    copies = [
        pltpu.make_async_copy(block, out_ref.at[mine ^ place], done.at[i])
        for i, (block, place) in enumerate(zip(blocks, places))
    ]
    for copy in copies:
        copy.start()
    for copy in copies:
        copy.wait()


def write_rows(blocks, places, target=None):
    rows, width = blocks[0].shape
    hbm, vmem = pl.BlockSpec(memory_space=pltpu.HBM), pl.BlockSpec(memory_space=pltpu.VMEM)
    kernel = functools.partial(write_kernel, places)
    args, specs, aliases = tuple(blocks), [vmem] * len(blocks), {}
    if target is not None:
        kernel = lambda t, *refs: write_kernel(places, *refs)
        args, specs, aliases = (target, *args), [hbm] + specs, {0: 0}
    return call(
        kernel,
        jax.ShapeDtypeStruct((4, rows, width), BF),
        args,
        0,
        4 * len(blocks) * rows * width,
        in_specs=specs,
        out_specs=hbm,
        input_output_aliases=aliases,
        scratch_shapes=[pltpu.SemaphoreType.DMA((len(blocks),))],
    )


def swap(x, axis, k=1):
    return lax.ppermute(x, axis, [(i, i ^ k) for i in range(lax.axis_size(axis))])


def onward(x):
    return lax.ppermute(x, "seq", [(i, i + 1) for i in range(lax.axis_size("seq") - 1)])


def exchange(blocks):
    got = {k: swap(blocks[k], "seq", k) for k in reversed(range(1, len(blocks)))}
    return [got[k] for k in range(1, len(blocks))]


def after(x, *others):
    return lax.optimization_barrier((x, *others))[0]


def pairwise(
    teacher_queries, teacher_keys, teacher_values, doc_ids, owner, student_hidden, norm_gain, proj
):
    n = 4
    me, mine = indices()
    side = lax.axis_index("side")
    rows = teacher_queries.shape[0]
    heads = teacher_queries.shape[1] // HD
    kv_local = teacher_keys.shape[1] // HD
    group = heads * 2 // kv_local
    capacity, width = student_hidden.shape
    slots = capacity // n
    student = student_hidden.reshape(n, slots, width)
    tiles = width // LANES
    line = lax.broadcasted_iota(I32, (tiles + 2, LANES), 0)
    ids = jnp.where(line == tiles, owner[:, 0][None, :], doc_ids[None, :]).astype(F32)
    gain = jnp.pad(norm_gain.reshape(tiles, LANES), ((0, 2), (0, 0)))
    small = jnp.where(line < tiles, gain, ids)

    *made, hidden = norm_pieces(student, small)
    pieces = [made[0]] + exchange(made)

    head = side * heads // group
    parcel = jnp.concatenate(
        [
            lax.dynamic_slice_in_dim(teacher_keys, head * HD, HD, 1),
            lax.dynamic_slice_in_dim(teacher_values, head * HD, HD, 1),
        ]
    )
    parcels = [after(lax.optimization_barrier(parcel), made[0])]
    parcels.append(onward(parcels[0]))
    normed_own, drop = pick_rows([after(piece, parcels[1]) for piece in pieces], rows)

    far = swap(normed_own, "mp")
    mate = swap(after(normed_own, far, *parcels[2:]), "side")
    parcels.append(onward(after(parcels[1], normed_own)))
    far_mate = swap(after(far, parcels[2]), "side")
    entries = [far_mate, far, mate, normed_own]

    away = away_partial(entries, proj)
    own, over_own, normed = kept_partials([after(e, away) for e in entries], proj)
    parcels.append(onward(after(parcels[2], away)))
    got_over = after(swap(away, "seq", 1), over_own, parcels[3])
    over = lax.optimization_barrier((over_own + got_over.astype(F32)).astype(BF))
    got_far = swap(over, "seq", 2)
    got_beside = swap(beside_partial(after(normed, over), proj), "seq", 1)
    teacher_rows = attention_rows(after(teacher_queries, over), parcels, pieces)
    predicted = lax.optimization_barrier(own + got_far.astype(F32)) + got_beside.astype(F32)
    delta = (predicted - teacher_rows.astype(F32)).astype(BF)

    delta_far = swap(delta, "seq", 2)
    own_product = product(delta, proj)
    delta_beside = swap(after(delta, own_product), "seq", 1)
    delta_last = swap(delta_far, "seq", 1)
    deltas = [delta, delta_beside, delta_far, delta_last]
    products = [own_product, product(delta_beside, proj), product(delta_far, proj)]

    near, mates_near, over, mates_over = route_products(products, delta_last, proj)
    got_cross = swap(mates_over, "side")
    cross = lax.optimization_barrier((over.astype(F32) + got_cross.astype(F32)).astype(BF))
    got_near = swap(after(mates_near, cross), "side")
    crossed = swap(cross, "mp")

    factor = 1.0 / math.sqrt(rows * n)
    deltas = after(jnp.concatenate([deltas[k] for k in (0, 2, 1, 3)]), cross)
    grad_proj = lax.optimization_barrier(dot(normed, deltas, ((0,), (0,))) * factor)
    crossed = after(crossed, grad_proj)
    leaving = leaving_rows(range(n), drop, near, got_near, crossed)

    arrived = [leaving[0]] + exchange(leaving)
    across = [swap(block, "mp") for block in arrived]
    own_ready = [after(block, leaving[0]) for block in arrived]
    grad_own = grad_rows(0, hidden, small, own_ready)
    grad_mate = swap(grad_own, "side")
    grad_far = grad_rows(1, hidden, small, across)
    grad_last = swap(grad_far, "side")
    grad_hidden = write_rows([grad_own, grad_mate, grad_far], (0, 1, 2))
    grad_hidden = write_rows([grad_last], (3,), grad_hidden).reshape(capacity, width)
    return (grad_hidden, grad_proj)


def general(
    teacher_queries, teacher_keys, teacher_values, doc_ids, owner, student_hidden, norm_gain, proj
):
    n = lax.axis_size("seq")
    me = lax.axis_index("seq")
    side = lax.axis_index("side")
    plane = lax.axis_size("mp") * lax.axis_size("side")
    mine = lax.axis_index("mp") * lax.axis_size("side") + side
    rows = teacher_queries.shape[0]
    heads = teacher_queries.shape[1] // HD
    kv_local = teacher_keys.shape[1] // HD
    group = heads * lax.axis_size("side") // kv_local
    width = student_hidden.shape[1]
    depth = proj.shape[0]
    capacity = student_hidden.shape[0]
    slots = capacity // n
    shared = n // plane
    held = shared * slots

    hidden = lax.dynamic_slice_in_dim(student_hidden, mine * held, held, 0).astype(F32)
    inverse_rms = lax.rsqrt(jnp.mean(hidden * hidden, axis=1, keepdims=True) + 1e-06)
    normed = (hidden * inverse_rms * norm_gain).astype(BF)
    normed_slots = lax.all_to_all(
        normed.reshape(held, n, depth).transpose(1, 0, 2), "seq", 0, 0, tiled=True
    )

    head = side * heads // group
    key_head = lax.dynamic_slice_in_dim(teacher_keys, head * HD, HD, 1)
    value_head = lax.dynamic_slice_in_dim(teacher_values, head * HD, HD, 1)
    small = jnp.stack([doc_ids, owner[:, 0]]).astype(BF)
    parcel = jnp.concatenate([key_head, value_head, jnp.pad(small, ((0, 14), (0, 0)))])
    parcel = lax.all_gather(parcel, "seq", axis=0, tiled=False)
    keys, values = parcel[:, :rows], parcel[:, rows : 2 * rows]
    docs = parcel[:, 2 * rows].astype(I32)
    owners = parcel[:, 2 * rows + 1].astype(I32)

    query_pos = me * rows + jnp.arange(rows, dtype=I32)
    key_pos = jnp.arange(n * rows, dtype=I32)
    allowed = (docs.reshape(-1)[None, :] == doc_ids[:, None]) & (
        key_pos[None, :] <= query_pos[:, None]
    )
    stacked = teacher_queries.reshape(rows, heads, HD).transpose(1, 0, 2)
    scores = jnp.einsum("hqd,kd->hqk", stacked, keys.reshape(-1, HD), preferred_element_type=F32)
    scores = jnp.where(allowed[None], scores * (1.0 / math.sqrt(HD)), -1e30)
    top = jnp.max(scores, axis=2, keepdims=True)
    probs = jnp.where(allowed[None], jnp.exp(scores - top), 0.0)
    totals = jnp.sum(probs, axis=2, keepdims=True)
    weighted = jnp.einsum(
        "hqk,kd->hqd", probs.astype(BF), values.reshape(-1, HD), preferred_element_type=F32
    )
    teacher_rows = (weighted / totals).astype(BF).transpose(1, 0, 2).reshape(rows, heads * HD)

    own_blocks = lax.dynamic_slice_in_dim(owners, mine * shared, shared, 0)
    order = jnp.arange(rows, dtype=I32)
    same = (own_blocks[:, :, None] == own_blocks[:, None, :]) & (order[:, None] > order[None, :])
    rank = jnp.sum(same.astype(I32), axis=2)
    spot = own_blocks * held + jnp.arange(shared, dtype=I32)[:, None] * slots + rank
    pick = (spot.reshape(-1)[:, None] == jnp.arange(n * held, dtype=I32)[None, :]).astype(BF)

    normed_own = dot(pick, normed_slots.reshape(n * held, depth)).astype(BF)
    normed_rows = lax.all_gather(normed_own, ("mp", "side"), axis=0, tiled=True)
    partial = dot(normed_rows, proj).astype(BF)
    predicted = lax.psum_scatter(partial, "seq", scatter_dimension=0, tiled=True).astype(F32)
    delta = (predicted - teacher_rows.astype(F32)).astype(BF)
    deltas = lax.all_gather(delta, "seq", axis=0, tiled=True)

    products = dot(deltas, proj, ((1,), (1,))).astype(BF)
    feature_rows = lax.psum_scatter(products, ("mp", "side"), scatter_dimension=0, tiled=True)
    feature_slots = dot(pick, feature_rows, ((0,), (0,))).astype(BF).reshape(n, held, depth)
    received = lax.all_to_all(feature_slots, "seq", 0, 0, tiled=True)
    feature_grad = received.transpose(1, 0, 2).reshape(held, width)

    gain_grad = feature_grad.astype(F32) * norm_gain
    mean_term = jnp.mean(gain_grad * hidden, axis=1, keepdims=True)
    grad_own = (inverse_rms * gain_grad - inverse_rms**3 * hidden * mean_term).astype(BF)
    grad_hidden = lax.all_gather(grad_own, ("mp", "side"), axis=0, tiled=True)

    grad_proj = dot(normed_rows, deltas, ((0,), (0,))) * (1.0 / math.sqrt(rows * n))
    return (grad_hidden, grad_proj)


def solution(mesh):
    sizes = mesh.shape
    paired = PAIRWISE and (sizes["seq"], sizes["mp"], sizes["side"]) == (4, 2, 2)
    return jax.shard_map(
        pairwise if paired else general,
        mesh=mesh,
        in_specs=(
            P(("groups", "seq"), ("mp", "side")),
            P(("groups", "seq"), "mp"),
            P(("groups", "seq"), "mp"),
            P(("groups", "seq")),
            P(("groups", "seq"), None),
            P(("groups", "seq"), None),
            P(),
            P("seq", ("mp", "side")),
        ),
        out_specs=(P(("groups", "seq"), None), P(("groups", "seq"), ("mp", "side"))),
        check_vma=False,
    )
```
